32 devices in a mesh: dp: 8 (over y, x, core), mp: 4 (over z).
Axes of the slice: x: 2, y: 2, z: 4, core: 2. Of those that a mesh axis runs over, the one named last changes fastest.
Arguments:
- tokens: bfloat16 [2, 8, 1024, 768], P(None, 'dp', 'mp'), may hold values from -6 to 6
- cotangent: bfloat16 [2, 8, 1024, 768], P(None, 'dp', 'mp'), may hold values from -0.078125 to 0.078125
- segment_ids: int32 [2, 8, 1024], P(None, 'dp'), may hold values from 0 to 7, never falling along the last dimension, each value on 1 to 512 neighbouring positions
- targets: int32 [2, 8, 8], P(None, 'dp'), may hold values from 0 to 62
- attention_weights: float32 [4, 768, 768], P(None, 'dp', 'mp')
- feedforward_weights: float32 [2, 768, 3072], P(None, 'dp', 'mp')
- projection: float32 [768, 768], P('dp', 'mp'), may hold values from -0.21875 to 0.21875
- norm_gains: float32 [3, 768], replicated
- bias_table: float32 [32, 12], replicated, may hold values from -4 to 4
- attention_first: float32 [4, 768, 768], P(None, 'dp', 'mp'), may hold values from -0.00061035156 to 0.00061035156
- attention_second: float32 [4, 768, 768], P(None, 'dp', 'mp'), may hold values from 1.303713e-10 to 5.214852e-10
- feedforward_first: float32 [2, 768, 3072], P(None, 'dp', 'mp'), may hold values from -0.00061035156 to 0.00061035156
- feedforward_second: float32 [2, 768, 3072], P(None, 'dp', 'mp'), may hold values from 1.303713e-10 to 5.214852e-10
- projection_first: float32 [768, 768], P('dp', 'mp'), may hold values from -0.00061035156 to 0.00061035156
- projection_second: float32 [768, 768], P('dp', 'mp'), may hold values from 1.303713e-10 to 5.214852e-10
- gains_first: float32 [3, 768], replicated, may hold values from -0.00061035156 to 0.00061035156
- gains_second: float32 [3, 768], replicated, may hold values from 1.303713e-10 to 5.214852e-10
- bias_first: float32 [32, 12], replicated, may hold values from -0.00061035156 to 0.00061035156
- bias_second: float32 [32, 12], replicated, may hold values from 1.303713e-10 to 5.214852e-10
Outputs:
- output: bfloat16 [2, 8, 1024, 768], P(None, 'dp', 'mp')
- tokens_grad: float32 [2, 8, 1024, 768], P(None, 'dp', 'mp')
- grad_norm: float32 [], replicated
- attention_new: float32 [4, 768, 768], P(None, 'dp', 'mp')
- attention_first_new: float32 [4, 768, 768], P(None, 'dp', 'mp')
- attention_second_new: float32 [4, 768, 768], P(None, 'dp', 'mp')
- feedforward_new: float32 [2, 768, 3072], P(None, 'dp', 'mp')
- feedforward_first_new: float32 [2, 768, 3072], P(None, 'dp', 'mp')
- feedforward_second_new: float32 [2, 768, 3072], P(None, 'dp', 'mp')
- projection_new: float32 [768, 768], P('dp', 'mp')
- projection_first_new: float32 [768, 768], P('dp', 'mp')
- projection_second_new: float32 [768, 768], P('dp', 'mp')
- gains_new: float32 [3, 768], replicated
- gains_first_new: float32 [3, 768], replicated
- gains_second_new: float32 [3, 768], replicated
- bias_new: float32 [32, 12], replicated
- bias_first_new: float32 [32, 12], replicated
- bias_second_new: float32 [32, 12], replicated
The draws below stay inside these ranges and needn't reach their ends.
Inputs may be any that keep to these rules, and one draw needn't show every extreme that they name: `segment_ids`: along every row the segment numbers never fall; each of the 8 numbers occurs, at most 512 times, one exactly 512 times.
All inputs are finite; a program needn't handle non-finite values.
Results may differ from the reference program's by a relative error of at most 0.015.
Values may be sent and summed in bfloat16 or wider, within the bound.
No kernel may reach another device: no remote copies, remote signals or barrier semaphores. Data moves between devices by JAX's collectives and lax.ppermute only.
A program may use at most 192 MiB of HBM per device.

```python
import math
import jax
import jax.numpy as jnp
import numpy as np
from jax import lax

D = 768
H = 12
HD = 64
FF = 3072
NB = 32
ROW = 1024
SEGS = 8
MB = 2
STEP = 10
SEQS = 8
NSEG = 64
SEG_MOST = 512


def draw_attention_weights(key, part):
    key = jax.random.fold_in(key, 11)
    base_draw = jnp.clip(jax.random.normal(key, (4, D, D), jnp.float32), -4.0, 4.0)
    factor = jnp.where(jnp.arange(4) == 3, 8.0, 1.0).astype(jnp.float32)[:, None, None]
    return base_draw * factor * D ** (-0.5)


def draw_feedforward_weights(key, part):
    key = jax.random.fold_in(key, 12)
    base_draw = jnp.clip(jax.random.normal(key, (2, D, FF), jnp.float32), -4.0, 4.0)
    column_scale = 0.5 + jnp.arange(FF, dtype=jnp.float32) / FF
    fan_scale = jnp.array([D ** (-0.5), FF ** (-0.5)], jnp.float32)[:, None, None]
    return base_draw * column_scale[None, None, :] * fan_scale


def draw_norm_gains(key, part):
    key = jax.random.fold_in(key, 13)
    jitter = jax.random.uniform(key, (3, D), jnp.float32, 0.85, 1.15)
    ramp = jnp.arange(D, dtype=jnp.float32) / D
    rising = 0.5 + ramp
    return jitter * rising[None, :]


def plant(result, rng, least, largest):
    place = [jax.random.randint(jax.random.fold_in(rng, axis), (), 0, length) for axis, length in enumerate(result.shape)]
    longest = result.shape.index(max(result.shape))
    beside = place[:longest] + [(place[longest] + 1) % result.shape[longest]] + place[longest + 1:]
    return result.at[tuple(place)].set(least).at[tuple(beside)].set(largest)


def levels(own_key, extent, split, smallest, top_value):
    factor_of, own = 1.0, jax.random.fold_in(own_key, 6)
    for dim, parts in split:
        heights = jnp.exp(jax.random.uniform(jax.random.fold_in(own, dim), (parts,), jnp.float32, smallest / len(split), top_value / len(split)))
        factor_of = factor_of * jnp.repeat(heights, extent[dim] // parts).reshape([-1 if axis == dim else 1 for axis in range(len(extent))])
    return factor_of


def length_profile(amount, total, bound, skew):
    weights = [(1 << 20) // math.isqrt(grade ** skew) + 1 for grade in range(2, amount + 1)]
    surplus, given = total - bound - (amount - 1), [1] * (amount - 1)
    while surplus > 0:
        free = [i for i in range(amount - 1) if given[i] < bound]
        pool, budget = sum([weights[i] for i in free]), surplus
        for i in free:
            extra = min(bound - given[i], max(1, budget * weights[i] // pool), surplus)
            given[i] = given[i] + extra
            surplus = surplus - extra
    return np.array([bound] + given)


def uneven_parts(stream_key, amount, total, limit, skew):
    if amount == 2:
        one = jax.random.randint(stream_key, (), max(1, total - limit), min(limit, total - 1) + 1)
        return jnp.stack([one, total - one])
    lengths = jnp.asarray(length_profile(amount, total, limit, skew), jnp.int32)
    pairs = (amount - 1) // 2
    giver, taker = lengths[1:1 + 2 * pairs:2], lengths[2:2 + 2 * pairs:2]
    margin = jnp.minimum(giver - 1, limit - taker)
    passed = jax.random.randint(jax.random.fold_in(stream_key, 1), (pairs,), 0, 1 << 20) % (margin + 1)
    lengths = lengths.at[1:1 + 2 * pairs:2].set(giver - passed).at[2:2 + 2 * pairs:2].set(taker + passed)
    return lengths[jax.random.permutation(jax.random.fold_in(stream_key, 2), amount)]


def bell_draw(rng, extent, spread, most, pieces=(), held_as=jnp.bfloat16):
    values = spread * jax.random.normal(rng, extent, jnp.float32)
    if pieces:
        values = values * levels(rng, extent, pieces, -0.22, 0.18)
    return jnp.clip(values, -most, most).astype(held_as)


def setup_inputs(seed: int = 0) -> dict:
    splits = jax.random.split(jax.random.key(seed), 20)
    tokens = bell_draw(splits[0], (MB, SEQS, ROW, D), 1.0, 6.0, ((1, 8), (2, 4)))
    cotangent = bell_draw(splits[1], (MB, SEQS, ROW, D), (50 * D ** -1 * (ROW // SEGS) ** -0.5), 0.078125, ((1, 8), (2, 4)))
    segment_ids = jax.vmap(lambda own: jnp.searchsorted(jnp.cumsum(uneven_parts(own, SEGS, ROW, SEG_MOST, 1)), jnp.arange(ROW), side="right"))(jax.random.split(splits[2], MB * SEQS)).reshape((MB, SEQS, ROW)).astype(jnp.int32)
    targets = plant(jax.random.randint(splits[3], (MB, SEQS, SEGS), 0, NSEG - 1), jax.random.fold_in(splits[3], 1), 0, (NSEG - 1) - 1).astype(jnp.int32)
    attention_weights = draw_attention_weights(jax.random.fold_in(splits[19], 71), 0)
    feedforward_weights = draw_feedforward_weights(jax.random.fold_in(splits[19], 71), 0)
    projection = bell_draw(splits[6], (D, D), D ** -0.5, 0.21875, ((0, 8), (1, 4)), jnp.float32)
    norm_gains = draw_norm_gains(jax.random.fold_in(splits[19], 71), 0)
    bias_table = bell_draw(splits[8], (NB, H), 1.0, 4.0, (), jnp.float32)
    attention_first = bell_draw(splits[9], (4, D, D), (0.111 * (5 * D * D + 2 * D * FF + 3 * D + NB * H) ** -0.5), 0.00061035156, ((1, 8), (2, 4)), jnp.float32)
    attention_second = jnp.clip(jnp.exp(math.log(5.21485188365034e-10) - 1.3862944 * jax.random.uniform(splits[10], (4, D, D), jnp.float32) ** levels(splits[10], (4, D, D), ((1, 8), (2, 4)), -0.2, 0.2)), 1.303712970912585e-10, 5.21485188365034e-10)
    feedforward_first = bell_draw(splits[11], (2, D, FF), (0.111 * (5 * D * D + 2 * D * FF + 3 * D + NB * H) ** -0.5), 0.00061035156, ((1, 8), (2, 4)), jnp.float32)
    feedforward_second = jnp.clip(jnp.exp(math.log(5.21485188365034e-10) - 1.3862944 * jax.random.uniform(splits[12], (2, D, FF), jnp.float32) ** levels(splits[12], (2, D, FF), ((1, 8), (2, 4)), -0.2, 0.2)), 1.303712970912585e-10, 5.21485188365034e-10)
    projection_first = bell_draw(splits[13], (D, D), (0.111 * (5 * D * D + 2 * D * FF + 3 * D + NB * H) ** -0.5), 0.00061035156, ((0, 8), (1, 4)), jnp.float32)
    projection_second = jnp.clip(jnp.exp(math.log(5.21485188365034e-10) - 1.3862944 * jax.random.uniform(splits[14], (D, D), jnp.float32) ** levels(splits[14], (D, D), ((0, 8), (1, 4)), -0.2, 0.2)), 1.303712970912585e-10, 5.21485188365034e-10)
    gains_first = bell_draw(splits[15], (3, D), (0.111 * (5 * D * D + 2 * D * FF + 3 * D + NB * H) ** -0.5), 0.00061035156, (), jnp.float32)
    gains_second = jnp.clip(jnp.exp(jax.random.uniform(splits[16], (3, D), jnp.float32, math.log(1.303712970912585e-10), math.log(5.21485188365034e-10))), 1.303712970912585e-10, 5.21485188365034e-10)
    bias_first = bell_draw(splits[17], (NB, H), (0.111 * (5 * D * D + 2 * D * FF + 3 * D + NB * H) ** -0.5), 0.00061035156, (), jnp.float32)
    bias_second = jnp.clip(jnp.exp(jax.random.uniform(splits[18], (NB, H), jnp.float32, math.log(1.303712970912585e-10), math.log(5.21485188365034e-10))), 1.303712970912585e-10, 5.21485188365034e-10)
    return dict(tokens=tokens, cotangent=cotangent, segment_ids=segment_ids, targets=targets, attention_weights=attention_weights, feedforward_weights=feedforward_weights, projection=projection, norm_gains=norm_gains, bias_table=bias_table, attention_first=attention_first, attention_second=attention_second, feedforward_first=feedforward_first, feedforward_second=feedforward_second, projection_first=projection_first, projection_second=projection_second, gains_first=gains_first, gains_second=gains_second, bias_first=bias_first, bias_second=bias_second)


@jax.custom_vjp
def low(v):
    return lax.optimization_barrier(v.astype(jnp.bfloat16)).astype(jnp.float32)

@jax.custom_vjp
def low_back(v):
    return v

def low_keep(v):
    return (low(v), None)

def low_pass(kept, grad):
    return (grad,)

def back_keep(v):
    return (v, None)

def back_low(kept, grad):
    return (low(grad),)
low.defvjp(low_keep, low_pass)
low_back.defvjp(back_keep, back_low)
EPS_NORM = 1e-06
EPS_ADAM = 1e-08
SIM_SCALE = 50.0
NEG_FILL = -1000000000.0
BETA_ONE = 0.9
BETA_TWO = 0.999
CLIP_NORM = 1.0
RATE_MATRIX = 0.05
RATE_SMALL = 0.2
DECAY_MATRIX = 0.01
LIMITS = (12, 16, 23, 32, 46, 64, 91)
HIGHEST = lax.Precision.HIGHEST

def bucket_of(relative):
    distance = jnp.abs(relative)
    far_bucket = 8 + sum(((distance >= threshold).astype(jnp.int32) for threshold in LIMITS))
    near_bucket = jnp.where(distance < 8, distance, far_bucket)
    return near_bucket + 16 * (relative > 0).astype(jnp.int32)

def rms_scale(values):
    return values * lax.rsqrt(lax.optimization_barrier(jnp.mean(values * values, axis=-1, keepdims=True)) + EPS_NORM)

def product(left_side, right_side):
    return jnp.dot(left_side, right_side, precision=HIGHEST, preferred_element_type=jnp.float32)

def row_forward(row_tokens, row_segments, weights_low, norm_gains, bias_table, bucket_grid):
    attn_low, ffn_low, proj_low = weights_low
    length = row_tokens.shape[0]
    normed_one = low(rms_scale(row_tokens) * norm_gains[0])
    queries = low(low_back(product(normed_one, attn_low[0]))).reshape(length, H, HD)
    keys_all = low(low_back(product(normed_one, attn_low[1]))).reshape(length, H, HD)
    values_all = low(low_back(product(normed_one, attn_low[2]))).reshape(length, H, HD)
    raw_scores = jnp.einsum('qhd,khd->hqk', queries, keys_all, precision=HIGHEST) * HD ** (-0.5)
    bias_grid = jnp.transpose(bias_table[bucket_grid], (2, 0, 1))
    same_segment = row_segments[:, None] == row_segments[None, :]
    scores = low_back(jnp.where(same_segment[None], raw_scores + bias_grid, NEG_FILL))
    probs = jax.nn.softmax(scores, axis=-1)
    mixed = jnp.einsum('hqk,khd->qhd', low(probs), values_all, precision=HIGHEST).reshape(length, D)
    mixed = low(low_back(mixed))
    hidden_one = row_tokens + low_back(product(mixed, attn_low[3].T))
    normed_two = low(rms_scale(hidden_one) * norm_gains[1])
    pre_act = low_back(product(normed_two, ffn_low[0]))
    activated = low(jax.nn.gelu(pre_act))
    hidden_two = hidden_one + low_back(product(activated, ffn_low[1].T))
    normed_three = rms_scale(hidden_two) * norm_gains[2]
    member = (row_segments[None, :] == jnp.arange(SEGS, dtype=jnp.int32)[:, None]).astype(jnp.float32)
    counts = lax.optimization_barrier(jnp.sum(member, axis=1, keepdims=True))
    pooled = product(member, normed_three) / counts
    embedded = low_back(product(low(pooled), proj_low))
    unit = embedded * lax.rsqrt(lax.optimization_barrier(jnp.sum(embedded * embedded, axis=1, keepdims=True)) + EPS_NORM)
    return (hidden_two, unit)

def objective(params, inputs, segment_rows, picked, cotangent_rows, bucket_grid):
    attention_weights, feedforward_weights, projection, norm_gains, bias_table = params
    weights_low = (low(attention_weights), low(feedforward_weights), low(projection))

    def one_row(row_pair):
        return row_forward(row_pair[0], row_pair[1], weights_low, norm_gains, bias_table, bucket_grid)
    hidden, units = lax.map(jax.checkpoint(one_row), (inputs, segment_rows))
    units = low(low_back(units.reshape(MB, NSEG, D)))
    sims = jnp.einsum('bid,bjd->bij', units, units, precision=HIGHEST)
    self_mask = jnp.eye(NSEG, dtype=bool)
    logits = low_back(jnp.where(self_mask[None], NEG_FILL, SIM_SCALE * sims))
    log_total = jax.nn.logsumexp(logits, axis=-1)
    chosen = jnp.take_along_axis(logits, picked[..., None], axis=-1)[..., 0]
    total = jnp.sum(cotangent_rows * hidden) + jnp.sum(log_total - chosen)
    return (total, hidden)

def adam_update(weight_now, clipped, first_old, second_old, step_rate, weight_decay):
    first_new = BETA_ONE * first_old + (1.0 - BETA_ONE) * clipped
    second_new = BETA_TWO * second_old + (1.0 - BETA_TWO) * clipped * clipped
    first_hat = first_new / (1.0 - BETA_ONE ** STEP)
    second_hat = second_new / (1.0 - BETA_TWO ** STEP)
    weight_new = weight_now - step_rate * (first_hat / (jnp.sqrt(second_hat) + EPS_ADAM) + weight_decay * weight_now)
    return (weight_new, first_new, second_new)

def reference(tokens, cotangent, segment_ids, targets, attention_weights, feedforward_weights, projection, norm_gains, bias_table, attention_first, attention_second, feedforward_first, feedforward_second, projection_first, projection_second, gains_first, gains_second, bias_first, bias_second):
    inputs = tokens.astype(jnp.float32).reshape(MB * SEQS, ROW, D)
    cotangent_rows = cotangent.astype(jnp.float32).reshape(MB * SEQS, ROW, D)
    segment_rows = segment_ids.reshape(MB * SEQS, ROW)
    flat_targets = targets.reshape(MB, NSEG)
    positions = jnp.arange(NSEG, dtype=jnp.int32)
    picked = flat_targets + (flat_targets >= positions[None, :]).astype(jnp.int32)
    spots = jnp.arange(ROW, dtype=jnp.int32)
    bucket_grid = bucket_of(spots[None, :] - spots[:, None])
    params = (attention_weights, feedforward_weights, projection, norm_gains, bias_table)

    def closed(param_set, token_set):
        return objective(param_set, token_set, segment_rows, picked, cotangent_rows, bucket_grid)
    total, pullback, hidden = jax.vjp(closed, params, inputs, has_aux=True)
    gradients, tokens_grad = pullback(jnp.ones_like(total))
    squares = sum((jnp.sum(gradient * gradient) for gradient in gradients))
    grad_norm = jnp.sqrt(squares)
    factor = jnp.minimum(1.0, CLIP_NORM / (grad_norm + 1e-06))
    firsts = (attention_first, feedforward_first, projection_first, gains_first, bias_first)
    seconds = (attention_second, feedforward_second, projection_second, gains_second, bias_second)
    rates = (RATE_MATRIX, RATE_MATRIX, RATE_MATRIX, RATE_SMALL, RATE_SMALL)
    decays = (DECAY_MATRIX, DECAY_MATRIX, DECAY_MATRIX, 0.0, 0.0)
    results = []
    for weight_now, gradient, first_old, second_old, step_rate, weight_decay in zip(params, gradients, firsts, seconds, rates, decays):
        results.extend(adam_update(weight_now, gradient * factor, first_old, second_old, step_rate, weight_decay))
    output = hidden.astype(jnp.bfloat16).reshape(MB, SEQS, ROW, D)
    tokens_grad = tokens_grad.reshape(MB, SEQS, ROW, D)
    return (output, tokens_grad, grad_norm, results[0], results[1], results[2], results[3], results[4], results[5], results[6], results[7], results[8], results[9], results[10], results[11], results[12], results[13], results[14])
```

```python
import functools

import jax
import jax.numpy as jnp
from jax import lax
from jax.experimental import pallas as pl
from jax.experimental.pallas import tpu as pltpu
from jax.sharding import PartitionSpec as P

D = 768
HD = 64
STEP = 10
SEG_MOST = 512

EPS_NORM = 1e-06
EPS_ADAM = 1e-08
SIM_SCALE = 50.0
NEG_FILL = -1000000000.0
BETA_ONE = 0.9
BETA_TWO = 0.999
CLIP_NORM = 1.0
RATE_MATRIX = 0.05
RATE_SMALL = 0.2
DECAY_MATRIX = 0.01
LIMITS = (12, 16, 23, 32, 46, 64, 91)
FAR = LIMITS[-1]
MASKED = -float(2**30)
HIGHEST = lax.Precision.HIGHEST
BF16 = jnp.bfloat16
F32 = jnp.float32
NN = (((1,), (0,)), ((), ()))
NT = (((1,), (1,)), ((), ()))
TN = (((0,), (0,)), ((), ()))
VMEM_LIMIT = 48 * 1024 * 1024


def dot(left, right, dims=NN, precision=None):
    return lax.dot_general(left, right, dims, precision=precision, preferred_element_type=F32)


def bucket_of(relative):
    distance = jnp.abs(relative)
    far_bucket = 8 + sum(((distance >= threshold).astype(jnp.int32) for threshold in LIMITS))
    near_bucket = jnp.where(distance < 8, distance, far_bucket)
    return near_bucket + 16 * (relative > 0).astype(jnp.int32)


def norm_factor(values):
    return lax.rsqrt(jnp.mean(values * values, axis=-1, keepdims=True) + EPS_NORM)


def norm_back(values, factor, upstream):
    return factor * upstream - values * (factor * factor * factor) * jnp.mean(
        upstream * values, axis=-1, keepdims=True
    )


def adam_update(weight_now, clipped, first_old, second_old, step_rate, weight_decay):
    first_new = BETA_ONE * first_old + (1.0 - BETA_ONE) * clipped
    second_new = BETA_TWO * second_old + (1.0 - BETA_TWO) * clipped * clipped
    first_hat = first_new / (1.0 - BETA_ONE**STEP)
    second_hat = second_new / (1.0 - BETA_TWO**STEP)
    weight_new = weight_now - step_rate * (
        first_hat / (jnp.sqrt(second_hat) + EPS_ADAM) + weight_decay * weight_now
    )
    return (weight_new, first_new, second_new)


def swap(values, axis, mask):
    count = lax.axis_size(axis)
    return lax.ppermute(values, axis, [(i, i ^ mask) for i in range(count)])


def shift(values, axis, step):
    count = lax.axis_size(axis)
    pairs = [(i, i + step) for i in range(count) if 0 <= i + step < count]
    return lax.ppermute(values, axis, pairs)


def outer_masks():
    return [1 << bit for bit in range(1, lax.axis_size("dp").bit_length() - 1)]


def core_masks():
    return [1] if lax.axis_size("dp") > 1 else []


def gather_columns(values):
    count = lax.axis_size("mp")
    return jnp.concatenate([values] + [swap(values, "mp", k) for k in range(1, count)], axis=-1)


def gather_rows(values, low_first):
    held = values[:, None]
    order = outer_masks()
    for mask in order if low_first else order[::-1]:
        other = swap(held, "dp", mask)
        if low_first:
            held = jnp.concatenate([held, other], axis=1)
        else:
            c, n, r, w = held.shape
            held = jnp.stack([held, other], axis=2).reshape(c, 2 * n, r, w)
    for mask in core_masks():
        held = jnp.concatenate([held, swap(held, "dp", mask)], axis=1)
    c, n, r, w = held.shape
    return held.reshape(c, n * r, w)


def reduce_rows(values, low_first):
    count = lax.axis_size("dp")
    c, _, w = values.shape
    held = values.reshape(c, count, D // count, w)
    for mask in core_masks():
        half = held.shape[1] // 2
        other = swap(held[:, half:].astype(BF16), "dp", mask)
        held = held[:, :half].astype(F32) + other.astype(F32)
    order = outer_masks()
    for mask in order if low_first else order[::-1]:
        half = held.shape[1] // 2
        if low_first:
            parts = held.reshape(c, half, 2, D // count, w)
            stay, leave = parts[:, :, 0], parts[:, :, 1]
        else:
            stay, leave = held[:, :half], held[:, half:]
        other = swap(leave.astype(BF16), "dp", mask)
        held = stay.astype(F32) + other.astype(F32)
    return held.reshape(c, D // count, w)


def reduce_columns(values):
    count = lax.axis_size("mp")
    width = values.shape[-1] // count
    parts = [values[..., k * width : (k + 1) * width] for k in range(count)]
    total = parts[0].astype(F32)
    for k in range(1, count):
        total = total + swap(parts[k].astype(BF16), "mp", k).astype(F32)
    return total


def sum_over(values, axis):
    bit = 1
    while bit < lax.axis_size(axis):
        values = values + swap(values, axis, bit)
        bit *= 2
    return values


def gather_near(values):
    bit = 1
    while bit < lax.axis_size("dp"):
        values = jnp.concatenate([values, swap(values, "dp", bit)], axis=0)
        bit *= 2
    return values


def bias_kernel(line_ref, tile_ref):
    rows = tile_ref.shape[2]
    for block in range(tile_ref.shape[1]):
        line = jnp.broadcast_to(line_ref[0, block : block + 1, :], (rows, 2 * rows))
        tile_ref[0, block] = pltpu.roll(line, 0, 1, stride=1, stride_axis=0)[:, :rows]


def bias_tiles(table, rows):
    heads = table.shape[1]
    lane = jnp.arange(2 * rows, dtype=jnp.int32)
    back = jnp.where(lane < rows, lane, lane - 2 * rows)
    relative = (jnp.arange(3, dtype=jnp.int32)[:, None] - 1) * rows - back[None, :]
    hot = (bucket_of(relative)[..., None] == jnp.arange(table.shape[0])).astype(F32)
    lines = dot(table, hot.reshape(-1, table.shape[0]), (((0,), (1,)), ((), ())), HIGHEST)
    lines = lines.reshape(heads, 3, 2 * rows)
    return pl.pallas_call(
        bias_kernel,
        grid=(heads,),
        in_specs=[pl.BlockSpec((1, 3, 2 * rows), lambda h: (h, 0, 0))],
        out_specs=pl.BlockSpec((1, 3, rows, rows), lambda h: (h, 0, 0, 0)),
        out_shape=jax.ShapeDtypeStruct((heads, 3, rows, rows), F32),
        compiler_params=pltpu.CompilerParams(vmem_limit_bytes=VMEM_LIMIT),
    )(lines)


def own_lanes(shape, part):
    lane = lax.broadcasted_iota(jnp.int32, shape, 1)
    return (lane < HD) if part == 0 else (lane >= HD)


def block_choices(reach):
    return [
        (lo, hi) for lo in range(reach + 1) for hi in range(reach + 1) if lo + hi < 2 * reach
    ]


def forward_kernel(reach, range_ref, far_ref, q_ref, k_ref, v_ref, qf_ref, kf_ref, bias_ref, o_ref, log_ref):
    pair = pl.program_id(0)
    rows = q_ref.shape[0]
    score_scale = HD ** (-0.5)

    def work(lo, hi):
        query = q_ref[...] * jnp.asarray(score_scale, BF16)
        mixed, logs = [], []
        for part in range(2):
            own_q = own_lanes((rows, 2 * HD), part)
            query_low = jnp.where(own_q, query, qf_ref[...])
            scores = []
            for block in range(-lo, hi + 1):
                spot = pl.ds((block + reach) * rows, rows)
                key_low = jnp.where(own_q, k_ref[spot, :], kf_ref[spot, :])
                score = dot(key_low, query_low, NT)
                if abs(block) <= 1:
                    score = score + bias_ref[part, block + 1]
                else:
                    score = score + far_ref[int(block > 0), 2 * pair + part]
                scores.append(score)
            peak = jnp.max(functools.reduce(jnp.maximum, scores), axis=0, keepdims=True)
            total = jnp.zeros((2 * HD, rows), F32)
            for number, block in enumerate(range(-lo, hi + 1)):
                spot = pl.ds((block + reach) * rows, rows)
                probs = jnp.exp(scores[number] - peak).astype(BF16)
                value_low = jnp.where(own_q, v_ref[spot, :], jnp.ones((), BF16))
                total = total + dot(value_low, probs, TN)
            row_sum = total[HD * (1 - part) : HD * (1 - part) + 1, :]
            mixed.append(total[HD * part : HD * (part + 1), :] / row_sum)
            logs.append(peak + jnp.log(row_sum))
        o_ref[...] = jnp.concatenate(mixed, axis=0).T.astype(BF16)
        log_ref[0] = jnp.concatenate(logs + [jnp.zeros((6, rows), F32)], axis=0)

    for lo, hi in block_choices(reach):
        pl.when((range_ref[0] == lo) & (range_ref[1] == hi))(functools.partial(work, lo, hi))


def backward_kernel(
    reach, range_ref, far_ref, q_ref, k_ref, v_ref, qf_ref, kf_ref, bias_ref, do_ref, o_ref, log_ref,
    dq_ref, dk_ref, dv_ref, db_ref,
):
    pair = pl.program_id(0)
    rows = q_ref.shape[0]
    score_scale = HD ** (-0.5)

    def work(lo, hi):
        query = q_ref[...] * jnp.asarray(score_scale, BF16)
        upstream = do_ref[...]
        products = (upstream.astype(F32) * o_ref[...].astype(F32)).T
        nothing = jnp.zeros((), BF16)
        ahead = lax.broadcasted_iota(jnp.int32, (rows, rows), 0) - lax.broadcasted_iota(
            jnp.int32, (rows, rows), 1
        )
        own, query_low, query_own, up_own, delta, log_row, dq, near, far = ([None, None] for _ in range(9))
        for part in range(2):
            own[part] = own_lanes((rows, 2 * HD), part)
            query_low[part] = jnp.where(own[part], query, qf_ref[...])
            query_own[part] = jnp.where(own[part], query, nothing)
            up_own[part] = jnp.where(own[part], upstream, nothing)
            delta[part] = jnp.sum(products[HD * part : HD * (part + 1), :], axis=0, keepdims=True)
            log_row[part] = log_ref[0, part : part + 1, :]
            dq[part] = jnp.zeros((2 * HD, rows), F32)
            near[part] = jnp.zeros((rows, rows), F32)
            far[part] = [jnp.zeros((1, rows), F32), jnp.zeros((1, rows), F32)]
        for block in range(-reach, reach + 1):
            spot = pl.ds((block + reach) * rows, rows)
            if not -lo <= block <= hi:
                dk_ref[spot, :] = jnp.zeros((rows, 2 * HD), BF16)
                dv_ref[spot, :] = jnp.zeros((rows, 2 * HD), BF16)
                continue
            dk = jnp.zeros((rows, 2 * HD), F32)
            dv = jnp.zeros((rows, 2 * HD), F32)
            for part in range(2):
                key = k_ref[spot, :]
                score = dot(jnp.where(own[part], key, kf_ref[spot, :]), query_low[part], NT)
                if abs(block) <= 1:
                    score = score + bias_ref[part, block + 1]
                else:
                    score = score + far_ref[int(block > 0), 2 * pair + part]
                probs = jnp.exp(score - log_row[part])
                dprobs = dot(v_ref[spot, :], up_own[part], NT)
                dscore = probs * (dprobs - delta[part])
                probs_low, dscore_low = probs.astype(BF16), dscore.astype(BF16)
                dv = dv + dot(probs_low, up_own[part])
                dk = dk + dot(dscore_low, query_own[part])
                dq[part] = dq[part] + dot(key, dscore_low, TN)
                if block == 0:
                    close = jnp.abs(ahead) < FAR
                    near[part] = near[part] + jnp.where(close, dscore, 0.0)
                    far[part][0] += jnp.sum(jnp.where(ahead <= -FAR, dscore, 0.0), axis=0, keepdims=True)
                    far[part][1] += jnp.sum(jnp.where(ahead >= FAR, dscore, 0.0), axis=0, keepdims=True)
                elif abs(block) == 1:
                    close = (ahead < FAR - rows) if block > 0 else (ahead > rows - FAR)
                    near[part] = near[part] + jnp.where(close, dscore, 0.0)
                    far[part][int(block > 0)] += jnp.sum(jnp.where(close, 0.0, dscore), axis=0, keepdims=True)
                else:
                    far[part][int(block > 0)] += jnp.sum(dscore, axis=0, keepdims=True)
            dk_ref[spot, :] = dk.astype(BF16)
            dv_ref[spot, :] = dv.astype(BF16)
        dq_ref[...] = (
            jnp.concatenate([dq[0][:HD], dq[1][HD:]], axis=0).T * score_scale
        ).astype(BF16)
        flip = (
            lax.broadcasted_iota(jnp.int32, (rows, rows), 0) + lax.broadcasted_iota(jnp.int32, (rows, rows), 1)
            == rows - 1
        ).astype(BF16)
        for part in range(2):
            turned = dot(flip, near[part].astype(BF16))
            turned = pltpu.roll(turned, 0, 1, stride=1, stride_axis=0)
            line = jnp.sum(turned, axis=0, keepdims=True)
            db_ref[0, part] = jnp.concatenate(
                [line, far[part][0], far[part][1], jnp.zeros((5, rows), F32)], axis=0
            )

    for lo, hi in block_choices(reach):
        pl.when((range_ref[0] == lo) & (range_ref[1] == hi))(functools.partial(work, lo, hi))


def attention_specs(rows, window, pairs):
    smem = pl.BlockSpec(memory_space=pltpu.SMEM)
    return [
        smem,
        smem,
        pl.BlockSpec((rows, 2 * HD), lambda p: (0, p)),
        pl.BlockSpec((window, 2 * HD), lambda p: (0, p)),
        pl.BlockSpec((window, 2 * HD), lambda p: (0, p)),
        pl.BlockSpec((rows, 2 * HD), lambda p: (0, 0)),
        pl.BlockSpec((window, 2 * HD), lambda p: (0, 0)),
        pl.BlockSpec((2, 3, rows, rows), lambda p: (p, 0, 0, 0)),
    ]


def attend(reach, *operands):
    rows, width = operands[2].shape
    window = operands[3].shape[0]
    pairs = width // (2 * HD)
    return pl.pallas_call(
        functools.partial(forward_kernel, reach),
        grid=(pairs,),
        in_specs=attention_specs(rows, window, pairs),
        out_specs=[
            pl.BlockSpec((rows, 2 * HD), lambda p: (0, p)),
            pl.BlockSpec((1, 8, rows), lambda p: (p, 0, 0)),
        ],
        out_shape=[
            jax.ShapeDtypeStruct((rows, width), BF16),
            jax.ShapeDtypeStruct((pairs, 8, rows), F32),
        ],
        compiler_params=pltpu.CompilerParams(vmem_limit_bytes=VMEM_LIMIT),
        name="attend",
    )(*operands)


def attend_back(reach, *operands):
    rows, width = operands[2].shape
    window = operands[3].shape[0]
    pairs = width // (2 * HD)
    tall = pl.BlockSpec((window, 2 * HD), lambda p: (0, p))
    short = pl.BlockSpec((rows, 2 * HD), lambda p: (0, p))
    return pl.pallas_call(
        functools.partial(backward_kernel, reach),
        grid=(pairs,),
        in_specs=attention_specs(rows, window, pairs)
        + [short, short, pl.BlockSpec((1, 8, rows), lambda p: (p, 0, 0))],
        out_specs=[short, tall, tall, pl.BlockSpec((1, 2, 8, rows), lambda p: (p, 0, 0, 0))],
        out_shape=[
            jax.ShapeDtypeStruct((rows, width), BF16),
            jax.ShapeDtypeStruct((window, width), BF16),
            jax.ShapeDtypeStruct((window, width), BF16),
            jax.ShapeDtypeStruct((pairs, 2, 8, rows), F32),
        ],
        compiler_params=pltpu.CompilerParams(vmem_limit_bytes=VMEM_LIMIT),
        name="attend_back",
    )(*operands)


def local(
    tokens,
    cotangent,
    segment_ids,
    targets,
    attention_weights,
    feedforward_weights,
    projection,
    norm_gains,
    bias_table,
    attention_first,
    attention_second,
    feedforward_first,
    feedforward_second,
    projection_first,
    projection_second,
    gains_first,
    gains_second,
    bias_first,
    bias_second,
):
    wide_count = lax.axis_size("dp")
    narrow_count = lax.axis_size("mp")
    wide_rank = lax.axis_index("dp")
    narrow_rank = lax.axis_index("mp")
    micro_count, _, rows, _ = tokens.shape
    segment_count = targets.shape[2]
    block = D // wide_count
    heads_part = attention_weights.shape[2] // HD
    reach = min(narrow_count - 1, -(-(SEG_MOST - 1) // rows))
    span = 2 * reach + 1

    feature = jnp.arange(D, dtype=jnp.int32)
    place = feature // block
    order = outer_masks() + core_masks()
    away = sum(((place >> bit) & 1) * mask for bit, mask in enumerate(order)) + jnp.zeros_like(place)
    source = (wide_rank ^ away) * block + feature % block
    turn = (feature[:, None] == source[None, :]).astype(BF16)
    turn_wide = turn.astype(F32)

    attention_low = attention_weights.astype(BF16)
    feedforward_low = feedforward_weights.astype(BF16)
    projection_low = projection.astype(BF16)

    token_rows = dot(tokens.reshape(micro_count * rows, D), turn)
    gains = dot(norm_gains, turn_wide, precision=HIGHEST)
    factor_one = norm_factor(token_rows)
    normed_one = (token_rows * factor_one * gains[0]).astype(BF16)
    normed_one = normed_one.reshape(micro_count, rows, D)

    attn_cols = gather_columns(attention_low)
    attn_qo = gather_rows(jnp.stack([attn_cols[0], attn_cols[3]]), True)
    attn_kv = gather_rows(attn_cols[1:3], False)
    w_query, w_out = attn_qo[0], attn_qo[1]
    w_key, w_value = attn_kv[0], attn_kv[1]

    windows = []
    for micro in range(micro_count):
        left, right = [], []
        from_left = from_right = normed_one[micro]
        for _ in range(reach):
            from_left, from_right = shift(from_left, "mp", 1), shift(from_right, "mp", -1)
            left.insert(0, from_left)
            right.append(from_right)
        windows.append(jnp.concatenate(left + [normed_one[micro]] + right, axis=0))

    ffn_cols = gather_columns(feedforward_low)
    w_up = gather_rows(ffn_cols[0:1], True)[0]
    w_down = gather_rows(ffn_cols[1:2], False)[0]
    proj_all = lax.all_gather(projection_low, ("dp", "mp"), axis=0, tiled=False)
    proj_all = proj_all.reshape(wide_count, narrow_count, block, D // narrow_count)
    proj_all = proj_all.transpose(0, 2, 1, 3).reshape(D, D)

    table = jnp.concatenate(
        [
            lax.dynamic_slice_in_dim(bias_table, (narrow_rank ^ k) * heads_part, heads_part, 1)
            for k in range(narrow_count)
        ],
        axis=1,
    )
    tiles = bias_tiles(table, rows)
    far_bias = jnp.stack([table[15], table[31]])
    lanes = jnp.arange(2 * HD, dtype=jnp.int32) % HD
    padded = jnp.pad(
        segment_ids[:, 0], ((0, 0), (reach * rows, reach * rows)), constant_values=segment_count
    )
    window_segments = lax.dynamic_slice_in_dim(padded, narrow_rank * rows, span * rows, 1)
    own_segments = window_segments[:, reach * rows : (reach + 1) * rows]
    key_marks = (window_segments[:, :, None] == lanes).astype(BF16)
    query_marks = jnp.where(
        (own_segments[:, :, None] != lanes) & (lanes <= segment_count), MASKED, 0.0
    ).astype(BF16)
    first, last = own_segments[:, 0], own_segments[:, -1]
    low_count = sum(
        (window_segments[:, (reach - n) * rows + rows - 1] == first).astype(jnp.int32)
        for n in range(1, reach + 1)
    )
    high_count = sum(
        (window_segments[:, (reach + n) * rows] == last).astype(jnp.int32)
        for n in range(1, reach + 1)
    )
    ranges = jnp.stack([low_count, high_count], axis=1)

    mixed, kept = [], []
    for micro in range(micro_count):
        queries = dot(normed_one[micro], w_query).astype(BF16)
        keys = dot(windows[micro], w_key).astype(BF16)
        values = dot(windows[micro], w_value).astype(BF16)
        operands = (
            ranges[micro], far_bias, queries, keys, values, query_marks[micro], key_marks[micro], tiles
        )
        mixed_part, logs = attend(reach, *operands)
        mixed.append(mixed_part)
        kept.append((operands, mixed_part, logs))
    mixed = jnp.concatenate(mixed, axis=0)
    hidden_one = token_rows + dot(mixed, w_out, NT)

    factor_two = norm_factor(hidden_one)
    normed_two = (hidden_one * factor_two * gains[1]).astype(BF16)
    pre_act = dot(normed_two, w_up)
    activated, gelu_pull = jax.vjp(jax.nn.gelu, pre_act)
    activated = activated.astype(BF16)
    hidden_two = hidden_one + dot(activated, w_down, NT)
    output = dot(hidden_two.astype(BF16), turn, NT).astype(BF16)

    factor_three = norm_factor(hidden_two)
    unit_three = hidden_two * factor_three
    normed_three = (unit_three * gains[2]).reshape(micro_count, rows, D)
    numbers = jnp.arange(segment_count, dtype=jnp.int32)
    member = (own_segments[:, None, :] == numbers[None, :, None]).astype(F32)
    counts = jnp.sum(
        (segment_ids[:, 0][:, None, :] == numbers[None, :, None]).astype(F32), axis=2, keepdims=True
    )
    pooled = lax.dot_general(
        member, normed_three, (((2,), (1,)), ((0,), (0,))), precision=HIGHEST, preferred_element_type=F32
    )
    pooled = sum_over(pooled, "mp") / counts
    pooled = dot(pooled.reshape(-1, D).astype(BF16), turn, NT).astype(BF16)
    pooled_all = gather_near(pooled.reshape(1, micro_count, segment_count, D))
    targets_all = gather_near(targets[:, 0].astype(F32)[None])
    every = wide_count * segment_count
    pooled_all = pooled_all.transpose(1, 0, 2, 3).reshape(micro_count, every, D)
    owner = wide_rank ^ jnp.arange(wide_count, dtype=jnp.int32)
    absolute = (owner[:, None] * segment_count + numbers[None, :]).reshape(every)
    picked = targets_all.astype(jnp.int32).transpose(1, 0, 2).reshape(micro_count, every)
    picked = picked + (picked >= absolute[None]).astype(jnp.int32)
    embedded = dot(pooled_all.reshape(-1, D), proj_all).reshape(micro_count, every, D)
    inverse = lax.rsqrt(jnp.sum(embedded * embedded, axis=2, keepdims=True) + EPS_NORM)
    unit = (embedded * inverse).astype(BF16)
    sims = lax.dot_general(
        unit, unit, (((2,), (2,)), ((0,), (0,))), preferred_element_type=F32
    )
    logits = jnp.where(jnp.eye(every, dtype=bool)[None], NEG_FILL, SIM_SCALE * sims)
    logit_grad = (
        jax.nn.softmax(logits, axis=-1) - (picked[:, :, None] == absolute[None, None, :]).astype(F32)
    ).astype(BF16)
    unit_grad = SIM_SCALE * (
        lax.dot_general(logit_grad, unit, (((2,), (1,)), ((0,), (0,))), preferred_element_type=F32)
        + lax.dot_general(logit_grad, unit, (((1,), (1,)), ((0,), (0,))), preferred_element_type=F32)
    )
    unit_grad = unit_grad.astype(BF16).astype(F32)
    along = jnp.sum(unit_grad * embedded, axis=2, keepdims=True)
    embed_grad = (
        inverse * unit_grad - embedded * (inverse * inverse * inverse) * along
    ).astype(BF16)
    proj_reduced = dot(
        lax.dynamic_slice_in_dim(pooled_all.reshape(-1, D), wide_rank * block, block, 1),
        lax.dynamic_slice_in_dim(
            embed_grad.reshape(-1, D), narrow_rank * projection.shape[1], projection.shape[1], 1
        ),
        TN,
    )
    pooled_grad = dot(embed_grad[:, :segment_count].reshape(-1, D), proj_all, NT)
    pooled_grad = dot(pooled_grad, turn_wide, precision=HIGHEST)
    pooled_grad = pooled_grad.reshape(micro_count, segment_count, D) / counts
    normed_three_grad = lax.dot_general(
        member, pooled_grad, (((1,), (1,)), ((0,), (0,))), precision=HIGHEST, preferred_element_type=F32
    ).reshape(micro_count * rows, D)
    gain_three = jnp.sum(normed_three_grad * unit_three, axis=0)

    upstream = dot(cotangent.reshape(micro_count * rows, D), turn)
    hidden_two_grad = upstream + norm_back(hidden_two, factor_three, normed_three_grad * gains[2])
    hidden_two_low = hidden_two_grad.astype(BF16)
    act_grad = dot(hidden_two_low, w_down)
    pre_grad = gelu_pull(act_grad)[0].astype(BF16)
    down_part = dot(hidden_two_low, activated, TN).astype(BF16)
    down_rows = reduce_rows(down_part[None], False)
    up_part = dot(normed_two, pre_grad, TN).astype(BF16)
    up_rows = reduce_rows(up_part[None], True)
    ffn_reduced = reduce_columns(jnp.concatenate([up_rows, down_rows]))
    normed_two_grad = dot(pre_grad, w_up, NT)
    gain_two = jnp.sum(normed_two_grad * hidden_one * factor_two, axis=0)
    hidden_one_grad = hidden_two_grad + norm_back(
        hidden_one, factor_two, normed_two_grad * gains[1]
    )
    hidden_one_low = hidden_one_grad.astype(BF16)
    mixed_grad = dot(hidden_one_low, w_out).astype(BF16).reshape(micro_count, rows, D)
    out_part = dot(hidden_one_low, mixed, TN).astype(BF16)

    query_grads, key_grads, value_grads, bias_parts, normed_one_grads = [], [], [], [], []
    for micro in range(micro_count):
        operands, mixed_part, logs = kept[micro]
        dq, dk, dv, db = attend_back(reach, *operands, mixed_grad[micro], mixed_part, logs)
        query_grads.append(dq)
        key_grads.append(dk)
        value_grads.append(dv)
        bias_parts.append(db)
        partial = (dot(dk, w_key, NT) + dot(dv, w_value, NT)).reshape(span, rows, D)
        own = partial[reach] + dot(dq, w_query, NT)
        to_left = to_right = None
        for n in range(reach, 0, -1):
            leave_left, leave_right = partial[reach - n], partial[reach + n]
            if to_left is not None:
                leave_left = leave_left + to_left
                leave_right = leave_right + to_right
            to_left = shift(leave_left.astype(BF16), "mp", -1).astype(F32)
            to_right = shift(leave_right.astype(BF16), "mp", 1).astype(F32)
        normed_one_grads.append(own + to_left + to_right)
    windows_all = jnp.concatenate(windows, axis=0)
    query_part = dot(normed_one.reshape(-1, D), jnp.concatenate(query_grads), TN).astype(BF16)
    key_part = dot(windows_all, jnp.concatenate(key_grads), TN).astype(BF16)
    value_part = dot(windows_all, jnp.concatenate(value_grads), TN).astype(BF16)
    qo_rows = reduce_rows(jnp.stack([query_part, out_part]), True)
    kv_rows = reduce_rows(jnp.stack([key_part, value_part]), False)
    attn_reduced = reduce_columns(
        jnp.concatenate([qo_rows[0:1], kv_rows, qo_rows[1:2]])
    )
    normed_one_grad = jnp.concatenate(normed_one_grads, axis=0)
    gain_one = jnp.sum(normed_one_grad * token_rows * factor_one, axis=0)
    tokens_grad = hidden_one_grad + norm_back(token_rows, factor_one, normed_one_grad * gains[0])
    tokens_grad = dot(tokens_grad, turn_wide, NT, HIGHEST)

    bias_sum = sum(bias_parts)
    heads = table.shape[1]
    bias_sum = bias_sum.reshape(heads, 8, rows)
    spot = (jnp.arange(rows, dtype=jnp.int32) + 1) % rows
    relative = jnp.where(spot < FAR, -spot, rows - spot)
    buckets = jnp.arange(table.shape[0], dtype=jnp.int32)
    near_hot = (bucket_of(relative)[:, None] == buckets[None, :]) & (
        jnp.abs(relative) < FAR
    )[:, None]
    table_grad = dot(near_hot.astype(F32), bias_sum[:, 0], (((0,), (1,)), ((), ())), HIGHEST)
    table_grad = (
        table_grad
        + (buckets == 15).astype(F32)[:, None] * jnp.sum(bias_sum[:, 1], axis=1)[None, :]
        + (buckets == 31).astype(F32)[:, None] * jnp.sum(bias_sum[:, 2], axis=1)[None, :]
    )
    full_table = jnp.zeros_like(bias_table)
    for k in range(narrow_count):
        full_table = lax.dynamic_update_slice_in_dim(
            full_table,
            table_grad[:, k * heads_part : (k + 1) * heads_part],
            (narrow_rank ^ k) * heads_part,
            1,
        )
    gains_part = dot(jnp.stack([gain_one, gain_two, gain_three]), turn_wide, NT, HIGHEST)
    small = jnp.concatenate(
        [gains_part, jnp.pad(full_table.reshape(1, -1), ((0, 0), (0, D - full_table.size)))]
    )
    small = sum_over(sum_over(small, "dp"), "mp")
    gains_grad = small[:3]
    table_full_grad = small[3, : full_table.size].reshape(full_table.shape)
    local_squares = (
        jnp.sum(attn_reduced * attn_reduced)
        + jnp.sum(ffn_reduced * ffn_reduced)
        + jnp.sum(proj_reduced * proj_reduced)
    )
    total_squares = sum_over(
        sum_over(jnp.broadcast_to(local_squares, (8, 128)), "dp"), "mp"
    )[0, 0]
    total_squares = (
        total_squares
        + jnp.sum(gains_grad * gains_grad)
        + jnp.sum(table_full_grad * table_full_grad)
    )
    grad_norm = jnp.sqrt(total_squares)
    factor = jnp.minimum(1.0, CLIP_NORM / (grad_norm + 1e-06))
    attn_new = adam_update(
        attention_weights, attn_reduced * factor, attention_first, attention_second,
        RATE_MATRIX, DECAY_MATRIX,
    )
    ffn_new = adam_update(
        feedforward_weights, ffn_reduced * factor, feedforward_first, feedforward_second,
        RATE_MATRIX, DECAY_MATRIX,
    )
    proj_new = adam_update(
        projection, proj_reduced * factor, projection_first, projection_second,
        RATE_MATRIX, DECAY_MATRIX,
    )
    gains_new = adam_update(
        norm_gains, gains_grad * factor, gains_first, gains_second, RATE_SMALL, 0.0
    )
    table_new = adam_update(
        bias_table, table_full_grad * factor, bias_first, bias_second, RATE_SMALL, 0.0
    )
    return (
        output.reshape(tokens.shape),
        tokens_grad.reshape(tokens.shape),
        grad_norm,
        *attn_new,
        *ffn_new,
        *proj_new,
        *gains_new,
        *table_new,
    )


def solution(mesh):
    return jax.shard_map(
        local,
        mesh=mesh,
        in_specs=(
            P(None, "dp", "mp", None),
            P(None, "dp", "mp", None),
            P(None, "dp", None),
            P(None, "dp", None),
            P(None, "dp", "mp"),
            P(None, "dp", "mp"),
            P("dp", "mp"),
            P(),
            P(),
            P(None, "dp", "mp"),
            P(None, "dp", "mp"),
            P(None, "dp", "mp"),
            P(None, "dp", "mp"),
            P("dp", "mp"),
            P("dp", "mp"),
            P(),
            P(),
            P(),
            P(),
        ),
        out_specs=(
            P(None, "dp", "mp", None),
            P(None, "dp", "mp", None),
            P(),
            P(None, "dp", "mp"),
            P(None, "dp", "mp"),
            P(None, "dp", "mp"),
            P(None, "dp", "mp"),
            P(None, "dp", "mp"),
            P(None, "dp", "mp"),
            P("dp", "mp"),
            P("dp", "mp"),
            P("dp", "mp"),
            P(),
            P(),
            P(),
            P(),
            P(),
            P(),
        ),
        check_vma=False,
    )
```

```python
import functools

import jax
import jax.numpy as jnp
from jax import lax
from jax.experimental import pallas as pl
from jax.experimental.pallas import tpu as pltpu
from jax.sharding import PartitionSpec as P

D = 768
HD = 64
STEP = 10
SEG_MOST = 512

EPS_NORM = 1e-06
EPS_ADAM = 1e-08
SIM_SCALE = 50.0
NEG_FILL = -1000000000.0
BETA_ONE = 0.9
BETA_TWO = 0.999
CLIP_NORM = 1.0
RATE_MATRIX = 0.05
RATE_SMALL = 0.2
DECAY_MATRIX = 0.01
LIMITS = (12, 16, 23, 32, 46, 64, 91)
FAR = LIMITS[-1]
MASKED = -float(2**30)
HIGHEST = lax.Precision.HIGHEST
BF16 = jnp.bfloat16
F32 = jnp.float32
NN = (((1,), (0,)), ((), ()))
NT = (((1,), (1,)), ((), ()))
TN = (((0,), (0,)), ((), ()))
VMEM_LIMIT = 48 * 1024 * 1024


def dot(left, right, dims=NN, precision=None):
    return lax.dot_general(left, right, dims, precision=precision, preferred_element_type=F32)


def bucket_of(relative):
    distance = jnp.abs(relative)
    far_bucket = 8 + sum(((distance >= threshold).astype(jnp.int32) for threshold in LIMITS))
    near_bucket = jnp.where(distance < 8, distance, far_bucket)
    return near_bucket + 16 * (relative > 0).astype(jnp.int32)


def norm_factor(values):
    return lax.rsqrt(jnp.mean(values * values, axis=-1, keepdims=True) + EPS_NORM)


def norm_back(values, factor, upstream):
    return factor * upstream - values * (factor * factor * factor) * jnp.mean(
        upstream * values, axis=-1, keepdims=True
    )


def adam_update(weight_now, clipped, first_old, second_old, step_rate, weight_decay):
    first_new = BETA_ONE * first_old + (1.0 - BETA_ONE) * clipped
    second_new = BETA_TWO * second_old + (1.0 - BETA_TWO) * clipped * clipped
    first_hat = first_new / (1.0 - BETA_ONE**STEP)
    second_hat = second_new / (1.0 - BETA_TWO**STEP)
    weight_new = weight_now - step_rate * (
        first_hat / (jnp.sqrt(second_hat) + EPS_ADAM) + weight_decay * weight_now
    )
    return (weight_new, first_new, second_new)


def swap(values, axis, mask):
    count = lax.axis_size(axis)
    return lax.ppermute(values, axis, [(i, i ^ mask) for i in range(count)])


def link(values, odd):
    count = lax.axis_size("mp")
    pairs = [(i, i + 1) for i in range(int(odd), count - 1, 2)]
    return lax.ppermute(values, "mp", pairs + [(j, i) for i, j in pairs])


def gather_columns_chain(values):
    bit = 1
    while bit < lax.axis_size("mp"):
        values = jnp.concatenate([values, swap(values, "mp", bit)], axis=-1)
        bit *= 2
    return values


def after(values, *earlier):
    return lax.optimization_barrier((values,) + earlier)[0]


def outer_masks():
    return [1 << bit for bit in range(1, lax.axis_size("dp").bit_length() - 1)]


def core_masks():
    return [1] if lax.axis_size("dp") > 1 else []


def gather_columns(values):
    return [swap(values, "mp", k) for k in range(1, lax.axis_size("mp"))]


def plane_masks():
    masks = [0]
    for mask in outer_masks():
        masks += [held | mask for held in masks]
    return masks[1:]


def gather_plane(values):
    return jnp.stack([values] + [swap(values, "dp", mask) for mask in plane_masks()], axis=1)


def halves(values):
    c, n, r, w = values.shape
    near = values.reshape(c, n * r, w)
    return near, swap(near, "dp", 1)


def to_blocks(values):
    c, rows, w = values.shape
    count = lax.axis_size("dp") // 2
    return values.reshape(c, count, rows // count, w)


def add_low(stay, *received):
    return sum([part.astype(F32) for part in received], stay.astype(F32)).astype(BF16)


def split_outer(terms, masks, first):
    spot = 0 if first else len(masks) - 1
    n, r, w = terms[0].shape
    split = [term.reshape(n >> (spot + 1), 2, 1 << spot, r, w) for term in terms]
    stay, leave = ([term[:, k].reshape(n // 2, r, w) for term in split] for k in range(2))
    return stay, add_low(*leave), masks[spot], masks[:spot] + masks[spot + 1 :]


def gather_outer(part, number, low_first):
    masks = outer_masks()
    return swap(part, "dp", masks[number] if low_first else masks[len(masks) - 1 - number])


def join_outer(part, received, low_first):
    if low_first:
        return jnp.concatenate([part, received], axis=0)
    n, r, w = part.shape
    return jnp.stack([part, received], axis=1).reshape(2 * n, r, w)


def send_plane(held):
    return [swap(held[:, number + 1], "dp", mask) for number, mask in enumerate(plane_masks())]


def send_columns(values):
    count = lax.axis_size("mp")
    width = values.shape[-1] // count
    return [swap(values[..., k * width : (k + 1) * width], "mp", k) for k in range(1, count)]


def send_columns_chain(values):
    count = lax.axis_size("mp")
    if count == 1:
        return values[..., :0]
    return swap(values[..., values.shape[-1] // 2 :], "mp", count // 2)


def finish_columns_chain(values, received):
    bit = lax.axis_size("mp") // 2
    while bit:
        half = values.shape[-1] // 2
        values = values[..., :half].astype(F32) + received.astype(F32)
        bit //= 2
        if bit:
            received = swap(values[..., half // 2 :].astype(BF16), "mp", bit)
    return values


def add_columns(values, received):
    width = values.shape[-1] // lax.axis_size("mp")
    return sum([part.astype(F32) for part in received], values[..., :width].astype(F32))


def sum_over(values, axis):
    bit = 1
    while bit < lax.axis_size(axis):
        values = values + swap(values, axis, bit)
        bit *= 2
    return values


def gather_near(values):
    bit = 1
    while bit < lax.axis_size("dp"):
        values = jnp.concatenate([values, swap(values, "dp", bit)], axis=0)
        bit *= 2
    return values


def bias_kernel(line_ref, tile_ref):
    rows = tile_ref.shape[2]
    for block in range(tile_ref.shape[1]):
        line = jnp.broadcast_to(line_ref[0, block : block + 1, :], (rows, 2 * rows))
        tile_ref[0, block] = pltpu.roll(line, 0, 1, stride=1, stride_axis=0)[:, :rows]


def bias_tiles(table, rows):
    heads = table.shape[1]
    lane = jnp.arange(2 * rows, dtype=jnp.int32)
    back = jnp.where(lane < rows, lane, lane - 2 * rows)
    relative = (jnp.arange(3, dtype=jnp.int32)[:, None] - 1) * rows - back[None, :]
    hot = (bucket_of(relative)[..., None] == jnp.arange(table.shape[0])).astype(F32)
    lines = dot(table, hot.reshape(-1, table.shape[0]), (((0,), (1,)), ((), ())), HIGHEST)
    lines = lines.reshape(heads, 3, 2 * rows)
    return pl.pallas_call(
        bias_kernel,
        grid=(heads,),
        in_specs=[pl.BlockSpec((1, 3, 2 * rows), lambda h: (h, 0, 0))],
        out_specs=pl.BlockSpec((1, 3, rows, rows), lambda h: (h, 0, 0, 0)),
        out_shape=jax.ShapeDtypeStruct((heads, 3, rows, rows), F32),
        compiler_params=pltpu.CompilerParams(vmem_limit_bytes=VMEM_LIMIT),
    )(lines)


def own_lanes(shape, part):
    lane = lax.broadcasted_iota(jnp.int32, shape, 1)
    return (lane < HD) if part == 0 else (lane >= HD)


def block_choices(reach):
    return [
        (lo, hi) for lo in range(reach + 1) for hi in range(reach + 1) if lo + hi < 2 * reach
    ]


def whole_rows(near_ref, far_ref, number):
    return jnp.concatenate([near_ref[number], far_ref[number]], axis=0)


def forward_kernel(reach, range_ref, far_ref, q_ref, k_ref, v_ref, qf_ref, kf_ref, bias_ref, o_ref, log_ref):
    pair = pl.program_id(0)
    rows = q_ref.shape[0]
    score_scale = HD ** (-0.5)
    low, high = range_ref[0], range_ref[1]

    def slot_of(block):
        return pl.ds(pl.multiple_of(range_ref[2 + block + reach] * rows, rows), rows)

    def work(lo, hi):
        query = q_ref[...] * jnp.asarray(score_scale, BF16)
        mixed, logs = [], []
        for part in range(2):
            own_q = own_lanes((rows, 2 * HD), part)
            query_low = jnp.where(own_q, query, qf_ref[...])
            scores = []
            for block in range(-lo, hi + 1):
                spot = pl.ds((block + reach) * rows, rows)
                key_low = jnp.where(own_q, k_ref[slot_of(block), :], kf_ref[spot, :])
                score = dot(key_low, query_low, NT)
                if abs(block) <= 1:
                    score = score + bias_ref[part, block + 1]
                else:
                    score = score + far_ref[int(block > 0), 2 * pair + part]
                scores.append(score)
            peak = jnp.max(functools.reduce(jnp.maximum, scores), axis=0, keepdims=True)
            total = jnp.zeros((2 * HD, rows), F32)
            for number, block in enumerate(range(-lo, hi + 1)):
                probs = jnp.exp(scores[number] - peak).astype(BF16)
                value_low = jnp.where(own_q, v_ref[slot_of(block), :], jnp.ones((), BF16))
                total = total + dot(value_low, probs, TN)
            row_sum = total[HD * (1 - part) : HD * (1 - part) + 1, :]
            mixed.append(total[HD * part : HD * (part + 1), :] / row_sum)
            logs.append(peak + jnp.log(row_sum))
        o_ref[...] = jnp.concatenate(mixed, axis=0).T.astype(BF16)
        log_ref[0] = jnp.concatenate(logs + [jnp.zeros((6, rows), F32)], axis=0)

    for lo, hi in block_choices(reach):
        pl.when((low == lo) & (high == hi))(functools.partial(work, lo, hi))


def backward_kernel(
    reach, range_ref, far_ref, q_ref, k_ref, v_ref, qf_ref, kf_ref, bias_ref, do_ref, o_ref, log_ref,
    dq_ref, dk_ref, dv_ref, bias_grad_ref,
):
    pair = pl.program_id(0)
    rows = q_ref.shape[0]
    score_scale = HD ** (-0.5)
    low, high = range_ref[0], range_ref[1]

    def slot_of(block):
        return pl.ds(pl.multiple_of(range_ref[2 + block + reach] * rows, rows), rows)

    def work(lo, hi):
        query = q_ref[...] * jnp.asarray(score_scale, BF16)
        upstream = do_ref[...]
        products = (upstream.astype(F32) * o_ref[...].astype(F32)).T
        nothing = jnp.zeros((), BF16)
        ahead = lax.broadcasted_iota(jnp.int32, (rows, rows), 0) - lax.broadcasted_iota(
            jnp.int32, (rows, rows), 1
        )
        own, query_low, query_own, up_own, delta, log_row, dq, near, far = ([None, None] for _ in range(9))
        for part in range(2):
            own[part] = own_lanes((rows, 2 * HD), part)
            query_low[part] = jnp.where(own[part], query, qf_ref[...])
            query_own[part] = jnp.where(own[part], query, nothing)
            up_own[part] = jnp.where(own[part], upstream, nothing)
            delta[part] = jnp.sum(products[HD * part : HD * (part + 1), :], axis=0, keepdims=True)
            log_row[part] = log_ref[0, part : part + 1, :]
            dq[part] = jnp.zeros((2 * HD, rows), F32)
            near[part] = jnp.zeros((rows, rows), F32)
            far[part] = [jnp.zeros((1, rows), F32), jnp.zeros((1, rows), F32)]
        for block in range(-reach, reach + 1):
            if not -lo <= block <= hi:
                dk_ref[slot_of(block), :] = jnp.zeros((rows, 2 * HD), BF16)
                dv_ref[slot_of(block), :] = jnp.zeros((rows, 2 * HD), BF16)
                continue
            spot = pl.ds((block + reach) * rows, rows)
            dk = jnp.zeros((rows, 2 * HD), F32)
            dv = jnp.zeros((rows, 2 * HD), F32)
            for part in range(2):
                key = k_ref[slot_of(block), :]
                score = dot(jnp.where(own[part], key, kf_ref[spot, :]), query_low[part], NT)
                if abs(block) <= 1:
                    score = score + bias_ref[part, block + 1]
                else:
                    score = score + far_ref[int(block > 0), 2 * pair + part]
                probs = jnp.exp(score - log_row[part])
                dprobs = dot(v_ref[slot_of(block), :], up_own[part], NT)
                dscore = probs * (dprobs - delta[part])
                probs_low, dscore_low = probs.astype(BF16), dscore.astype(BF16)
                dv = dv + dot(probs_low, up_own[part])
                dk = dk + dot(dscore_low, query_own[part])
                dq[part] = dq[part] + dot(key, dscore_low, TN)
                if block == 0:
                    close = jnp.abs(ahead) < FAR
                    near[part] = near[part] + jnp.where(close, dscore, 0.0)
                    far[part][0] += jnp.sum(jnp.where(ahead <= -FAR, dscore, 0.0), axis=0, keepdims=True)
                    far[part][1] += jnp.sum(jnp.where(ahead >= FAR, dscore, 0.0), axis=0, keepdims=True)
                elif abs(block) == 1:
                    close = (ahead < FAR - rows) if block > 0 else (ahead > rows - FAR)
                    near[part] = near[part] + jnp.where(close, dscore, 0.0)
                    far[part][int(block > 0)] += jnp.sum(jnp.where(close, 0.0, dscore), axis=0, keepdims=True)
                else:
                    far[part][int(block > 0)] += jnp.sum(dscore, axis=0, keepdims=True)
            dk_ref[slot_of(block), :] = dk.astype(BF16)
            dv_ref[slot_of(block), :] = dv.astype(BF16)
        dq_ref[...] = (
            jnp.concatenate([dq[0][:HD], dq[1][HD:]], axis=0).T * score_scale
        ).astype(BF16)
        flip = (
            lax.broadcasted_iota(jnp.int32, (rows, rows), 0) + lax.broadcasted_iota(jnp.int32, (rows, rows), 1)
            == rows - 1
        ).astype(BF16)
        for part in range(2):
            turned = dot(flip, near[part].astype(BF16))
            turned = pltpu.roll(turned, 0, 1, stride=1, stride_axis=0)
            line = jnp.sum(turned, axis=0, keepdims=True)
            bias_grad_ref[0, part] = jnp.concatenate(
                [line, far[part][0], far[part][1], jnp.zeros((5, rows), F32)], axis=0
            )

    for lo, hi in block_choices(reach):
        pl.when((low == lo) & (high == hi))(functools.partial(work, lo, hi))


def pair_block(*shape):
    count = len(shape)
    return pl.BlockSpec(shape, lambda p: (0,) * (count - 1) + (p,))


def same_block(*shape):
    count = len(shape)
    return pl.BlockSpec(shape, lambda p: (0,) * count)


def attention_specs(rows, window, pairs):
    smem = pl.BlockSpec(memory_space=pltpu.SMEM)
    return [
        smem,
        smem,
        pair_block(rows, 2 * HD),
        pair_block(window, 2 * HD),
        pl.BlockSpec((window, 2 * HD), lambda p: (0, pairs + p)),
        same_block(rows, 2 * HD),
        same_block(window, 2 * HD),
        pl.BlockSpec((2, 3, rows, rows), lambda p: (p, 0, 0, 0)),
    ]


LITTLE = pl.CostEstimate(flops=10**5, bytes_accessed=10**4, transcendentals=0)


def attend(reach, ranges, far_bias, queries, both, *operands):
    rows, width = queries.shape
    window = both.shape[0]
    pairs = width // (2 * HD)
    return pl.pallas_call(
        functools.partial(forward_kernel, reach),
        grid=(pairs,),
        in_specs=attention_specs(rows, window, pairs),
        out_specs=[pair_block(rows, 2 * HD), pl.BlockSpec((1, 8, rows), lambda p: (p, 0, 0))],
        out_shape=[
            jax.ShapeDtypeStruct((rows, width), BF16),
            jax.ShapeDtypeStruct((pairs, 8, rows), F32),
        ],
        compiler_params=pltpu.CompilerParams(vmem_limit_bytes=VMEM_LIMIT),
        cost_estimate=LITTLE,
        name="attend",
    )(ranges, far_bias, queries, both, both, *operands)


def attend_back(reach, ranges, far_bias, queries, both, *operands):
    rows, width = queries.shape
    window = both.shape[0]
    pairs = width // (2 * HD)
    tall, short = pair_block(window, 2 * HD), pair_block(rows, 2 * HD)
    return pl.pallas_call(
        functools.partial(backward_kernel, reach),
        grid=(pairs,),
        in_specs=attention_specs(rows, window, pairs)
        + [short, short, pl.BlockSpec((1, 8, rows), lambda p: (p, 0, 0))],
        out_specs=[short, tall, tall, pl.BlockSpec((1, 2, 8, rows), lambda p: (p, 0, 0, 0))],
        out_shape=[
            jax.ShapeDtypeStruct((rows, width), BF16),
            jax.ShapeDtypeStruct((window, width), BF16),
            jax.ShapeDtypeStruct((window, width), BF16),
            jax.ShapeDtypeStruct((pairs, 2, 8, rows), F32),
        ],
        compiler_params=pltpu.CompilerParams(vmem_limit_bytes=VMEM_LIMIT),
        cost_estimate=LITTLE,
        name="attend_back",
    )(ranges, far_bias, queries, both, both, *operands)


def flatten_kernel(rows_ref, flat_ref):
    flat_ref[...] = rows_ref[...].T


def flatten(window, rows):
    return pl.pallas_call(
        flatten_kernel,
        grid=(window.shape[0] // rows,),
        in_specs=[pl.BlockSpec((rows, window.shape[1]), lambda n: (n, 0))],
        out_specs=pair_block(window.shape[1], rows),
        out_shape=jax.ShapeDtypeStruct(window.shape[::-1], BF16),
        compiler_params=pltpu.CompilerParams(vmem_limit_bytes=VMEM_LIMIT),
        cost_estimate=LITTLE,
        name="flatten",
    )(window)


def collect_kernel(count, *refs):
    half = refs[-1].shape[1]
    flat_refs, grad_refs = refs[:count], refs[count : 4 * count]
    out_part_ref, keep_ref, send_ref = refs[4 * count :]
    for number in range(3):
        grad = jnp.zeros((2 * half, keep_ref.shape[2]), F32)
        for flat_ref, grad_ref in zip(flat_refs, grad_refs[number::3]):
            grad = grad + dot(flat_ref[:, : grad_ref.shape[0]], grad_ref[...])
        keep_ref[number] = grad[:half].astype(BF16)
        send_ref[number] = grad[half:].astype(BF16)
    keep_ref[3] = out_part_ref[:half, :]
    send_ref[3] = out_part_ref[half:, :]


def collect(windows_flat, grads, out_part):
    count = len(grads)
    chunk = 4 * HD
    flat_grads = [part for grad in grads for part in grad]
    return pl.pallas_call(
        functools.partial(collect_kernel, count),
        grid=(D // chunk,),
        in_specs=[same_block(*part.shape) for part in windows_flat]
        + [pair_block(part.shape[0], chunk) for part in (*flat_grads, out_part)],
        out_specs=[pair_block(4, D // 2, chunk)] * 2,
        out_shape=[jax.ShapeDtypeStruct((4, D // 2, D), BF16)] * 2,
        compiler_params=pltpu.CompilerParams(vmem_limit_bytes=VMEM_LIMIT),
        cost_estimate=LITTLE,
        name="collect",
    )(*windows_flat, *flat_grads, out_part)


CUBE = 0.044715
ROOT = (2.0 / 3.141592653589793) ** 0.5


def feed_kernel(normed_ref, hidden_ref, near_ref, other_ref, out_ref, act_ref, slope_ref):
    @pl.when(pl.program_id(0) == 0)
    def _():
        out_ref[...] = hidden_ref[...]

    pre = dot(normed_ref[...], whole_rows(near_ref, other_ref, 0))
    square = pre * pre
    bend = jnp.tanh(ROOT * pre * (1.0 + CUBE * square))
    gate = 0.5 * (1.0 + bend)
    act = (pre * gate).astype(BF16)
    slope = gate + 0.5 * pre * (1.0 - bend * bend) * (ROOT * (1.0 + 3.0 * CUBE * square))
    act_ref[...] = act
    slope_ref[...] = slope.astype(BF16)
    out_ref[...] += dot(act, whole_rows(near_ref, other_ref, 1), NT)


def feed_back_kernel(
    normed_ref, up_ref, near_ref, other_ref, act_ref, slope_ref, out_ref, keep_ref, send_ref,
    normed_flat_ref, up_flat_ref,
):
    half = keep_ref.shape[1]

    @pl.when(pl.program_id(0) == 0)
    def _():
        out_ref[...] = jnp.zeros_like(out_ref)
        normed_flat_ref[...] = normed_ref[...].T
        up_flat_ref[...] = up_ref[...].T

    act_grad = dot(up_ref[...], whole_rows(near_ref, other_ref, 1))
    pre_grad = (act_grad * slope_ref[...].astype(F32)).astype(BF16)
    out_ref[...] += dot(pre_grad, whole_rows(near_ref, other_ref, 0), NT)
    for number, grad in enumerate(
        (dot(normed_flat_ref[...], pre_grad), dot(up_flat_ref[...], act_ref[...]))
    ):
        keep_ref[number] = grad[:half].astype(BF16)
        send_ref[number] = grad[half:].astype(BF16)


def unit_chunk(units):
    return 512 if units % 512 == 0 else units


def feed(normed, hidden, near, other):
    count, width = normed.shape
    _, half, units = near.shape
    chunk = unit_chunk(units)
    weights = pair_block(2, half, chunk)
    wide = pair_block(count, chunk)
    return pl.pallas_call(
        feed_kernel,
        grid=(units // chunk,),
        in_specs=[same_block(count, width), same_block(count, width), weights, weights],
        out_specs=[same_block(count, width), wide, wide],
        out_shape=[
            jax.ShapeDtypeStruct((count, width), F32),
            jax.ShapeDtypeStruct((count, units), BF16),
            jax.ShapeDtypeStruct((count, units), BF16),
        ],
        compiler_params=pltpu.CompilerParams(vmem_limit_bytes=VMEM_LIMIT),
        cost_estimate=LITTLE,
        name="feed",
    )(normed, hidden, near, other)


def feed_back(normed, upstream, near, other, act, slope):
    count, width = normed.shape
    _, half, units = near.shape
    chunk = unit_chunk(units)
    weights = pair_block(2, half, chunk)
    wide = pair_block(count, chunk)
    return pl.pallas_call(
        feed_back_kernel,
        grid=(units // chunk,),
        in_specs=[same_block(count, width), same_block(count, width), weights, weights, wide, wide],
        out_specs=[same_block(count, width), weights, weights],
        out_shape=[
            jax.ShapeDtypeStruct((count, width), F32),
            jax.ShapeDtypeStruct((2, half, units), BF16),
            jax.ShapeDtypeStruct((2, half, units), BF16),
        ],
        scratch_shapes=[pltpu.VMEM((width, count), BF16), pltpu.VMEM((width, count), BF16)],
        compiler_params=pltpu.CompilerParams(vmem_limit_bytes=VMEM_LIMIT),
        cost_estimate=LITTLE,
        name="feed_back",
    )(normed, upstream, near, other, act, slope)


def contrast_kernel(
    micro_count, segment_count, rank_ref, pooled_ref, near_ref, other_ref, turn_ref, grad_ref, proj_grad_ref
):
    every = pooled_ref.shape[0]
    own = micro_count * segment_count

    def place(axis):
        number = lax.broadcasted_iota(jnp.int32, (every, every), axis)
        segment = number % segment_count
        micro = (number // segment_count) % micro_count
        owner = rank_ref[0] ^ (number // own)
        return owner * segment_count + segment, micro

    spot, micro = place(0)
    other_spot, other_micro = place(1)
    together = micro == other_micro
    pooled = dot(pooled_ref[:, :D], turn_ref[...]).astype(BF16)
    proj = jnp.concatenate([near_ref[...], other_ref[...]], axis=0)
    marks = pooled_ref[:, D:].astype(F32)
    target = (marks[:, 0:1] * 16.0 + marks[:, 1:2]).astype(jnp.int32)
    picked = target + (target >= spot).astype(jnp.int32)
    chosen = together & (picked == other_spot)
    embedded = dot(pooled, proj)
    inverse = lax.rsqrt(jnp.sum(embedded * embedded, axis=1, keepdims=True) + EPS_NORM)
    unit = (embedded * inverse).astype(BF16)
    logits = jnp.where(together & (spot != other_spot), SIM_SCALE * dot(unit, unit, NT), NEG_FILL)
    shifted = jnp.exp(logits - jnp.max(logits, axis=1, keepdims=True))
    shares = shifted / jnp.sum(shifted, axis=1, keepdims=True)
    logit_grad = (shares - chosen.astype(F32)).astype(BF16)
    unit_grad = SIM_SCALE * (dot(logit_grad, unit) + dot(logit_grad, unit, TN))
    unit_grad = unit_grad.astype(BF16).astype(F32)
    along = jnp.sum(unit_grad * embedded, axis=1, keepdims=True)
    embed_grad = inverse * unit_grad - embedded * (inverse * inverse * inverse) * along
    embed_grad = embed_grad.astype(BF16)
    grad_ref[...] = dot(embed_grad[:own], proj, NT)
    proj_grad_ref[...] = dot(pooled, embed_grad, TN)


def contrast(rank, pooled, near, other, turn, micro_count, segment_count):
    vmem = pl.BlockSpec(memory_space=pltpu.VMEM)
    return pl.pallas_call(
        functools.partial(contrast_kernel, micro_count, segment_count),
        in_specs=[pl.BlockSpec(memory_space=pltpu.SMEM), vmem, vmem, vmem, vmem],
        out_specs=[vmem, vmem],
        out_shape=[
            jax.ShapeDtypeStruct((micro_count * segment_count, D), F32),
            jax.ShapeDtypeStruct((D, D), F32),
        ],
        compiler_params=pltpu.CompilerParams(vmem_limit_bytes=VMEM_LIMIT),
        cost_estimate=LITTLE,
        name="contrast",
    )(rank, pooled, near, other, turn)


def local(
    tokens,
    cotangent,
    segment_ids,
    targets,
    attention_weights,
    feedforward_weights,
    projection,
    norm_gains,
    bias_table,
    attention_first,
    attention_second,
    feedforward_first,
    feedforward_second,
    projection_first,
    projection_second,
    gains_first,
    gains_second,
    bias_first,
    bias_second,
):
    wide_count = lax.axis_size("dp")
    narrow_count = lax.axis_size("mp")
    wide_rank = lax.axis_index("dp")
    narrow_rank = lax.axis_index("mp")
    micro_count, _, rows, _ = tokens.shape
    segment_count = targets.shape[2]
    block = D // wide_count
    heads_part = attention_weights.shape[2] // HD
    reach = min(narrow_count - 1, -(-(SEG_MOST - 1) // rows))
    span = 2 * reach + 1

    feature = jnp.arange(D, dtype=jnp.int32)
    place = feature // block
    order = outer_masks() + core_masks()
    away = sum(((place >> bit) & 1) * mask for bit, mask in enumerate(order)) + jnp.zeros_like(place)
    source = (wide_rank ^ away) * block + feature % block
    turn = (feature[:, None] == source[None, :]).astype(BF16)
    turn_wide = turn.astype(F32)

    attention_low = attention_weights.astype(BF16)
    feedforward_low = feedforward_weights.astype(BF16)
    projection_low = projection.astype(BF16)

    token_rows = dot(tokens.reshape(micro_count * rows, D), turn)
    gains = dot(norm_gains, turn_wide, precision=HIGHEST)
    factor_one = norm_factor(token_rows)
    normed_one = (token_rows * factor_one * gains[0]).astype(BF16)
    normed_one = normed_one.reshape(micro_count, rows, D)

    head = jnp.arange(bias_table.shape[1], dtype=jnp.int32)
    head_source = (narrow_rank ^ (head // heads_part)) * heads_part + head % heads_part
    head_turn = (head[:, None] == head_source[None, :]).astype(F32)

    is_even = narrow_rank % 2 == 0

    def hop(held):
        return link(held[1], False), link(held[0], True)

    hops = [[] for _ in range(micro_count)]

    def window_of(micro):
        return jnp.concatenate([normed_one[micro]] + [part for pair in hops[micro] for part in pair])

    def project(micro):
        return (
            dot(normed_one[micro], w_query).astype(BF16),
            dot(windows[micro], w_both).astype(BF16),
        )

    def finish_hops(micro):
        while len(hops[micro]) < reach:
            hops[micro].append(hop(hops[micro][-1]))

    def chain_step(values, bit):
        return jnp.concatenate([values, swap(values, "mp", bit)], axis=-1)

    bits = []
    while 1 << len(bits) < narrow_count:
        bits.append(1 << len(bits))
    attn_parts = gather_columns(attention_low)
    ffn_cols = feedforward_low
    for bit in bits[:1]:
        ffn_cols = chain_step(ffn_cols, bit)
    attn_parts, ffn_cols, normed_late = after((attn_parts, ffn_cols, normed_one))
    segment_ids, bias_late = after((segment_ids, bias_table), *attn_parts)
    table = dot(bias_late, head_turn, precision=HIGHEST)
    tiles = bias_tiles(table, rows)
    attn_held = gather_plane(jnp.concatenate([attention_low] + attn_parts, axis=-1))
    for bit in bits[1:]:
        ffn_cols = chain_step(ffn_cols, bit)
    attn_held, ffn_cols, normed_late, tiles = after((attn_held, ffn_cols, normed_late, tiles))
    attn_near, attn_other = halves(attn_held)
    first_hop = hop((normed_late, normed_late))
    parts = [ffn_cols[0][None], ffn_cols[1][None]]

    def outer_received(number):
        return [gather_outer(part, number, first) for part, first in zip(parts, (True, False))]

    def outer_joined(received):
        return [
            join_outer(part, got, first) for part, got, first in zip(parts, received, (True, False))
        ]

    outer_count = len(outer_masks())
    received = outer_received(0)
    attn_other, first_hop, received = after((attn_other, first_hop, received))
    parts = outer_joined(received)
    attn_all = jnp.concatenate([attn_near, attn_other], axis=1)
    w_query, w_out = attn_all[0], attn_all[3]
    w_both = jnp.concatenate([attn_all[1], attn_all[2]], axis=1)
    for micro in range(micro_count):
        hops[micro].append((first_hop[0][micro], first_hop[1][micro]))
    finish_hops(0)
    w_both, w_query, hops, parts = after((w_both, w_query, hops, parts))
    windows = [window_of(0)]
    projected = [project(0)]
    slots = jnp.stack(
        [
            jnp.int32(0)
            if n == 0
            else jnp.where(is_even == (n > 0), 2 * abs(n) - 1, 2 * abs(n)).astype(jnp.int32)
            for n in range(-reach, reach + 1)
        ]
    )

    far_bias = jnp.stack([table[15], table[31]])
    lanes = jnp.arange(2 * HD, dtype=jnp.int32) % HD
    padded = jnp.pad(
        segment_ids[:, 0], ((0, 0), (reach * rows, reach * rows)), constant_values=segment_count
    )
    window_segments = lax.dynamic_slice_in_dim(padded, narrow_rank * rows, span * rows, 1)
    own_segments = window_segments[:, reach * rows : (reach + 1) * rows]
    key_marks = (window_segments[:, :, None] == lanes).astype(BF16)
    query_marks = jnp.where(
        (own_segments[:, :, None] != lanes) & (lanes <= segment_count), MASKED, 0.0
    ).astype(BF16)
    first, last = own_segments[:, 0], own_segments[:, -1]
    low_count = sum(
        (window_segments[:, (reach - n) * rows + rows - 1] == first).astype(jnp.int32)
        for n in range(1, reach + 1)
    )
    high_count = sum(
        (window_segments[:, (reach + n) * rows] == last).astype(jnp.int32)
        for n in range(1, reach + 1)
    )
    ranges = jnp.concatenate(
        [
            jnp.stack([low_count, high_count], axis=1),
            jnp.broadcast_to(slots, (micro_count, span)),
        ],
        axis=1,
    )

    mixed, kept = [], []
    proj_parts = []
    for micro in range(micro_count):
        came, received = [], []
        parts, projected[micro] = after((parts, projected[micro]))
        if micro == 0 and outer_count > 1:
            received = outer_received(1)
        if micro + 1 < micro_count:
            finish_hops(micro + 1)
            came = hops[micro + 1]
        else:
            proj_parts = gather_columns(after(projection_low, projected[micro][0]))
        operands = (
            ranges[micro], far_bias, *projected[micro], query_marks[micro], key_marks[micro], tiles
        )
        mixed_part, logs = attend(reach, *operands)
        came, mixed_part, proj_parts = after((came, mixed_part, proj_parts))
        if came:
            hops[micro + 1] = came
            windows.append(window_of(micro + 1))
            projected.append(project(micro + 1))
        if received:
            last_received = received
        kept.append((operands, mixed_part, logs))
        mixed.append(mixed_part)
    if outer_count > 1:
        last_received, mixed = after((last_received, mixed))
        parts = outer_joined(last_received)
    for number in range(2, outer_count):
        parts = outer_joined(outer_received(number))
    ffn_near, ffn_other = halves(jnp.stack(parts))
    hidden_one = token_rows + dot(jnp.concatenate(mixed, axis=0), w_out, NT)
    proj_held = gather_plane(jnp.concatenate([projection_low] + proj_parts, axis=-1)[None])
    windows_flat = [flatten(window, rows) for window in windows]
    hidden_one, ffn_other, proj_held, windows_flat = after(
        (hidden_one, ffn_other, proj_held, windows_flat)
    )
    proj_near, proj_other = halves(proj_held)

    factor_two = norm_factor(hidden_one)
    normed_two = (hidden_one * factor_two * gains[1]).astype(BF16)
    hidden_two, activated, slopes = feed(normed_two, hidden_one, ffn_near, ffn_other)
    hidden_two, proj_other = after((hidden_two, proj_other))
    output = dot(hidden_two.astype(BF16), turn, NT).astype(BF16)

    factor_three = norm_factor(hidden_two)
    unit_three = hidden_two * factor_three
    normed_three = (unit_three * gains[2]).reshape(micro_count, rows, D)
    numbers = jnp.arange(segment_count, dtype=jnp.int32)
    member = (own_segments[:, None, :] == numbers[None, :, None]).astype(F32)
    counts = jnp.sum(
        (segment_ids[:, 0][:, None, :] == numbers[None, :, None]).astype(F32), axis=2, keepdims=True
    )
    pooled = lax.dot_general(
        member, normed_three, (((2,), (1,)), ((0,), (0,))), precision=HIGHEST, preferred_element_type=F32
    )
    pooled = sum_over(pooled, "mp") / counts
    pooled = dot(pooled.reshape(-1, D).astype(BF16), turn, NT).astype(BF16)
    pooled = pooled.reshape(1, micro_count, segment_count, D)
    marks = jnp.stack([targets[:, 0] // 16, targets[:, 0] % 16], axis=-1).astype(BF16)
    marks = jnp.pad(marks[None], ((0, 0), (0, 0), (0, 0), (0, 126)))
    pooled_all = gather_near(jnp.concatenate([pooled, marks], axis=-1))
    rank = jnp.stack([wide_rank, narrow_rank]).astype(jnp.int32)
    pooled_grad, proj_grad = contrast(
        rank, pooled_all.reshape(-1, pooled_all.shape[-1]), proj_near[0], proj_other[0], turn,
        micro_count, segment_count,
    )
    proj_reduced = proj_grad[:block, : projection.shape[1]]
    pooled_grad = pooled_grad.reshape(micro_count, segment_count, D) / counts
    normed_three_grad = lax.dot_general(
        member, pooled_grad, (((1,), (1,)), ((0,), (0,))), precision=HIGHEST, preferred_element_type=F32
    ).reshape(micro_count * rows, D)
    gain_three = jnp.sum(normed_three_grad * unit_three, axis=0)

    upstream = dot(cotangent.reshape(micro_count * rows, D), turn)
    hidden_two_grad = upstream + norm_back(hidden_two, factor_three, normed_three_grad * gains[2])
    hidden_two_low = hidden_two_grad.astype(BF16)
    normed_two_grad, ffn_keep, ffn_send = feed_back(
        normed_two, hidden_two_low, ffn_near, ffn_other, activated, slopes
    )
    ffn_received = swap(ffn_send, "dp", 1)
    gain_two = jnp.sum(normed_two_grad * hidden_one * factor_two, axis=0)
    hidden_one_grad = hidden_two_grad + norm_back(
        hidden_one, factor_two, normed_two_grad * gains[1]
    )
    hidden_one_low = hidden_one_grad.astype(BF16)
    mixed_grad = dot(hidden_one_low, w_out).astype(BF16).reshape(micro_count, rows, D)
    out_part = dot(hidden_one_low, jnp.concatenate(mixed, axis=0), TN).astype(BF16)
    ffn_received, mixed_grad, out_part = after((ffn_received, mixed_grad, out_part))

    def outer_split(parts):
        return [split_outer(terms, masks, first) for (terms, masks), first in zip(parts, (False, True))]

    ffn_blocks = [to_blocks(ffn_keep), to_blocks(ffn_received)]
    parts = [([held[number] for held in ffn_blocks], outer_masks()) for number in range(2)]
    grads, owns, bias_parts, flows = [], [], [], []

    def leave(flow, n):
        even, odd = flow[2 * n - 2], flow[2 * n - 1]
        return link(even, False), link(odd, True)

    def join(flow, n, came):
        if n > 0:
            flow[2 * n - 1] = add_low(flow[2 * n - 1], came[0])
            flow[2 * n - 2] = add_low(flow[2 * n - 2], came[1])

    def flow_of(dq, dk, dv):
        partial = dot(dk, w_both[:, :D], NT) + dot(dv, w_both[:, D:], NT)
        own = partial[:rows] + dot(dq, w_query, NT)
        low_parts = partial.astype(BF16)
        return own, [low_parts[n * rows : (n + 1) * rows] for n in range(1, span)]

    came = []
    for micro in range(micro_count):
        operands, mixed_part, logs = kept[micro]
        last = micro == micro_count - 1
        steps = outer_split(parts) if parts[0][1] else []
        upstream_low, flows, sent = after(
            (mixed_grad[micro], flows, [step[1] for step in steps])
        )
        received = [swap(leaves, "dp", step[2]) for leaves, step in zip(sent, steps)]
        came = [leave(flow, reach) for flow in flows]
        dq, dk, dv, bias_part = attend_back(reach, *operands, upstream_low, mixed_part, logs)
        flow = None if last else flow_of(dq, dk, dv)
        received, came, dq, dk, dv, flow = after(
            (received, came, dq, dk, dv, flow)
        )
        if steps:
            parts = [(step[0] + [got], step[3]) for step, got in zip(steps, received)]
        grads.append((dq, dk, dv))
        bias_parts.append(bias_part)
        if not last:
            owns.append(flow[0])
            flows.append(list(flow[1]))
    while parts[0][1]:
        parts = [
            (stay + [swap(leaves, "dp", mask)], masks)
            for stay, leaves, mask, masks in outer_split(parts)
        ]
    others = came
    for flow, got in zip(flows, others):
        join(flow, reach - 1, got)
    ffn_last = [add_low(*terms)[0] for terms, _ in parts]
    ffn_last, grads = after((ffn_last, grads))
    up_column = send_columns_chain(ffn_last[0])
    attn_keep, attn_send = collect(windows_flat, grads, out_part)
    attn_keep, attn_send, up_column, flows, owns, last_grads = after(
        (attn_keep, attn_send, up_column, flows, owns, grads[-1])
    )
    last = flow_of(*last_grads)
    owns.append(last[0])
    last = list(last[1])
    attn_received = swap(attn_send, "dp", 1)
    down_column = send_columns_chain(after(ffn_last[1], attn_keep))
    came = leave(last, reach) if reach > 1 else ()
    attn_received, down_column, came = after((attn_received, down_column, came))
    attn_held = to_blocks(add_low(attn_keep, attn_received))
    if reach > 1:
        join(last, reach - 1, came)
    flow = [jnp.stack(pair) for pair in zip(*flows, last)]
    attn_held, flow = after((attn_held, flow))
    attn_received = send_plane(attn_held)
    for n in range(reach - 1, 0, -1):
        came = leave(flow, n)
        join(flow, n - 1, came)
    attn_received, came = after((attn_received, came))
    attn_last = add_low(attn_held[:, 0], *attn_received)
    attn_columns = send_columns(attn_last)
    normed_one_grad = jnp.stack(owns) + came[0].astype(F32) + came[1].astype(F32)
    normed_one_grad = normed_one_grad.reshape(micro_count * rows, D)
    ffn_column, ffn_last = after((jnp.stack([up_column, down_column]), jnp.stack(ffn_last)), *attn_received)
    ffn_reduced = finish_columns_chain(ffn_last, ffn_column)
    gain_one = jnp.sum(normed_one_grad * token_rows * factor_one, axis=0)
    tokens_grad = hidden_one_grad + norm_back(token_rows, factor_one, normed_one_grad * gains[0])
    tokens_grad = dot(tokens_grad, turn_wide, NT, HIGHEST)
    attn_columns, tokens_grad, gain_one = after((attn_columns, tokens_grad, gain_one))
    attn_reduced = add_columns(attn_last, attn_columns)

    bias_sum = sum(bias_parts)
    heads = table.shape[1]
    bias_sum = bias_sum.reshape(heads, 8, rows)
    spot = (jnp.arange(rows, dtype=jnp.int32) + 1) % rows
    relative = jnp.where(spot < FAR, -spot, rows - spot)
    buckets = jnp.arange(table.shape[0], dtype=jnp.int32)
    near_hot = (bucket_of(relative)[:, None] == buckets[None, :]) & (
        jnp.abs(relative) < FAR
    )[:, None]
    table_grad = dot(near_hot.astype(F32), bias_sum[:, 0], (((0,), (1,)), ((), ())), HIGHEST)
    table_grad = (
        table_grad
        + (buckets == 15).astype(F32)[:, None] * jnp.sum(bias_sum[:, 1], axis=1)[None, :]
        + (buckets == 31).astype(F32)[:, None] * jnp.sum(bias_sum[:, 2], axis=1)[None, :]
    )
    full_table = dot(table_grad, head_turn, NT, HIGHEST)
    gains_part = dot(jnp.stack([gain_one, gain_two, gain_three]), turn_wide, NT, HIGHEST)
    local_squares = (
        jnp.sum(attn_reduced * attn_reduced)
        + jnp.sum(ffn_reduced * ffn_reduced)
        + jnp.sum(proj_reduced * proj_reduced)
    )
    small = jnp.concatenate(
        [
            gains_part,
            jnp.pad(full_table.reshape(1, -1), ((0, 0), (0, D - full_table.size))),
            jnp.broadcast_to(local_squares, (4, D)),
        ]
    )
    small = sum_over(sum_over(small, "dp"), "mp")
    gains_grad = small[:3]
    table_full_grad = small[3, : full_table.size].reshape(full_table.shape)
    total_squares = (
        small[4, 0] + jnp.sum(gains_grad * gains_grad) + jnp.sum(table_full_grad * table_full_grad)
    )
    grad_norm = jnp.sqrt(total_squares)
    factor = jnp.minimum(1.0, CLIP_NORM / (grad_norm + 1e-06))
    attn_new = adam_update(
        attention_weights, attn_reduced * factor, attention_first, attention_second,
        RATE_MATRIX, DECAY_MATRIX,
    )
    ffn_new = adam_update(
        feedforward_weights, ffn_reduced * factor, feedforward_first, feedforward_second,
        RATE_MATRIX, DECAY_MATRIX,
    )
    proj_new = adam_update(
        projection, proj_reduced * factor, projection_first, projection_second,
        RATE_MATRIX, DECAY_MATRIX,
    )
    gains_new = adam_update(
        norm_gains, gains_grad * factor, gains_first, gains_second, RATE_SMALL, 0.0
    )
    table_new = adam_update(
        bias_table, table_full_grad * factor, bias_first, bias_second, RATE_SMALL, 0.0
    )
    return (
        output.reshape(tokens.shape),
        tokens_grad.reshape(tokens.shape),
        grad_norm,
        *attn_new,
        *ffn_new,
        *proj_new,
        *gains_new,
        *table_new,
    )


def solution(mesh):
    return jax.shard_map(
        local,
        mesh=mesh,
        in_specs=(
            P(None, "dp", "mp", None),
            P(None, "dp", "mp", None),
            P(None, "dp", None),
            P(None, "dp", None),
            P(None, "dp", "mp"),
            P(None, "dp", "mp"),
            P("dp", "mp"),
            P(),
            P(),
            P(None, "dp", "mp"),
            P(None, "dp", "mp"),
            P(None, "dp", "mp"),
            P(None, "dp", "mp"),
            P("dp", "mp"),
            P("dp", "mp"),
            P(),
            P(),
            P(),
            P(),
        ),
        out_specs=(
            P(None, "dp", "mp", None),
            P(None, "dp", "mp", None),
            P(),
            P(None, "dp", "mp"),
            P(None, "dp", "mp"),
            P(None, "dp", "mp"),
            P(None, "dp", "mp"),
            P(None, "dp", "mp"),
            P(None, "dp", "mp"),
            P("dp", "mp"),
            P("dp", "mp"),
            P("dp", "mp"),
            P(),
            P(),
            P(),
            P(),
            P(),
            P(),
        ),
        check_vma=False,
    )
```

```python
import functools

import jax
import jax.numpy as jnp
from jax import lax
from jax.experimental import pallas as pl
from jax.experimental.pallas import tpu as pltpu
from jax.sharding import PartitionSpec as P

D = 768
HD = 64
STEP = 10
SEG_MOST = 512

EPS_NORM = 1e-06
EPS_ADAM = 1e-08
SIM_SCALE = 50.0
NEG_FILL = -1000000000.0
BETA_ONE = 0.9
BETA_TWO = 0.999
CLIP_NORM = 1.0
RATE_MATRIX = 0.05
RATE_SMALL = 0.2
DECAY_MATRIX = 0.01
LIMITS = (12, 16, 23, 32, 46, 64, 91)
FAR = LIMITS[-1]
MASKED = -float(2**30)
HIGHEST = lax.Precision.HIGHEST
BF16 = jnp.bfloat16
F32 = jnp.float32
NN = (((1,), (0,)), ((), ()))
NT = (((1,), (1,)), ((), ()))
TN = (((0,), (0,)), ((), ()))
VMEM_LIMIT = 48 * 1024 * 1024


def dot(left, right, dims=NN, precision=None):
    return lax.dot_general(left, right, dims, precision=precision, preferred_element_type=F32)


def bucket_of(relative):
    distance = jnp.abs(relative)
    far_bucket = 8 + sum(((distance >= threshold).astype(jnp.int32) for threshold in LIMITS))
    near_bucket = jnp.where(distance < 8, distance, far_bucket)
    return near_bucket + 16 * (relative > 0).astype(jnp.int32)


def norm_factor(values):
    return lax.rsqrt(jnp.mean(values * values, axis=-1, keepdims=True) + EPS_NORM)


def norm_back(values, factor, upstream):
    return factor * upstream - values * (factor * factor * factor) * jnp.mean(
        upstream * values, axis=-1, keepdims=True
    )


def adam_update(weight_now, clipped, first_old, second_old, step_rate, weight_decay):
    first_new = BETA_ONE * first_old + (1.0 - BETA_ONE) * clipped
    second_new = BETA_TWO * second_old + (1.0 - BETA_TWO) * clipped * clipped
    first_hat = first_new / (1.0 - BETA_ONE**STEP)
    second_hat = second_new / (1.0 - BETA_TWO**STEP)
    weight_new = weight_now - step_rate * (
        first_hat / (jnp.sqrt(second_hat) + EPS_ADAM) + weight_decay * weight_now
    )
    return (weight_new, first_new, second_new)


def swap(values, axis, mask):
    count = lax.axis_size(axis)
    return lax.ppermute(values, axis, [(i, i ^ mask) for i in range(count)])


def link(values, odd):
    count = lax.axis_size("mp")
    pairs = [(i, i + 1) for i in range(int(odd), count - 1, 2)]
    return lax.ppermute(values, "mp", pairs + [(j, i) for i, j in pairs])


def gather_columns_chain(values):
    bit = 1
    while bit < lax.axis_size("mp"):
        values = jnp.concatenate([values, swap(values, "mp", bit)], axis=-1)
        bit *= 2
    return values


def after(values, *earlier):
    return lax.optimization_barrier((values,) + earlier)[0]


def outer_masks():
    return [1 << bit for bit in range(1, lax.axis_size("dp").bit_length() - 1)]


def core_masks():
    return [1] if lax.axis_size("dp") > 1 else []


def gather_columns(values):
    return [swap(values, "mp", k) for k in range(1, lax.axis_size("mp"))]


def plane_masks():
    masks = [0]
    for mask in outer_masks():
        masks += [held | mask for held in masks]
    return masks[1:]


def gather_plane(values):
    return jnp.stack([values] + [swap(values, "dp", mask) for mask in plane_masks()], axis=1)


def halves(values):
    c, n, r, w = values.shape
    near = values.reshape(c, n * r, w)
    return near, swap(near, "dp", 1)


def to_blocks(values):
    c, rows, w = values.shape
    count = lax.axis_size("dp") // 2
    return values.reshape(c, count, rows // count, w)


def add_low(stay, *received):
    return sum([part.astype(F32) for part in received], stay.astype(F32)).astype(BF16)


def split_outer(terms, masks, first):
    spot = 0 if first else len(masks) - 1
    n, r, w = terms[0].shape
    split = [term.reshape(n >> (spot + 1), 2, 1 << spot, r, w) for term in terms]
    stay, leave = ([term[:, k].reshape(n // 2, r, w) for term in split] for k in range(2))
    return stay, add_low(*leave), masks[spot], masks[:spot] + masks[spot + 1 :]


def gather_outer(part, number, low_first):
    masks = outer_masks()
    return swap(part, "dp", masks[number] if low_first else masks[len(masks) - 1 - number])


def join_outer(part, received, low_first):
    if low_first:
        return jnp.concatenate([part, received], axis=0)
    n, r, w = part.shape
    return jnp.stack([part, received], axis=1).reshape(2 * n, r, w)


def send_plane(held):
    return [swap(held[:, number + 1], "dp", mask) for number, mask in enumerate(plane_masks())]


def send_columns(values):
    count = lax.axis_size("mp")
    width = values.shape[-1] // count
    return [swap(values[..., k * width : (k + 1) * width], "mp", k) for k in range(1, count)]


def send_columns_chain(values):
    count = lax.axis_size("mp")
    if count == 1:
        return values[..., :0]
    return swap(values[..., values.shape[-1] // 2 :], "mp", count // 2)


def finish_columns_chain(values, received):
    bit = lax.axis_size("mp") // 2
    while bit:
        half = values.shape[-1] // 2
        values = values[..., :half].astype(F32) + received.astype(F32)
        bit //= 2
        if bit:
            received = swap(values[..., half // 2 :].astype(BF16), "mp", bit)
    return values


def add_columns(values, received):
    width = values.shape[-1] // lax.axis_size("mp")
    return sum([part.astype(F32) for part in received], values[..., :width].astype(F32))


def sum_over(values, axis):
    bit = 1
    while bit < lax.axis_size(axis):
        values = values + swap(values, axis, bit)
        bit *= 2
    return values


def sum_at_once(values, axis):
    received = [values] + [swap(values, axis, mask) for mask in range(1, lax.axis_size(axis))]
    while len(received) > 1:
        received = [one + two for one, two in zip(received[::2], received[1::2])]
    return received[0]


def sum_everywhere(values):
    if lax.axis_size("dp") != 8:
        return sum_over(sum_over(values, "dp"), "mp")
    values = values + swap(values, "dp", 1)
    across = [swap(values, "dp", mask) for mask in (2, 4, 6)]
    values = (values + across[0]) + (across[1] + across[2])
    return sum_at_once(values, "mp")


def gather_wide(values):
    if lax.axis_size("dp") != 8:
        return gather_near(values)
    values = jnp.concatenate([values, swap(values, "dp", 1)], axis=0)
    return jnp.concatenate([values] + [swap(values, "dp", mask) for mask in (2, 4, 6)], axis=0)


def gather_near(values):
    bit = 1
    while bit < lax.axis_size("dp"):
        values = jnp.concatenate([values, swap(values, "dp", bit)], axis=0)
        bit *= 2
    return values


def bias_kernel(line_ref, tile_ref):
    rows = tile_ref.shape[2]
    for block in range(tile_ref.shape[1]):
        line = jnp.broadcast_to(line_ref[0, block : block + 1, :], (rows, 2 * rows))
        tile_ref[0, block] = pltpu.roll(line, 0, 1, stride=1, stride_axis=0)[:, :rows]


def bias_tiles(table, rows):
    heads = table.shape[1]
    lane = jnp.arange(2 * rows, dtype=jnp.int32)
    back = jnp.where(lane < rows, lane, lane - 2 * rows)
    relative = (jnp.arange(3, dtype=jnp.int32)[:, None] - 1) * rows - back[None, :]
    hot = (bucket_of(relative)[..., None] == jnp.arange(table.shape[0])).astype(F32)
    lines = dot(table, hot.reshape(-1, table.shape[0]), (((0,), (1,)), ((), ())), HIGHEST)
    lines = lines.reshape(heads, 3, 2 * rows)
    return pl.pallas_call(
        bias_kernel,
        grid=(heads,),
        in_specs=[pl.BlockSpec((1, 3, 2 * rows), lambda h: (h, 0, 0))],
        out_specs=pl.BlockSpec((1, 3, rows, rows), lambda h: (h, 0, 0, 0)),
        out_shape=jax.ShapeDtypeStruct((heads, 3, rows, rows), F32),
        compiler_params=pltpu.CompilerParams(vmem_limit_bytes=VMEM_LIMIT),
    )(lines)


def own_lanes(shape, part):
    lane = lax.broadcasted_iota(jnp.int32, shape, 1)
    return (lane < HD) if part == 0 else (lane >= HD)


def block_choices(reach):
    return [
        (lo, hi) for lo in range(reach + 1) for hi in range(reach + 1) if lo + hi < 2 * reach
    ]


def whole_rows(near_ref, far_ref, number):
    return jnp.concatenate([near_ref[number], far_ref[number]], axis=0)


def forward_kernel(reach, range_ref, far_ref, q_ref, k_ref, v_ref, qf_ref, kf_ref, bias_ref, o_ref, log_ref):
    pair = pl.program_id(0)
    rows = q_ref.shape[0]
    score_scale = HD ** (-0.5)
    low, high = range_ref[0], range_ref[1]

    def slot_of(block):
        return pl.ds(pl.multiple_of(range_ref[2 + block + reach] * rows, rows), rows)

    def work(lo, hi):
        query = q_ref[...] * jnp.asarray(score_scale, BF16)
        mixed, logs = [], []
        for part in range(2):
            own_q = own_lanes((rows, 2 * HD), part)
            query_low = jnp.where(own_q, query, qf_ref[...])
            scores = []
            for block in range(-lo, hi + 1):
                spot = pl.ds((block + reach) * rows, rows)
                key_low = jnp.where(own_q, k_ref[slot_of(block), :], kf_ref[spot, :])
                score = dot(key_low, query_low, NT)
                if abs(block) <= 1:
                    score = score + bias_ref[part, block + 1]
                else:
                    score = score + far_ref[int(block > 0), 2 * pair + part]
                scores.append(score)
            peak = jnp.max(functools.reduce(jnp.maximum, scores), axis=0, keepdims=True)
            total = jnp.zeros((2 * HD, rows), F32)
            for number, block in enumerate(range(-lo, hi + 1)):
                probs = jnp.exp(scores[number] - peak).astype(BF16)
                value_low = jnp.where(own_q, v_ref[slot_of(block), :], jnp.ones((), BF16))
                total = total + dot(value_low, probs, TN)
            row_sum = total[HD * (1 - part) : HD * (1 - part) + 1, :]
            mixed.append(total[HD * part : HD * (part + 1), :] / row_sum)
            logs.append(peak + jnp.log(row_sum))
        o_ref[...] = jnp.concatenate(mixed, axis=0).T.astype(BF16)
        log_ref[0] = jnp.concatenate(logs + [jnp.zeros((6, rows), F32)], axis=0)

    for lo, hi in block_choices(reach):
        pl.when((low == lo) & (high == hi))(functools.partial(work, lo, hi))


def backward_kernel(
    reach, range_ref, far_ref, q_ref, k_ref, v_ref, qf_ref, kf_ref, bias_ref, do_ref, o_ref, log_ref,
    dq_ref, dk_ref, dv_ref, bias_grad_ref,
):
    pair = pl.program_id(0)
    rows = q_ref.shape[0]
    score_scale = HD ** (-0.5)
    low, high = range_ref[0], range_ref[1]

    def slot_of(block):
        return pl.ds(pl.multiple_of(range_ref[2 + block + reach] * rows, rows), rows)

    def work(lo, hi):
        query = q_ref[...] * jnp.asarray(score_scale, BF16)
        upstream = do_ref[...]
        products = (upstream.astype(F32) * o_ref[...].astype(F32)).T
        nothing = jnp.zeros((), BF16)
        ahead = lax.broadcasted_iota(jnp.int32, (rows, rows), 0) - lax.broadcasted_iota(
            jnp.int32, (rows, rows), 1
        )
        own, query_low, query_own, up_own, delta, log_row, dq, near, far = ([None, None] for _ in range(9))
        for part in range(2):
            own[part] = own_lanes((rows, 2 * HD), part)
            query_low[part] = jnp.where(own[part], query, qf_ref[...])
            query_own[part] = jnp.where(own[part], query, nothing)
            up_own[part] = jnp.where(own[part], upstream, nothing)
            delta[part] = jnp.sum(products[HD * part : HD * (part + 1), :], axis=0, keepdims=True)
            log_row[part] = log_ref[0, part : part + 1, :]
            dq[part] = jnp.zeros((2 * HD, rows), F32)
            near[part] = jnp.zeros((rows, rows), F32)
            far[part] = [jnp.zeros((1, rows), F32), jnp.zeros((1, rows), F32)]
        for block in range(-reach, reach + 1):
            if not -lo <= block <= hi:
                dk_ref[slot_of(block), :] = jnp.zeros((rows, 2 * HD), BF16)
                dv_ref[slot_of(block), :] = jnp.zeros((rows, 2 * HD), BF16)
                continue
            spot = pl.ds((block + reach) * rows, rows)
            dk = jnp.zeros((rows, 2 * HD), F32)
            dv = jnp.zeros((rows, 2 * HD), F32)
            for part in range(2):
                key = k_ref[slot_of(block), :]
                score = dot(jnp.where(own[part], key, kf_ref[spot, :]), query_low[part], NT)
                if abs(block) <= 1:
                    score = score + bias_ref[part, block + 1]
                else:
                    score = score + far_ref[int(block > 0), 2 * pair + part]
                probs = jnp.exp(score - log_row[part])
                dprobs = dot(v_ref[slot_of(block), :], up_own[part], NT)
                dscore = probs * (dprobs - delta[part])
                probs_low, dscore_low = probs.astype(BF16), dscore.astype(BF16)
                dv = dv + dot(probs_low, up_own[part])
                dk = dk + dot(dscore_low, query_own[part])
                dq[part] = dq[part] + dot(key, dscore_low, TN)
                if block == 0:
                    close = jnp.abs(ahead) < FAR
                    near[part] = near[part] + jnp.where(close, dscore, 0.0)
                    far[part][0] += jnp.sum(jnp.where(ahead <= -FAR, dscore, 0.0), axis=0, keepdims=True)
                    far[part][1] += jnp.sum(jnp.where(ahead >= FAR, dscore, 0.0), axis=0, keepdims=True)
                elif abs(block) == 1:
                    close = (ahead < FAR - rows) if block > 0 else (ahead > rows - FAR)
                    near[part] = near[part] + jnp.where(close, dscore, 0.0)
                    far[part][int(block > 0)] += jnp.sum(jnp.where(close, 0.0, dscore), axis=0, keepdims=True)
                else:
                    far[part][int(block > 0)] += jnp.sum(dscore, axis=0, keepdims=True)
            dk_ref[slot_of(block), :] = dk.astype(BF16)
            dv_ref[slot_of(block), :] = dv.astype(BF16)
        dq_ref[...] = (
            jnp.concatenate([dq[0][:HD], dq[1][HD:]], axis=0).T * score_scale
        ).astype(BF16)
        flip = (
            lax.broadcasted_iota(jnp.int32, (rows, rows), 0) + lax.broadcasted_iota(jnp.int32, (rows, rows), 1)
            == rows - 1
        ).astype(BF16)
        for part in range(2):
            turned = dot(flip, near[part].astype(BF16))
            turned = pltpu.roll(turned, 0, 1, stride=1, stride_axis=0)
            line = jnp.sum(turned, axis=0, keepdims=True)
            bias_grad_ref[0, part] = jnp.concatenate(
                [line, far[part][0], far[part][1], jnp.zeros((5, rows), F32)], axis=0
            )

    for lo, hi in block_choices(reach):
        pl.when((low == lo) & (high == hi))(functools.partial(work, lo, hi))


def pair_block(*shape):
    count = len(shape)
    return pl.BlockSpec(shape, lambda p: (0,) * (count - 1) + (p,))


def same_block(*shape):
    count = len(shape)
    return pl.BlockSpec(shape, lambda p: (0,) * count)


def attention_specs(rows, window, pairs):
    smem = pl.BlockSpec(memory_space=pltpu.SMEM)
    return [
        smem,
        smem,
        pair_block(rows, 2 * HD),
        pair_block(window, 2 * HD),
        pl.BlockSpec((window, 2 * HD), lambda p: (0, pairs + p)),
        same_block(rows, 2 * HD),
        same_block(window, 2 * HD),
        pl.BlockSpec((2, 3, rows, rows), lambda p: (p, 0, 0, 0)),
    ]


LITTLE = pl.CostEstimate(flops=10**5, bytes_accessed=10**4, transcendentals=0)


def attend(reach, ranges, far_bias, queries, both, *operands):
    rows, width = queries.shape
    window = both.shape[0]
    pairs = width // (2 * HD)
    return pl.pallas_call(
        functools.partial(forward_kernel, reach),
        grid=(pairs,),
        in_specs=attention_specs(rows, window, pairs),
        out_specs=[pair_block(rows, 2 * HD), pl.BlockSpec((1, 8, rows), lambda p: (p, 0, 0))],
        out_shape=[
            jax.ShapeDtypeStruct((rows, width), BF16),
            jax.ShapeDtypeStruct((pairs, 8, rows), F32),
        ],
        compiler_params=pltpu.CompilerParams(vmem_limit_bytes=VMEM_LIMIT),
        cost_estimate=LITTLE,
        name="attend",
    )(ranges, far_bias, queries, both, both, *operands)


def attend_back(reach, ranges, far_bias, queries, both, *operands):
    rows, width = queries.shape
    window = both.shape[0]
    pairs = width // (2 * HD)
    tall, short = pair_block(window, 2 * HD), pair_block(rows, 2 * HD)
    return pl.pallas_call(
        functools.partial(backward_kernel, reach),
        grid=(pairs,),
        in_specs=attention_specs(rows, window, pairs)
        + [short, short, pl.BlockSpec((1, 8, rows), lambda p: (p, 0, 0))],
        out_specs=[short, tall, tall, pl.BlockSpec((1, 2, 8, rows), lambda p: (p, 0, 0, 0))],
        out_shape=[
            jax.ShapeDtypeStruct((rows, width), BF16),
            jax.ShapeDtypeStruct((window, width), BF16),
            jax.ShapeDtypeStruct((window, width), BF16),
            jax.ShapeDtypeStruct((pairs, 2, 8, rows), F32),
        ],
        compiler_params=pltpu.CompilerParams(vmem_limit_bytes=VMEM_LIMIT),
        cost_estimate=LITTLE,
        name="attend_back",
    )(ranges, far_bias, queries, both, both, *operands)


def flatten_kernel(rows_ref, flat_ref):
    flat_ref[...] = rows_ref[...].T


def flatten(window, rows):
    return pl.pallas_call(
        flatten_kernel,
        grid=(window.shape[0] // rows,),
        in_specs=[pl.BlockSpec((rows, window.shape[1]), lambda n: (n, 0))],
        out_specs=pair_block(window.shape[1], rows),
        out_shape=jax.ShapeDtypeStruct(window.shape[::-1], BF16),
        compiler_params=pltpu.CompilerParams(vmem_limit_bytes=VMEM_LIMIT),
        cost_estimate=LITTLE,
        name="flatten",
    )(window)


def collect_kernel(count, *refs):
    half = refs[-1].shape[1]
    flat_refs, grad_refs = refs[:count], refs[count : 4 * count]
    out_part_ref, keep_ref, send_ref = refs[4 * count :]
    for number in range(3):
        grad = jnp.zeros((2 * half, keep_ref.shape[2]), F32)
        for flat_ref, grad_ref in zip(flat_refs, grad_refs[number::3]):
            grad = grad + dot(flat_ref[:, : grad_ref.shape[0]], grad_ref[...])
        keep_ref[number] = grad[:half].astype(BF16)
        send_ref[number] = grad[half:].astype(BF16)
    keep_ref[3] = out_part_ref[:half, :]
    send_ref[3] = out_part_ref[half:, :]


def collect(windows_flat, grads, out_part):
    count = len(grads)
    chunk = 4 * HD
    flat_grads = [part for grad in grads for part in grad]
    return pl.pallas_call(
        functools.partial(collect_kernel, count),
        grid=(D // chunk,),
        in_specs=[same_block(*part.shape) for part in windows_flat]
        + [pair_block(part.shape[0], chunk) for part in (*flat_grads, out_part)],
        out_specs=[pair_block(4, D // 2, chunk)] * 2,
        out_shape=[jax.ShapeDtypeStruct((4, D // 2, D), BF16)] * 2,
        compiler_params=pltpu.CompilerParams(vmem_limit_bytes=VMEM_LIMIT),
        cost_estimate=LITTLE,
        name="collect",
    )(*windows_flat, *flat_grads, out_part)


CUBE = 0.044715
ROOT = (2.0 / 3.141592653589793) ** 0.5


def feed_kernel(normed_ref, hidden_ref, near_ref, other_ref, out_ref, act_ref, slope_ref):
    @pl.when(pl.program_id(0) == 0)
    def _():
        out_ref[...] = hidden_ref[...]

    pre = dot(normed_ref[...], whole_rows(near_ref, other_ref, 0))
    square = pre * pre
    bend = jnp.tanh(ROOT * pre * (1.0 + CUBE * square))
    gate = 0.5 * (1.0 + bend)
    act = (pre * gate).astype(BF16)
    slope = gate + 0.5 * pre * (1.0 - bend * bend) * (ROOT * (1.0 + 3.0 * CUBE * square))
    act_ref[...] = act
    slope_ref[...] = slope.astype(BF16)
    out_ref[...] += dot(act, whole_rows(near_ref, other_ref, 1), NT)


def feed_back_kernel(
    normed_ref, up_ref, near_ref, other_ref, act_ref, slope_ref, out_ref, keep_ref, send_ref,
    normed_flat_ref, up_flat_ref,
):
    half = keep_ref.shape[1]

    @pl.when(pl.program_id(0) == 0)
    def _():
        out_ref[...] = jnp.zeros_like(out_ref)
        normed_flat_ref[...] = normed_ref[...].T
        up_flat_ref[...] = up_ref[...].T

    act_grad = dot(up_ref[...], whole_rows(near_ref, other_ref, 1))
    pre_grad = (act_grad * slope_ref[...].astype(F32)).astype(BF16)
    out_ref[...] += dot(pre_grad, whole_rows(near_ref, other_ref, 0), NT)
    for number, grad in enumerate(
        (dot(normed_flat_ref[...], pre_grad), dot(up_flat_ref[...], act_ref[...]))
    ):
        keep_ref[number] = grad[:half].astype(BF16)
        send_ref[number] = grad[half:].astype(BF16)


def unit_chunk(units):
    return 512 if units % 512 == 0 else units


def feed(normed, hidden, near, other):
    count, width = normed.shape
    _, half, units = near.shape
    chunk = unit_chunk(units)
    weights = pair_block(2, half, chunk)
    wide = pair_block(count, chunk)
    return pl.pallas_call(
        feed_kernel,
        grid=(units // chunk,),
        in_specs=[same_block(count, width), same_block(count, width), weights, weights],
        out_specs=[same_block(count, width), wide, wide],
        out_shape=[
            jax.ShapeDtypeStruct((count, width), F32),
            jax.ShapeDtypeStruct((count, units), BF16),
            jax.ShapeDtypeStruct((count, units), BF16),
        ],
        compiler_params=pltpu.CompilerParams(vmem_limit_bytes=VMEM_LIMIT),
        cost_estimate=LITTLE,
        name="feed",
    )(normed, hidden, near, other)


def feed_back(normed, upstream, near, other, act, slope):
    count, width = normed.shape
    _, half, units = near.shape
    chunk = unit_chunk(units)
    weights = pair_block(2, half, chunk)
    wide = pair_block(count, chunk)
    return pl.pallas_call(
        feed_back_kernel,
        grid=(units // chunk,),
        in_specs=[same_block(count, width), same_block(count, width), weights, weights, wide, wide],
        out_specs=[same_block(count, width), weights, weights],
        out_shape=[
            jax.ShapeDtypeStruct((count, width), F32),
            jax.ShapeDtypeStruct((2, half, units), BF16),
            jax.ShapeDtypeStruct((2, half, units), BF16),
        ],
        scratch_shapes=[pltpu.VMEM((width, count), BF16), pltpu.VMEM((width, count), BF16)],
        compiler_params=pltpu.CompilerParams(vmem_limit_bytes=VMEM_LIMIT),
        cost_estimate=LITTLE,
        name="feed_back",
    )(normed, upstream, near, other, act, slope)


def contrast_kernel(
    micro_count, segment_count, rank_ref, pooled_ref, near_ref, other_ref, turn_ref, grad_ref, proj_grad_ref
):
    every = pooled_ref.shape[0]
    own = micro_count * segment_count

    def place(axis):
        number = lax.broadcasted_iota(jnp.int32, (every, every), axis)
        segment = number % segment_count
        micro = (number // segment_count) % micro_count
        owner = rank_ref[0] ^ (number // own)
        return owner * segment_count + segment, micro

    spot, micro = place(0)
    other_spot, other_micro = place(1)
    together = micro == other_micro
    pooled = dot(pooled_ref[:, :D], turn_ref[...]).astype(BF16)
    proj = jnp.concatenate([near_ref[...], other_ref[...]], axis=0)
    marks = pooled_ref[:, D:].astype(F32)
    target = (marks[:, 0:1] * 16.0 + marks[:, 1:2]).astype(jnp.int32)
    picked = target + (target >= spot).astype(jnp.int32)
    chosen = together & (picked == other_spot)
    embedded = dot(pooled, proj)
    inverse = lax.rsqrt(jnp.sum(embedded * embedded, axis=1, keepdims=True) + EPS_NORM)
    unit = (embedded * inverse).astype(BF16)
    logits = jnp.where(together & (spot != other_spot), SIM_SCALE * dot(unit, unit, NT), NEG_FILL)
    shifted = jnp.exp(logits - jnp.max(logits, axis=1, keepdims=True))
    shares = shifted / jnp.sum(shifted, axis=1, keepdims=True)
    logit_grad = (shares - chosen.astype(F32)).astype(BF16)
    unit_grad = SIM_SCALE * (dot(logit_grad, unit) + dot(logit_grad, unit, TN))
    unit_grad = unit_grad.astype(BF16).astype(F32)
    along = jnp.sum(unit_grad * embedded, axis=1, keepdims=True)
    embed_grad = inverse * unit_grad - embedded * (inverse * inverse * inverse) * along
    embed_grad = embed_grad.astype(BF16)
    grad_ref[...] = dot(embed_grad[:own], proj, NT)
    proj_grad_ref[...] = dot(pooled, embed_grad, TN)


def contrast(rank, pooled, near, other, turn, micro_count, segment_count):
    vmem = pl.BlockSpec(memory_space=pltpu.VMEM)
    return pl.pallas_call(
        functools.partial(contrast_kernel, micro_count, segment_count),
        in_specs=[pl.BlockSpec(memory_space=pltpu.SMEM), vmem, vmem, vmem, vmem],
        out_specs=[vmem, vmem],
        out_shape=[
            jax.ShapeDtypeStruct((micro_count * segment_count, D), F32),
            jax.ShapeDtypeStruct((D, D), F32),
        ],
        compiler_params=pltpu.CompilerParams(vmem_limit_bytes=VMEM_LIMIT),
        cost_estimate=LITTLE,
        name="contrast",
    )(rank, pooled, near, other, turn)


def pack_kernel(parts, *refs):
    ffn_ref, proj_ref, gains_ref, table_ref, total_ref, small_ref = refs[parts:]
    squares = jnp.zeros((1, 1), F32)

    def square(values):
        return jnp.sum(jnp.sum(values * values, axis=1, keepdims=True), axis=0, keepdims=True)

    for layer in range(total_ref.shape[0]):
        total = refs[0][layer].astype(F32)
        for ref in refs[1:parts]:
            total = total + ref[layer].astype(F32)
        total_ref[layer] = total
        squares = squares + square(total)
    for layer in range(ffn_ref.shape[0]):
        squares = squares + square(ffn_ref[layer])
    squares = squares + square(proj_ref[...])
    small_ref[0:3, :] = gains_ref[...]
    small_ref[3:4, :] = table_ref[...]
    small_ref[4:8, :] = jnp.broadcast_to(squares, (4, small_ref.shape[1]))


def pack(parts, ffn, proj, gains, table_row):
    return pl.pallas_call(
        functools.partial(pack_kernel, len(parts)),
        out_shape=[
            jax.ShapeDtypeStruct(parts[0].shape, F32),
            jax.ShapeDtypeStruct((8, gains.shape[1]), F32),
        ],
        compiler_params=pltpu.CompilerParams(vmem_limit_bytes=VMEM_LIMIT),
        name="pack",
    )(*parts, ffn, proj, gains, table_row)


def update_kernel(matrices, *refs):
    small_ref, grad_refs, rest = refs[0], refs[1 : matrices + 1], refs[matrices + 1 :]
    old_refs, norm_ref, new_refs = rest[: 3 * matrices + 3], rest[3 * matrices + 3], rest[3 * matrices + 4 :]
    few = small_ref[0:4, :]
    total = small_ref[4:5, 0:1] + jnp.sum(
        jnp.sum(few * few, axis=1, keepdims=True), axis=0, keepdims=True
    )
    norm = jnp.sqrt(total)
    norm_ref[...] = norm
    factor = jnp.minimum(1.0, CLIP_NORM / (norm + 1e-06))
    for number in range(matrices + 1):
        weight_ref, first_ref, second_ref = old_refs[3 * number : 3 * number + 3]
        is_matrix = number < matrices
        rate, decay = (RATE_MATRIX, DECAY_MATRIX) if is_matrix else (RATE_SMALL, 0.0)
        layers = range(weight_ref.shape[0]) if len(weight_ref.shape) == 3 else [Ellipsis]
        for layer in layers:
            grad = grad_refs[number][layer] if is_matrix else small_ref[0:3, :]
            results = adam_update(
                weight_ref[layer], grad * factor, first_ref[layer], second_ref[layer], rate, decay
            )
            for new_ref, result in zip(new_refs[3 * number : 3 * number + 3], results):
                new_ref[layer] = result


def update(small, grads, old):
    flat = [part for group in old for part in group]
    return pl.pallas_call(
        functools.partial(update_kernel, len(grads)),
        out_shape=[jax.ShapeDtypeStruct((1, 1), F32)]
        + [jax.ShapeDtypeStruct(part.shape, F32) for part in flat],
        compiler_params=pltpu.CompilerParams(vmem_limit_bytes=VMEM_LIMIT),
        name="update",
    )(small, *grads, *flat)


def local(
    tokens,
    cotangent,
    segment_ids,
    targets,
    attention_weights,
    feedforward_weights,
    projection,
    norm_gains,
    bias_table,
    attention_first,
    attention_second,
    feedforward_first,
    feedforward_second,
    projection_first,
    projection_second,
    gains_first,
    gains_second,
    bias_first,
    bias_second,
):
    wide_count = lax.axis_size("dp")
    narrow_count = lax.axis_size("mp")
    wide_rank = lax.axis_index("dp")
    narrow_rank = lax.axis_index("mp")
    micro_count, _, rows, _ = tokens.shape
    segment_count = targets.shape[2]
    block = D // wide_count
    heads_part = attention_weights.shape[2] // HD
    reach = min(narrow_count - 1, -(-(SEG_MOST - 1) // rows))
    span = 2 * reach + 1

    feature = jnp.arange(D, dtype=jnp.int32)
    place = feature // block
    order = outer_masks() + core_masks()
    away = sum(((place >> bit) & 1) * mask for bit, mask in enumerate(order)) + jnp.zeros_like(place)
    source = (wide_rank ^ away) * block + feature % block
    turn = (feature[:, None] == source[None, :]).astype(BF16)
    turn_wide = turn.astype(F32)

    attention_low = attention_weights.astype(BF16)
    feedforward_low = feedforward_weights.astype(BF16)
    projection_low = projection.astype(BF16)

    token_rows = dot(tokens.reshape(micro_count * rows, D), turn)
    gains = dot(norm_gains, turn_wide, precision=HIGHEST)
    factor_one = norm_factor(token_rows)
    normed_one = (token_rows * factor_one * gains[0]).astype(BF16)
    normed_one = normed_one.reshape(micro_count, rows, D)

    head = jnp.arange(bias_table.shape[1], dtype=jnp.int32)
    head_source = (narrow_rank ^ (head // heads_part)) * heads_part + head % heads_part
    head_turn = (head[:, None] == head_source[None, :]).astype(F32)

    is_even = narrow_rank % 2 == 0

    def hop(held):
        return link(held[1], False), link(held[0], True)

    hops = [[] for _ in range(micro_count)]

    def window_of(micro):
        return jnp.concatenate([normed_one[micro]] + [part for pair in hops[micro] for part in pair])

    def project(micro):
        return (
            dot(normed_one[micro], w_query).astype(BF16),
            dot(windows[micro], w_both).astype(BF16),
        )

    def finish_hops(micro):
        while len(hops[micro]) < reach:
            hops[micro].append(hop(hops[micro][-1]))

    def chain_step(values, bit):
        return jnp.concatenate([values, swap(values, "mp", bit)], axis=-1)

    bits = []
    while 1 << len(bits) < narrow_count:
        bits.append(1 << len(bits))
    attn_parts = gather_columns(attention_low)
    ffn_cols = feedforward_low
    for bit in bits[:1]:
        ffn_cols = chain_step(ffn_cols, bit)
    attn_parts, ffn_cols, normed_late = after((attn_parts, ffn_cols, normed_one))
    segment_ids, bias_late, targets_late = after((segment_ids, bias_table, targets), *attn_parts)
    table = dot(bias_late, head_turn, precision=HIGHEST)
    tiles = bias_tiles(table, rows)
    marks = jnp.stack([targets_late[:, 0] // 16, targets_late[:, 0] % 16], axis=-1).astype(BF16)
    marks = jnp.pad(marks[None], ((0, 0), (0, 0), (0, 0), (0, 126)))
    attn_held = gather_plane(jnp.concatenate([attention_low] + attn_parts, axis=-1))
    for bit in bits[1:]:
        ffn_cols = chain_step(ffn_cols, bit)
    attn_held, ffn_cols, normed_late, tiles, marks = after(
        (attn_held, ffn_cols, normed_late, tiles, marks)
    )
    attn_near, attn_other = halves(attn_held)
    first_hop = hop((normed_late, normed_late))
    parts = [ffn_cols[0][None], ffn_cols[1][None]]

    def outer_received(number):
        return [gather_outer(part, number, first) for part, first in zip(parts, (True, False))]

    def outer_joined(received):
        return [
            join_outer(part, got, first) for part, got, first in zip(parts, received, (True, False))
        ]

    outer_count = len(outer_masks())
    received = outer_received(0)
    attn_other, first_hop, received = after((attn_other, first_hop, received))
    parts = outer_joined(received)
    attn_all = jnp.concatenate([attn_near, attn_other], axis=1)
    w_query, w_out = attn_all[0], attn_all[3]
    w_both = jnp.concatenate([attn_all[1], attn_all[2]], axis=1)
    for micro in range(micro_count):
        hops[micro].append((first_hop[0][micro], first_hop[1][micro]))
    finish_hops(0)
    proj_parts = gather_columns(after(projection_low, attn_other))
    w_both, w_query, hops, parts, proj_parts = after((w_both, w_query, hops, parts, proj_parts))
    proj_cols = jnp.concatenate([projection_low] + proj_parts, axis=-1)[None]
    windows = [window_of(0)]
    projected = [project(0)]
    slots = jnp.stack(
        [
            jnp.int32(0)
            if n == 0
            else jnp.where(is_even == (n > 0), 2 * abs(n) - 1, 2 * abs(n)).astype(jnp.int32)
            for n in range(-reach, reach + 1)
        ]
    )

    far_bias = jnp.stack([table[15], table[31]])
    lanes = jnp.arange(2 * HD, dtype=jnp.int32) % HD
    padded = jnp.pad(
        segment_ids[:, 0], ((0, 0), (reach * rows, reach * rows)), constant_values=segment_count
    )
    window_segments = lax.dynamic_slice_in_dim(padded, narrow_rank * rows, span * rows, 1)
    own_segments = window_segments[:, reach * rows : (reach + 1) * rows]
    key_marks = (window_segments[:, :, None] == lanes).astype(BF16)
    query_marks = jnp.where(
        (own_segments[:, :, None] != lanes) & (lanes <= segment_count), MASKED, 0.0
    ).astype(BF16)
    first, last = own_segments[:, 0], own_segments[:, -1]
    low_count = sum(
        (window_segments[:, (reach - n) * rows + rows - 1] == first).astype(jnp.int32)
        for n in range(1, reach + 1)
    )
    high_count = sum(
        (window_segments[:, (reach + n) * rows] == last).astype(jnp.int32)
        for n in range(1, reach + 1)
    )
    ranges = jnp.concatenate(
        [
            jnp.stack([low_count, high_count], axis=1),
            jnp.broadcast_to(slots, (micro_count, span)),
        ],
        axis=1,
    )

    mixed, kept = [], []
    proj_held = []
    for micro in range(micro_count):
        came, received = [], []
        parts, projected[micro] = after((parts, projected[micro]))
        if micro == 0 and outer_count > 1:
            received = outer_received(1)
        if micro + 1 < micro_count:
            finish_hops(micro + 1)
            came = hops[micro + 1]
        else:
            proj_held = gather_plane(after(proj_cols, projected[micro][0]))
        operands = (
            ranges[micro], far_bias, *projected[micro], query_marks[micro], key_marks[micro], tiles
        )
        mixed_part, logs = attend(reach, *operands)
        came, mixed_part, proj_held = after((came, mixed_part, proj_held))
        if came:
            hops[micro + 1] = came
            windows.append(window_of(micro + 1))
            projected.append(project(micro + 1))
        if received:
            last_received = received
        kept.append((operands, mixed_part, logs))
        mixed.append(mixed_part)
    if outer_count > 1:
        last_received, mixed = after((last_received, mixed))
        parts = outer_joined(last_received)
    for number in range(2, outer_count):
        parts = outer_joined(outer_received(number))
    ffn_near, ffn_other = halves(jnp.stack(parts))
    hidden_one = token_rows + dot(jnp.concatenate(mixed, axis=0), w_out, NT)
    proj_near, proj_other = halves(proj_held)
    windows_flat = [flatten(window, rows) for window in windows]
    hidden_one, ffn_other, proj_other, windows_flat = after(
        (hidden_one, ffn_other, proj_other, windows_flat)
    )

    factor_two = norm_factor(hidden_one)
    normed_two = (hidden_one * factor_two * gains[1]).astype(BF16)
    hidden_two, activated, slopes = feed(normed_two, hidden_one, ffn_near, ffn_other)
    output = dot(hidden_two.astype(BF16), turn, NT).astype(BF16)

    factor_three = norm_factor(hidden_two)
    unit_three = hidden_two * factor_three
    normed_three = (unit_three * gains[2]).reshape(micro_count, rows, D)
    numbers = jnp.arange(segment_count, dtype=jnp.int32)
    member = (own_segments[:, None, :] == numbers[None, :, None]).astype(F32)
    counts = jnp.sum(
        (segment_ids[:, 0][:, None, :] == numbers[None, :, None]).astype(F32), axis=2, keepdims=True
    )
    pooled = lax.dot_general(
        member, normed_three, (((2,), (1,)), ((0,), (0,))), precision=HIGHEST, preferred_element_type=F32
    )
    pooled = sum_at_once(pooled, "mp") / counts
    pooled = dot(pooled.reshape(-1, D).astype(BF16), turn, NT).astype(BF16)
    pooled = pooled.reshape(1, micro_count, segment_count, D)
    pooled_all = gather_wide(jnp.concatenate([pooled, marks], axis=-1))
    rank = jnp.stack([wide_rank, narrow_rank]).astype(jnp.int32)
    pooled_grad, proj_grad = contrast(
        rank, pooled_all.reshape(-1, pooled_all.shape[-1]), proj_near[0], proj_other[0], turn,
        micro_count, segment_count,
    )
    proj_reduced = proj_grad[:block, : projection.shape[1]]
    pooled_grad = pooled_grad.reshape(micro_count, segment_count, D) / counts
    normed_three_grad = lax.dot_general(
        member, pooled_grad, (((1,), (1,)), ((0,), (0,))), precision=HIGHEST, preferred_element_type=F32
    ).reshape(micro_count * rows, D)
    gain_three = jnp.sum(normed_three_grad * unit_three, axis=0)

    upstream = dot(cotangent.reshape(micro_count * rows, D), turn)
    hidden_two_grad = upstream + norm_back(hidden_two, factor_three, normed_three_grad * gains[2])
    hidden_two_low = hidden_two_grad.astype(BF16)
    normed_two_grad, ffn_keep, ffn_send = feed_back(
        normed_two, hidden_two_low, ffn_near, ffn_other, activated, slopes
    )
    ffn_received = swap(ffn_send, "dp", 1)
    gain_two = jnp.sum(normed_two_grad * hidden_one * factor_two, axis=0)
    hidden_one_grad = hidden_two_grad + norm_back(
        hidden_one, factor_two, normed_two_grad * gains[1]
    )
    hidden_one_low = hidden_one_grad.astype(BF16)
    mixed_grad = dot(hidden_one_low, w_out).astype(BF16).reshape(micro_count, rows, D)
    out_part = dot(hidden_one_low, jnp.concatenate(mixed, axis=0), TN).astype(BF16)
    ffn_received, mixed_grad, out_part = after((ffn_received, mixed_grad, out_part))

    def outer_split(parts):
        return [split_outer(terms, masks, first) for (terms, masks), first in zip(parts, (False, True))]

    ffn_blocks = [to_blocks(ffn_keep), to_blocks(ffn_received)]
    parts = [([held[number] for held in ffn_blocks], outer_masks()) for number in range(2)]
    grads, owns, bias_parts, flows = [], [], [], []

    def leave(flow, n):
        even, odd = flow[2 * n - 2], flow[2 * n - 1]
        return link(even, False), link(odd, True)

    def join(flow, n, came):
        if n > 0:
            flow[2 * n - 1] = add_low(flow[2 * n - 1], came[0])
            flow[2 * n - 2] = add_low(flow[2 * n - 2], came[1])

    def flow_of(dq, dk, dv):
        partial = dot(dk, w_both[:, :D], NT) + dot(dv, w_both[:, D:], NT)
        own = partial[:rows] + dot(dq, w_query, NT)
        low_parts = partial.astype(BF16)
        return own, [low_parts[n * rows : (n + 1) * rows] for n in range(1, span)]

    came = []
    for micro in range(micro_count):
        operands, mixed_part, logs = kept[micro]
        last = micro == micro_count - 1
        steps = outer_split(parts) if parts[0][1] else []
        upstream_low, flows, sent = after(
            (mixed_grad[micro], flows, [step[1] for step in steps])
        )
        received = [swap(leaves, "dp", step[2]) for leaves, step in zip(sent, steps)]
        came = [leave(flow, reach) for flow in flows]
        dq, dk, dv, bias_part = attend_back(reach, *operands, upstream_low, mixed_part, logs)
        flow = None if last else flow_of(dq, dk, dv)
        received, came, dq, dk, dv, flow = after(
            (received, came, dq, dk, dv, flow)
        )
        if steps:
            parts = [(step[0] + [got], step[3]) for step, got in zip(steps, received)]
        grads.append((dq, dk, dv))
        bias_parts.append(bias_part)
        if not last:
            owns.append(flow[0])
            flows.append(list(flow[1]))
    while parts[0][1]:
        parts = [
            (stay + [swap(leaves, "dp", mask)], masks)
            for stay, leaves, mask, masks in outer_split(parts)
        ]
    others = came
    for flow, got in zip(flows, others):
        join(flow, reach - 1, got)
    ffn_last = [add_low(*terms)[0] for terms, _ in parts]
    ffn_last, grads = after((ffn_last, grads))
    ffn_last = jnp.stack(ffn_last)
    ffn_column = send_columns_chain(ffn_last)
    attn_keep, attn_send = collect(windows_flat, grads, out_part)
    last = flow_of(*grads[-1])
    attn_keep, attn_send, ffn_column, flows, owns, last = after(
        (attn_keep, attn_send, ffn_column, flows, owns, last)
    )
    owns.append(last[0])
    last = list(last[1])
    attn_received = swap(attn_send, "dp", 1)
    came = leave(last, reach) if reach > 1 else ()
    ffn_reduced = finish_columns_chain(ffn_last, ffn_column)
    attn_received, came, ffn_reduced = after((attn_received, came, ffn_reduced))
    attn_held = to_blocks(add_low(attn_keep, attn_received))
    if reach > 1:
        join(last, reach - 1, came)
    flow = [jnp.stack(pair) for pair in zip(*flows, last)]
    attn_held, flow = after((attn_held, flow))
    attn_received = send_plane(attn_held)
    for n in range(reach - 1, 0, -1):
        came = leave(flow, n)
        join(flow, n - 1, came)
    attn_received, came = after((attn_received, came))
    attn_last = add_low(attn_held[:, 0], *attn_received)
    attn_columns = send_columns(attn_last)
    normed_one_grad = jnp.stack(owns) + came[0].astype(F32) + came[1].astype(F32)
    normed_one_grad = normed_one_grad.reshape(micro_count * rows, D)
    gain_one = jnp.sum(normed_one_grad * token_rows * factor_one, axis=0)
    tokens_grad = hidden_one_grad + norm_back(token_rows, factor_one, normed_one_grad * gains[0])
    tokens_grad = dot(tokens_grad, turn_wide, NT, HIGHEST)
    attn_columns, tokens_grad, gain_one = after((attn_columns, tokens_grad, gain_one))

    bias_sum = sum(bias_parts)
    heads = table.shape[1]
    bias_sum = bias_sum.reshape(heads, 8, rows)
    spot = (jnp.arange(rows, dtype=jnp.int32) + 1) % rows
    relative = jnp.where(spot < FAR, -spot, rows - spot)
    buckets = jnp.arange(table.shape[0], dtype=jnp.int32)
    near_hot = (bucket_of(relative)[:, None] == buckets[None, :]) & (
        jnp.abs(relative) < FAR
    )[:, None]
    table_grad = dot(near_hot.astype(F32), bias_sum[:, 0], (((0,), (1,)), ((), ())), HIGHEST)
    table_grad = (
        table_grad
        + (buckets == 15).astype(F32)[:, None] * jnp.sum(bias_sum[:, 1], axis=1)[None, :]
        + (buckets == 31).astype(F32)[:, None] * jnp.sum(bias_sum[:, 2], axis=1)[None, :]
    )
    full_table = dot(table_grad, head_turn, NT, HIGHEST)
    gains_part = dot(jnp.stack([gain_one, gain_two, gain_three]), turn_wide, NT, HIGHEST)
    table_row = jnp.pad(full_table.reshape(1, -1), ((0, 0), (0, D - full_table.size)))
    attn_reduced, small = pack(
        [attn_last[..., : attn_columns[0].shape[-1]], *attn_columns],
        ffn_reduced, proj_reduced, gains_part, table_row,
    )
    small = sum_everywhere(small)
    table_full_grad = small[3, : full_table.size].reshape(full_table.shape)
    grad_norm, *updated = update(
        small,
        [attn_reduced, ffn_reduced, proj_reduced],
        [
            (attention_weights, attention_first, attention_second),
            (feedforward_weights, feedforward_first, feedforward_second),
            (projection, projection_first, projection_second),
            (norm_gains, gains_first, gains_second),
        ],
    )
    grad_norm = grad_norm.reshape(())
    attn_new, ffn_new, proj_new, gains_new = (updated[3 * k : 3 * k + 3] for k in range(4))
    factor = jnp.minimum(1.0, CLIP_NORM / (grad_norm + 1e-06))
    table_new = adam_update(
        bias_table, table_full_grad * factor, bias_first, bias_second, RATE_SMALL, 0.0
    )
    return (
        output.reshape(tokens.shape),
        tokens_grad.reshape(tokens.shape),
        grad_norm,
        *attn_new,
        *ffn_new,
        *proj_new,
        *gains_new,
        *table_new,
    )


def solution(mesh):
    return jax.shard_map(
        local,
        mesh=mesh,
        in_specs=(
            P(None, "dp", "mp", None),
            P(None, "dp", "mp", None),
            P(None, "dp", None),
            P(None, "dp", None),
            P(None, "dp", "mp"),
            P(None, "dp", "mp"),
            P("dp", "mp"),
            P(),
            P(),
            P(None, "dp", "mp"),
            P(None, "dp", "mp"),
            P(None, "dp", "mp"),
            P(None, "dp", "mp"),
            P("dp", "mp"),
            P("dp", "mp"),
            P(),
            P(),
            P(),
            P(),
        ),
        out_specs=(
            P(None, "dp", "mp", None),
            P(None, "dp", "mp", None),
            P(),
            P(None, "dp", "mp"),
            P(None, "dp", "mp"),
            P(None, "dp", "mp"),
            P(None, "dp", "mp"),
            P(None, "dp", "mp"),
            P(None, "dp", "mp"),
            P("dp", "mp"),
            P("dp", "mp"),
            P("dp", "mp"),
            P(),
            P(),
            P(),
            P(),
            P(),
            P(),
        ),
        check_vma=False,
    )
```

```python
import functools

import jax
import jax.numpy as jnp
from jax import lax
from jax.experimental import pallas as pl
from jax.experimental.pallas import tpu as pltpu
from jax.sharding import PartitionSpec as P

D = 768
HD = 64
STEP = 10
SEG_MOST = 512

EPS_NORM = 1e-06
EPS_ADAM = 1e-08
SIM_SCALE = 50.0
NEG_FILL = -1000000000.0
BETA_ONE = 0.9
BETA_TWO = 0.999
CLIP_NORM = 1.0
RATE_MATRIX = 0.05
RATE_SMALL = 0.2
DECAY_MATRIX = 0.01
LIMITS = (12, 16, 23, 32, 46, 64, 91)
FAR = LIMITS[-1]
MASKED = -float(2**30)
HIGHEST = lax.Precision.HIGHEST
BF16 = jnp.bfloat16
F32 = jnp.float32
NN = (((1,), (0,)), ((), ()))
NT = (((1,), (1,)), ((), ()))
TN = (((0,), (0,)), ((), ()))
VMEM_LIMIT = 48 * 1024 * 1024


def dot(left, right, dims=NN, precision=None):
    return lax.dot_general(left, right, dims, precision=precision, preferred_element_type=F32)


def bucket_of(relative):
    distance = jnp.abs(relative)
    far_bucket = 8 + sum(((distance >= threshold).astype(jnp.int32) for threshold in LIMITS))
    near_bucket = jnp.where(distance < 8, distance, far_bucket)
    return near_bucket + 16 * (relative > 0).astype(jnp.int32)


def norm_factor(values):
    return lax.rsqrt(jnp.mean(values * values, axis=-1, keepdims=True) + EPS_NORM)


def norm_back(values, factor, upstream):
    return factor * upstream - values * (factor * factor * factor) * jnp.mean(
        upstream * values, axis=-1, keepdims=True
    )


def adam_update(weight_now, clipped, first_old, second_old, step_rate, weight_decay):
    first_new = BETA_ONE * first_old + (1.0 - BETA_ONE) * clipped
    second_new = BETA_TWO * second_old + (1.0 - BETA_TWO) * clipped * clipped
    first_hat = first_new / (1.0 - BETA_ONE**STEP)
    second_hat = second_new / (1.0 - BETA_TWO**STEP)
    weight_new = weight_now - step_rate * (
        first_hat / (jnp.sqrt(second_hat) + EPS_ADAM) + weight_decay * weight_now
    )
    return (weight_new, first_new, second_new)


def swap(values, axis, mask):
    count = lax.axis_size(axis)
    return lax.ppermute(values, axis, [(i, i ^ mask) for i in range(count)])


def link(values, odd):
    count = lax.axis_size("mp")
    pairs = [(i, i + 1) for i in range(int(odd), count - 1, 2)]
    return lax.ppermute(values, "mp", pairs + [(j, i) for i, j in pairs])


def gather_columns_chain(values):
    bit = 1
    while bit < lax.axis_size("mp"):
        values = jnp.concatenate([values, swap(values, "mp", bit)], axis=-1)
        bit *= 2
    return values


def after(values, *earlier):
    return lax.optimization_barrier((values,) + earlier)[0]


def outer_masks():
    return [1 << bit for bit in range(1, lax.axis_size("dp").bit_length() - 1)]


def core_masks():
    return [1] if lax.axis_size("dp") > 1 else []


def gather_columns(values):
    return [swap(values, "mp", k) for k in range(1, lax.axis_size("mp"))]


def plane_masks():
    masks = [0]
    for mask in outer_masks():
        masks += [held | mask for held in masks]
    return masks[1:]


def gather_plane(values):
    return jnp.stack([values] + [swap(values, "dp", mask) for mask in plane_masks()], axis=1)


def halves(values):
    c, n, r, w = values.shape
    near = values.reshape(c, n * r, w)
    return near, swap(near, "dp", 1)


def to_blocks(values):
    c, rows, w = values.shape
    count = lax.axis_size("dp") // 2
    return values.reshape(c, count, rows // count, w)


def add_low(stay, *received):
    return sum([part.astype(F32) for part in received], stay.astype(F32)).astype(BF16)


def split_outer(terms, masks, first):
    spot = 0 if first else len(masks) - 1
    c, n, r, w = terms[0].shape
    split = [term.reshape(c, n >> (spot + 1), 2, 1 << spot, r, w) for term in terms]
    stay, leave = ([term[:, :, k].reshape(c, n // 2, r, w) for term in split] for k in range(2))
    return stay, add_low(*leave), masks[spot], masks[:spot] + masks[spot + 1 :]


def gather_outer(part, number, low_first):
    masks = outer_masks()
    return swap(part, "dp", masks[number] if low_first else masks[len(masks) - 1 - number])


def join_outer(part, received, low_first):
    if low_first:
        return jnp.concatenate([part, received], axis=0)
    n, r, w = part.shape
    return jnp.stack([part, received], axis=1).reshape(2 * n, r, w)


def send_columns(values):
    count = lax.axis_size("mp")
    width = values.shape[-1] // count
    return [swap(values[..., k * width : (k + 1) * width], "mp", k) for k in range(1, count)]


def send_columns_chain(values):
    count = lax.axis_size("mp")
    if count == 1:
        return values[..., :0]
    return swap(values[..., values.shape[-1] // 2 :], "mp", count // 2)


def finish_columns_chain(values, received):
    bit = lax.axis_size("mp") // 2
    while bit:
        half = values.shape[-1] // 2
        values = values[..., :half].astype(F32) + received.astype(F32)
        bit //= 2
        if bit:
            received = swap(values[..., half // 2 :].astype(BF16), "mp", bit)
    return values


def add_columns(values, received):
    width = values.shape[-1] // lax.axis_size("mp")
    return sum([part.astype(F32) for part in received], values[..., :width].astype(F32))


def sum_over(values, axis):
    bit = 1
    while bit < lax.axis_size(axis):
        values = values + swap(values, axis, bit)
        bit *= 2
    return values


def sum_at_once(values, axis):
    received = [values] + [swap(values, axis, mask) for mask in range(1, lax.axis_size(axis))]
    while len(received) > 1:
        received = [one + two for one, two in zip(received[::2], received[1::2])]
    return received[0]


def sum_everywhere(values):
    if lax.axis_size("dp") != 8:
        return sum_over(sum_over(values, "dp"), "mp")
    values = values + swap(values, "dp", 1)
    across = [swap(values, "dp", mask) for mask in (2, 4, 6)]
    values = (values + across[0]) + (across[1] + across[2])
    return sum_at_once(values, "mp")


def gather_wide(values):
    if lax.axis_size("dp") != 8:
        return gather_near(values)
    values = jnp.concatenate([values, swap(values, "dp", 1)], axis=0)
    return jnp.concatenate([values] + [swap(values, "dp", mask) for mask in (2, 4, 6)], axis=0)


def gather_near(values):
    bit = 1
    while bit < lax.axis_size("dp"):
        values = jnp.concatenate([values, swap(values, "dp", bit)], axis=0)
        bit *= 2
    return values


def bias_kernel(line_ref, tile_ref):
    rows = tile_ref.shape[2]
    for block in range(tile_ref.shape[1]):
        line = jnp.broadcast_to(line_ref[0, block : block + 1, :], (rows, 2 * rows))
        tile_ref[0, block] = pltpu.roll(line, 0, 1, stride=1, stride_axis=0)[:, :rows]


def bias_tiles(table, rows):
    heads = table.shape[1]
    lane = jnp.arange(2 * rows, dtype=jnp.int32)
    back = jnp.where(lane < rows, lane, lane - 2 * rows)
    relative = (jnp.arange(3, dtype=jnp.int32)[:, None] - 1) * rows - back[None, :]
    hot = (bucket_of(relative)[..., None] == jnp.arange(table.shape[0])).astype(F32)
    lines = dot(table, hot.reshape(-1, table.shape[0]), (((0,), (1,)), ((), ())), HIGHEST)
    lines = lines.reshape(heads, 3, 2 * rows)
    return pl.pallas_call(
        bias_kernel,
        grid=(heads,),
        in_specs=[pl.BlockSpec((1, 3, 2 * rows), lambda h: (h, 0, 0))],
        out_specs=pl.BlockSpec((1, 3, rows, rows), lambda h: (h, 0, 0, 0)),
        out_shape=jax.ShapeDtypeStruct((heads, 3, rows, rows), F32),
        compiler_params=pltpu.CompilerParams(vmem_limit_bytes=VMEM_LIMIT),
    )(lines)


def own_lanes(shape, part):
    lane = lax.broadcasted_iota(jnp.int32, shape, 1)
    return (lane < HD) if part == 0 else (lane >= HD)


def block_choices(reach):
    return [
        (lo, hi) for lo in range(reach + 1) for hi in range(reach + 1) if lo + hi < 2 * reach
    ]


def whole_rows(near_ref, far_ref, number):
    return jnp.concatenate([near_ref[number], far_ref[number]], axis=0)


def forward_kernel(reach, range_ref, far_ref, q_ref, k_ref, v_ref, qf_ref, kf_ref, bias_ref, o_ref, log_ref):
    pair = pl.program_id(0)
    rows = q_ref.shape[0]
    score_scale = HD ** (-0.5)
    low, high = range_ref[0], range_ref[1]

    def slot_of(block):
        return pl.ds(pl.multiple_of(range_ref[2 + block + reach] * rows, rows), rows)

    def work(lo, hi):
        query = q_ref[...] * jnp.asarray(score_scale, BF16)
        mixed, logs = [], []
        for part in range(2):
            own_q = own_lanes((rows, 2 * HD), part)
            query_low = jnp.where(own_q, query, qf_ref[...])
            scores = []
            for block in range(-lo, hi + 1):
                spot = pl.ds((block + reach) * rows, rows)
                key_low = jnp.where(own_q, k_ref[slot_of(block), :], kf_ref[spot, :])
                score = dot(key_low, query_low, NT)
                if abs(block) <= 1:
                    score = score + bias_ref[part, block + 1]
                else:
                    score = score + far_ref[int(block > 0), 2 * pair + part]
                scores.append(score)
            peak = jnp.max(functools.reduce(jnp.maximum, scores), axis=0, keepdims=True)
            total = jnp.zeros((2 * HD, rows), F32)
            for number, block in enumerate(range(-lo, hi + 1)):
                probs = jnp.exp(scores[number] - peak).astype(BF16)
                value_low = jnp.where(own_q, v_ref[slot_of(block), :], jnp.ones((), BF16))
                total = total + dot(value_low, probs, TN)
            row_sum = total[HD * (1 - part) : HD * (1 - part) + 1, :]
            mixed.append(total[HD * part : HD * (part + 1), :] / row_sum)
            logs.append(peak + jnp.log(row_sum))
        o_ref[...] = jnp.concatenate(mixed, axis=0).T.astype(BF16)
        log_ref[0] = jnp.concatenate(logs + [jnp.zeros((6, rows), F32)], axis=0)

    for lo, hi in block_choices(reach):
        pl.when((low == lo) & (high == hi))(functools.partial(work, lo, hi))


def backward_kernel(
    reach, range_ref, far_ref, q_ref, k_ref, v_ref, qf_ref, kf_ref, bias_ref, do_ref, o_ref, log_ref,
    dq_ref, dk_ref, dv_ref, bias_grad_ref,
):
    pair = pl.program_id(0)
    rows = q_ref.shape[0]
    score_scale = HD ** (-0.5)
    low, high = range_ref[0], range_ref[1]

    def slot_of(block):
        return pl.ds(pl.multiple_of(range_ref[2 + block + reach] * rows, rows), rows)

    def work(lo, hi):
        query = q_ref[...] * jnp.asarray(score_scale, BF16)
        upstream = do_ref[...]
        products = (upstream.astype(F32) * o_ref[...].astype(F32)).T
        nothing = jnp.zeros((), BF16)
        ahead = lax.broadcasted_iota(jnp.int32, (rows, rows), 0) - lax.broadcasted_iota(
            jnp.int32, (rows, rows), 1
        )
        own, query_low, query_own, up_own, delta, log_row, dq, near, far = ([None, None] for _ in range(9))
        for part in range(2):
            own[part] = own_lanes((rows, 2 * HD), part)
            query_low[part] = jnp.where(own[part], query, qf_ref[...])
            query_own[part] = jnp.where(own[part], query, nothing)
            up_own[part] = jnp.where(own[part], upstream, nothing)
            delta[part] = jnp.sum(products[HD * part : HD * (part + 1), :], axis=0, keepdims=True)
            log_row[part] = log_ref[0, part : part + 1, :]
            dq[part] = jnp.zeros((2 * HD, rows), F32)
            near[part] = jnp.zeros((rows, rows), F32)
            far[part] = [jnp.zeros((1, rows), F32), jnp.zeros((1, rows), F32)]
        for block in range(-reach, reach + 1):
            if not -lo <= block <= hi:
                dk_ref[slot_of(block), :] = jnp.zeros((rows, 2 * HD), BF16)
                dv_ref[slot_of(block), :] = jnp.zeros((rows, 2 * HD), BF16)
                continue
            spot = pl.ds((block + reach) * rows, rows)
            dk = jnp.zeros((rows, 2 * HD), F32)
            dv = jnp.zeros((rows, 2 * HD), F32)
            for part in range(2):
                key = k_ref[slot_of(block), :]
                score = dot(jnp.where(own[part], key, kf_ref[spot, :]), query_low[part], NT)
                if abs(block) <= 1:
                    score = score + bias_ref[part, block + 1]
                else:
                    score = score + far_ref[int(block > 0), 2 * pair + part]
                probs = jnp.exp(score - log_row[part])
                dprobs = dot(v_ref[slot_of(block), :], up_own[part], NT)
                dscore = probs * (dprobs - delta[part])
                probs_low, dscore_low = probs.astype(BF16), dscore.astype(BF16)
                dv = dv + dot(probs_low, up_own[part])
                dk = dk + dot(dscore_low, query_own[part])
                dq[part] = dq[part] + dot(key, dscore_low, TN)
                if block == 0:
                    close = jnp.abs(ahead) < FAR
                    near[part] = near[part] + jnp.where(close, dscore, 0.0)
                    far[part][0] += jnp.sum(jnp.where(ahead <= -FAR, dscore, 0.0), axis=0, keepdims=True)
                    far[part][1] += jnp.sum(jnp.where(ahead >= FAR, dscore, 0.0), axis=0, keepdims=True)
                elif abs(block) == 1:
                    close = (ahead < FAR - rows) if block > 0 else (ahead > rows - FAR)
                    near[part] = near[part] + jnp.where(close, dscore, 0.0)
                    far[part][int(block > 0)] += jnp.sum(jnp.where(close, 0.0, dscore), axis=0, keepdims=True)
                else:
                    far[part][int(block > 0)] += jnp.sum(dscore, axis=0, keepdims=True)
            dk_ref[slot_of(block), :] = dk.astype(BF16)
            dv_ref[slot_of(block), :] = dv.astype(BF16)
        dq_ref[...] = (
            jnp.concatenate([dq[0][:HD], dq[1][HD:]], axis=0).T * score_scale
        ).astype(BF16)
        flip = (
            lax.broadcasted_iota(jnp.int32, (rows, rows), 0) + lax.broadcasted_iota(jnp.int32, (rows, rows), 1)
            == rows - 1
        ).astype(BF16)
        for part in range(2):
            turned = dot(flip, near[part].astype(BF16))
            turned = pltpu.roll(turned, 0, 1, stride=1, stride_axis=0)
            line = jnp.sum(turned, axis=0, keepdims=True)
            bias_grad_ref[0, part] = jnp.concatenate(
                [line, far[part][0], far[part][1], jnp.zeros((5, rows), F32)], axis=0
            )

    for lo, hi in block_choices(reach):
        pl.when((low == lo) & (high == hi))(functools.partial(work, lo, hi))


def pair_block(*shape):
    count = len(shape)
    return pl.BlockSpec(shape, lambda p: (0,) * (count - 1) + (p,))


def same_block(*shape):
    count = len(shape)
    return pl.BlockSpec(shape, lambda p: (0,) * count)


def attention_specs(rows, window, pairs):
    smem = pl.BlockSpec(memory_space=pltpu.SMEM)
    return [
        smem,
        smem,
        pair_block(rows, 2 * HD),
        pair_block(window, 2 * HD),
        pl.BlockSpec((window, 2 * HD), lambda p: (0, pairs + p)),
        same_block(rows, 2 * HD),
        same_block(window, 2 * HD),
        pl.BlockSpec((2, 3, rows, rows), lambda p: (p, 0, 0, 0)),
    ]


LITTLE = pl.CostEstimate(flops=10**5, bytes_accessed=10**4, transcendentals=0)


def attend(reach, ranges, far_bias, queries, both, *operands):
    rows, width = queries.shape
    window = both.shape[0]
    pairs = width // (2 * HD)
    return pl.pallas_call(
        functools.partial(forward_kernel, reach),
        grid=(pairs,),
        in_specs=attention_specs(rows, window, pairs),
        out_specs=[pair_block(rows, 2 * HD), pl.BlockSpec((1, 8, rows), lambda p: (p, 0, 0))],
        out_shape=[
            jax.ShapeDtypeStruct((rows, width), BF16),
            jax.ShapeDtypeStruct((pairs, 8, rows), F32),
        ],
        compiler_params=pltpu.CompilerParams(vmem_limit_bytes=VMEM_LIMIT),
        cost_estimate=LITTLE,
        name="attend",
    )(ranges, far_bias, queries, both, both, *operands)


def attend_back(reach, ranges, far_bias, queries, both, *operands):
    rows, width = queries.shape
    window = both.shape[0]
    pairs = width // (2 * HD)
    tall, short = pair_block(window, 2 * HD), pair_block(rows, 2 * HD)
    return pl.pallas_call(
        functools.partial(backward_kernel, reach),
        grid=(pairs,),
        in_specs=attention_specs(rows, window, pairs)
        + [short, short, pl.BlockSpec((1, 8, rows), lambda p: (p, 0, 0))],
        out_specs=[short, tall, tall, pl.BlockSpec((1, 2, 8, rows), lambda p: (p, 0, 0, 0))],
        out_shape=[
            jax.ShapeDtypeStruct((rows, width), BF16),
            jax.ShapeDtypeStruct((window, width), BF16),
            jax.ShapeDtypeStruct((window, width), BF16),
            jax.ShapeDtypeStruct((pairs, 2, 8, rows), F32),
        ],
        compiler_params=pltpu.CompilerParams(vmem_limit_bytes=VMEM_LIMIT),
        cost_estimate=LITTLE,
        name="attend_back",
    )(ranges, far_bias, queries, both, both, *operands)


def flatten_kernel(rows_ref, flat_ref):
    flat_ref[...] = rows_ref[...].T


def flatten(window, rows):
    return pl.pallas_call(
        flatten_kernel,
        grid=(window.shape[0] // rows,),
        in_specs=[pl.BlockSpec((rows, window.shape[1]), lambda n: (n, 0))],
        out_specs=pair_block(window.shape[1], rows),
        out_shape=jax.ShapeDtypeStruct(window.shape[::-1], BF16),
        compiler_params=pltpu.CompilerParams(vmem_limit_bytes=VMEM_LIMIT),
        cost_estimate=LITTLE,
        name="flatten",
    )(window)


def collect_kernel(count, *refs):
    half = refs[-1].shape[1]
    flat_refs, grad_refs = refs[:count], refs[count : 4 * count]
    out_part_ref, keep_ref, send_ref = refs[4 * count :]
    for number in range(3):
        grad = jnp.zeros((2 * half, keep_ref.shape[2]), F32)
        for flat_ref, grad_ref in zip(flat_refs, grad_refs[number::3]):
            grad = grad + dot(flat_ref[:, : grad_ref.shape[0]], grad_ref[...])
        keep_ref[number] = grad[:half].astype(BF16)
        send_ref[number] = grad[half:].astype(BF16)
    keep_ref[3] = out_part_ref[:half, :]
    send_ref[3] = out_part_ref[half:, :]


def collect(windows_flat, grads, out_part):
    count = len(grads)
    chunk = 4 * HD
    flat_grads = [part for grad in grads for part in grad]
    return pl.pallas_call(
        functools.partial(collect_kernel, count),
        grid=(D // chunk,),
        in_specs=[same_block(*part.shape) for part in windows_flat]
        + [pair_block(part.shape[0], chunk) for part in (*flat_grads, out_part)],
        out_specs=[pair_block(4, D // 2, chunk)] * 2,
        out_shape=[jax.ShapeDtypeStruct((4, D // 2, D), BF16)] * 2,
        compiler_params=pltpu.CompilerParams(vmem_limit_bytes=VMEM_LIMIT),
        cost_estimate=LITTLE,
        name="collect",
    )(*windows_flat, *flat_grads, out_part)


CUBE = 0.044715
ROOT = (2.0 / 3.141592653589793) ** 0.5


def feed_kernel(normed_ref, hidden_ref, near_ref, other_ref, out_ref, act_ref, slope_ref):
    @pl.when(pl.program_id(0) == 0)
    def _():
        out_ref[...] = hidden_ref[...]

    pre = dot(normed_ref[...], whole_rows(near_ref, other_ref, 0))
    square = pre * pre
    bend = jnp.tanh(ROOT * pre * (1.0 + CUBE * square))
    gate = 0.5 * (1.0 + bend)
    act = (pre * gate).astype(BF16)
    slope = gate + 0.5 * pre * (1.0 - bend * bend) * (ROOT * (1.0 + 3.0 * CUBE * square))
    act_ref[...] = act
    slope_ref[...] = slope.astype(BF16)
    out_ref[...] += dot(act, whole_rows(near_ref, other_ref, 1), NT)


def feed_back_kernel(
    normed_ref, up_ref, near_ref, other_ref, act_ref, slope_ref, out_ref, keep_ref, send_ref,
    normed_flat_ref, up_flat_ref,
):
    half = keep_ref.shape[1]

    @pl.when(pl.program_id(0) == 0)
    def _():
        out_ref[...] = jnp.zeros_like(out_ref)
        normed_flat_ref[...] = normed_ref[...].T
        up_flat_ref[...] = up_ref[...].T

    act_grad = dot(up_ref[...], whole_rows(near_ref, other_ref, 1))
    pre_grad = (act_grad * slope_ref[...].astype(F32)).astype(BF16)
    out_ref[...] += dot(pre_grad, whole_rows(near_ref, other_ref, 0), NT)
    for number, grad in enumerate(
        (dot(normed_flat_ref[...], pre_grad), dot(up_flat_ref[...], act_ref[...]))
    ):
        keep_ref[number] = grad[:half].astype(BF16)
        send_ref[number] = grad[half:].astype(BF16)


def unit_chunk(units):
    return 512 if units % 512 == 0 else units


def feed(normed, hidden, near, other):
    count, width = normed.shape
    _, half, units = near.shape
    chunk = unit_chunk(units)
    weights = pair_block(2, half, chunk)
    wide = pair_block(count, chunk)
    return pl.pallas_call(
        feed_kernel,
        grid=(units // chunk,),
        in_specs=[same_block(count, width), same_block(count, width), weights, weights],
        out_specs=[same_block(count, width), wide, wide],
        out_shape=[
            jax.ShapeDtypeStruct((count, width), F32),
            jax.ShapeDtypeStruct((count, units), BF16),
            jax.ShapeDtypeStruct((count, units), BF16),
        ],
        compiler_params=pltpu.CompilerParams(vmem_limit_bytes=VMEM_LIMIT),
        cost_estimate=LITTLE,
        name="feed",
    )(normed, hidden, near, other)


def feed_back(normed, upstream, near, other, act, slope):
    count, width = normed.shape
    _, half, units = near.shape
    chunk = unit_chunk(units)
    weights = pair_block(2, half, chunk)
    wide = pair_block(count, chunk)
    return pl.pallas_call(
        feed_back_kernel,
        grid=(units // chunk,),
        in_specs=[same_block(count, width), same_block(count, width), weights, weights, wide, wide],
        out_specs=[same_block(count, width), weights, weights],
        out_shape=[
            jax.ShapeDtypeStruct((count, width), F32),
            jax.ShapeDtypeStruct((2, half, units), BF16),
            jax.ShapeDtypeStruct((2, half, units), BF16),
        ],
        scratch_shapes=[pltpu.VMEM((width, count), BF16), pltpu.VMEM((width, count), BF16)],
        compiler_params=pltpu.CompilerParams(vmem_limit_bytes=VMEM_LIMIT),
        cost_estimate=LITTLE,
        name="feed_back",
    )(normed, upstream, near, other, act, slope)


def contrast_kernel(
    micro_count, segment_count, rank_ref, pooled_ref, near_ref, other_ref, turn_ref, grad_ref, proj_grad_ref
):
    every = pooled_ref.shape[0]
    own = micro_count * segment_count

    def place(axis):
        number = lax.broadcasted_iota(jnp.int32, (every, every), axis)
        segment = number % segment_count
        micro = (number // segment_count) % micro_count
        owner = rank_ref[0] ^ (number // own)
        return owner * segment_count + segment, micro

    spot, micro = place(0)
    other_spot, other_micro = place(1)
    together = micro == other_micro
    pooled = dot(pooled_ref[:, :D], turn_ref[...]).astype(BF16)
    proj = jnp.concatenate([near_ref[...], other_ref[...]], axis=0)
    marks = pooled_ref[:, D:].astype(F32)
    target = (marks[:, 0:1] * 16.0 + marks[:, 1:2]).astype(jnp.int32)
    picked = target + (target >= spot).astype(jnp.int32)
    chosen = together & (picked == other_spot)
    embedded = dot(pooled, proj)
    inverse = lax.rsqrt(jnp.sum(embedded * embedded, axis=1, keepdims=True) + EPS_NORM)
    unit = (embedded * inverse).astype(BF16)
    logits = jnp.where(together & (spot != other_spot), SIM_SCALE * dot(unit, unit, NT), NEG_FILL)
    shifted = jnp.exp(logits - jnp.max(logits, axis=1, keepdims=True))
    shares = shifted / jnp.sum(shifted, axis=1, keepdims=True)
    logit_grad = (shares - chosen.astype(F32)).astype(BF16)
    unit_grad = SIM_SCALE * (dot(logit_grad, unit) + dot(logit_grad, unit, TN))
    unit_grad = unit_grad.astype(BF16).astype(F32)
    along = jnp.sum(unit_grad * embedded, axis=1, keepdims=True)
    embed_grad = inverse * unit_grad - embedded * (inverse * inverse * inverse) * along
    embed_grad = embed_grad.astype(BF16)
    grad_ref[...] = dot(embed_grad[:own], proj, NT)
    proj_grad_ref[...] = dot(pooled, embed_grad, TN)


def contrast(rank, pooled, near, other, turn, micro_count, segment_count):
    vmem = pl.BlockSpec(memory_space=pltpu.VMEM)
    return pl.pallas_call(
        functools.partial(contrast_kernel, micro_count, segment_count),
        in_specs=[pl.BlockSpec(memory_space=pltpu.SMEM), vmem, vmem, vmem, vmem],
        out_specs=[vmem, vmem],
        out_shape=[
            jax.ShapeDtypeStruct((micro_count * segment_count, D), F32),
            jax.ShapeDtypeStruct((D, D), F32),
        ],
        compiler_params=pltpu.CompilerParams(vmem_limit_bytes=VMEM_LIMIT),
        cost_estimate=LITTLE,
        name="contrast",
    )(rank, pooled, near, other, turn)


def pack_kernel(parts, *refs):
    ffn_ref, proj_ref, gains_ref, table_ref, total_ref, small_ref = refs[parts:]
    squares = jnp.zeros((1, 1), F32)

    def square(values):
        return jnp.sum(jnp.sum(values * values, axis=1, keepdims=True), axis=0, keepdims=True)

    for layer in range(total_ref.shape[0]):
        total = refs[0][layer].astype(F32)
        for ref in refs[1:parts]:
            total = total + ref[layer].astype(F32)
        total_ref[layer] = total
        squares = squares + square(total)
    for layer in range(ffn_ref.shape[0]):
        squares = squares + square(ffn_ref[layer])
    squares = squares + square(proj_ref[...])
    small_ref[0:3, :] = gains_ref[...]
    small_ref[3:4, :] = table_ref[...]
    small_ref[4:8, :] = jnp.broadcast_to(squares, (4, small_ref.shape[1]))


def pack(parts, ffn, proj, gains, table_row):
    return pl.pallas_call(
        functools.partial(pack_kernel, len(parts)),
        out_shape=[
            jax.ShapeDtypeStruct(parts[0].shape, F32),
            jax.ShapeDtypeStruct((8, gains.shape[1]), F32),
        ],
        compiler_params=pltpu.CompilerParams(vmem_limit_bytes=VMEM_LIMIT),
        name="pack",
    )(*parts, ffn, proj, gains, table_row)


def update_kernel(matrices, *refs):
    small_ref, grad_refs, rest = refs[0], refs[1 : matrices + 1], refs[matrices + 1 :]
    old_refs, norm_ref, new_refs = rest[: 3 * matrices + 3], rest[3 * matrices + 3], rest[3 * matrices + 4 :]
    few = small_ref[0:4, :]
    total = small_ref[4:5, 0:1] + jnp.sum(
        jnp.sum(few * few, axis=1, keepdims=True), axis=0, keepdims=True
    )
    norm = jnp.sqrt(total)
    norm_ref[...] = norm
    factor = jnp.minimum(1.0, CLIP_NORM / (norm + 1e-06))
    for number in range(matrices + 1):
        weight_ref, first_ref, second_ref = old_refs[3 * number : 3 * number + 3]
        is_matrix = number < matrices
        rate, decay = (RATE_MATRIX, DECAY_MATRIX) if is_matrix else (RATE_SMALL, 0.0)
        layers = range(weight_ref.shape[0]) if len(weight_ref.shape) == 3 else [Ellipsis]
        for layer in layers:
            grad = grad_refs[number][layer] if is_matrix else small_ref[0:3, :]
            results = adam_update(
                weight_ref[layer], grad * factor, first_ref[layer], second_ref[layer], rate, decay
            )
            for new_ref, result in zip(new_refs[3 * number : 3 * number + 3], results):
                new_ref[layer] = result


def update(small, grads, old):
    flat = [part for group in old for part in group]
    return pl.pallas_call(
        functools.partial(update_kernel, len(grads)),
        out_shape=[jax.ShapeDtypeStruct((1, 1), F32)]
        + [jax.ShapeDtypeStruct(part.shape, F32) for part in flat],
        compiler_params=pltpu.CompilerParams(vmem_limit_bytes=VMEM_LIMIT),
        name="update",
    )(small, *grads, *flat)


def local(
    tokens,
    cotangent,
    segment_ids,
    targets,
    attention_weights,
    feedforward_weights,
    projection,
    norm_gains,
    bias_table,
    attention_first,
    attention_second,
    feedforward_first,
    feedforward_second,
    projection_first,
    projection_second,
    gains_first,
    gains_second,
    bias_first,
    bias_second,
):
    wide_count = lax.axis_size("dp")
    narrow_count = lax.axis_size("mp")
    wide_rank = lax.axis_index("dp")
    narrow_rank = lax.axis_index("mp")
    micro_count, _, rows, _ = tokens.shape
    segment_count = targets.shape[2]
    block = D // wide_count
    heads_part = attention_weights.shape[2] // HD
    reach = min(narrow_count - 1, -(-(SEG_MOST - 1) // rows))
    span = 2 * reach + 1

    feature = jnp.arange(D, dtype=jnp.int32)
    place = feature // block
    order = outer_masks() + core_masks()
    away = sum(((place >> bit) & 1) * mask for bit, mask in enumerate(order)) + jnp.zeros_like(place)
    source = (wide_rank ^ away) * block + feature % block
    turn = (feature[:, None] == source[None, :]).astype(BF16)
    turn_wide = turn.astype(F32)

    attention_low = attention_weights.astype(BF16)
    feedforward_low = feedforward_weights.astype(BF16)
    projection_low = projection.astype(BF16)

    token_rows = dot(tokens.reshape(micro_count * rows, D), turn)
    gains = dot(norm_gains, turn_wide, precision=HIGHEST)
    factor_one = norm_factor(token_rows)
    normed_one = (token_rows * factor_one * gains[0]).astype(BF16)
    normed_one = normed_one.reshape(micro_count, rows, D)

    head = jnp.arange(bias_table.shape[1], dtype=jnp.int32)
    head_source = (narrow_rank ^ (head // heads_part)) * heads_part + head % heads_part
    head_turn = (head[:, None] == head_source[None, :]).astype(F32)

    is_even = narrow_rank % 2 == 0

    def hop(held):
        return link(held[1], False), link(held[0], True)

    hops = [[] for _ in range(micro_count)]

    def window_of(micro):
        return jnp.concatenate([normed_one[micro]] + [part for pair in hops[micro] for part in pair])

    def project(micro):
        return (
            dot(normed_one[micro], w_query).astype(BF16),
            dot(windows[micro], w_both).astype(BF16),
        )

    def finish_hops(micro):
        while len(hops[micro]) < reach:
            hops[micro].append(hop(hops[micro][-1]))

    def chain_step(values, bit):
        return jnp.concatenate([values, swap(values, "mp", bit)], axis=-1)

    bits = []
    while 1 << len(bits) < narrow_count:
        bits.append(1 << len(bits))
    attn_parts = gather_columns(attention_low)
    ffn_cols = feedforward_low
    for bit in bits[:1]:
        ffn_cols = chain_step(ffn_cols, bit)
    attn_parts, ffn_cols, normed_late = after((attn_parts, ffn_cols, normed_one))
    segment_ids, bias_late, targets_late = after((segment_ids, bias_table, targets), *attn_parts)
    table = dot(bias_late, head_turn, precision=HIGHEST)
    tiles = bias_tiles(table, rows)
    marks = jnp.stack([targets_late[:, 0] // 16, targets_late[:, 0] % 16], axis=-1).astype(BF16)
    marks = jnp.pad(marks[None], ((0, 0), (0, 0), (0, 0), (0, 126)))
    attn_held = gather_plane(jnp.concatenate([attention_low] + attn_parts, axis=-1))
    for bit in bits[1:]:
        ffn_cols = chain_step(ffn_cols, bit)
    attn_held, ffn_cols, normed_late, tiles, marks = after(
        (attn_held, ffn_cols, normed_late, tiles, marks)
    )
    attn_near, attn_other = halves(attn_held)
    first_hop = hop((normed_late, normed_late))
    parts = [ffn_cols[0][None], ffn_cols[1][None]]

    def outer_received(number):
        return [gather_outer(part, number, first) for part, first in zip(parts, (True, False))]

    def outer_joined(received):
        return [
            join_outer(part, got, first) for part, got, first in zip(parts, received, (True, False))
        ]

    outer_count = len(outer_masks())
    received = outer_received(0)
    attn_other, first_hop, received = after((attn_other, first_hop, received))
    parts = outer_joined(received)
    attn_all = jnp.concatenate([attn_near, attn_other], axis=1)
    w_query, w_out = attn_all[0], attn_all[3]
    w_both = jnp.concatenate([attn_all[1], attn_all[2]], axis=1)
    for micro in range(micro_count):
        hops[micro].append((first_hop[0][micro], first_hop[1][micro]))
    finish_hops(0)
    proj_parts = gather_columns(after(projection_low, attn_other))
    w_both, w_query, hops, parts, proj_parts = after((w_both, w_query, hops, parts, proj_parts))
    proj_cols = jnp.concatenate([projection_low] + proj_parts, axis=-1)[None]
    windows = [window_of(0)]
    projected = [project(0)]
    slots = jnp.stack(
        [
            jnp.int32(0)
            if n == 0
            else jnp.where(is_even == (n > 0), 2 * abs(n) - 1, 2 * abs(n)).astype(jnp.int32)
            for n in range(-reach, reach + 1)
        ]
    )

    far_bias = jnp.stack([table[15], table[31]])
    lanes = jnp.arange(2 * HD, dtype=jnp.int32) % HD
    padded = jnp.pad(
        segment_ids[:, 0], ((0, 0), (reach * rows, reach * rows)), constant_values=segment_count
    )
    window_segments = lax.dynamic_slice_in_dim(padded, narrow_rank * rows, span * rows, 1)
    own_segments = window_segments[:, reach * rows : (reach + 1) * rows]
    key_marks = (window_segments[:, :, None] == lanes).astype(BF16)
    query_marks = jnp.where(
        (own_segments[:, :, None] != lanes) & (lanes <= segment_count), MASKED, 0.0
    ).astype(BF16)
    first, last = own_segments[:, 0], own_segments[:, -1]
    low_count = sum(
        (window_segments[:, (reach - n) * rows + rows - 1] == first).astype(jnp.int32)
        for n in range(1, reach + 1)
    )
    high_count = sum(
        (window_segments[:, (reach + n) * rows] == last).astype(jnp.int32)
        for n in range(1, reach + 1)
    )
    ranges = jnp.concatenate(
        [
            jnp.stack([low_count, high_count], axis=1),
            jnp.broadcast_to(slots, (micro_count, span)),
        ],
        axis=1,
    )

    mixed, kept = [], []
    proj_held = []
    for micro in range(micro_count):
        came, received = [], []
        parts, projected[micro] = after((parts, projected[micro]))
        if micro == 0 and outer_count > 1:
            received = outer_received(1)
        if micro + 1 < micro_count:
            finish_hops(micro + 1)
            came = hops[micro + 1]
        else:
            proj_held = gather_plane(after(proj_cols, projected[micro][0]))
        operands = (
            ranges[micro], far_bias, *projected[micro], query_marks[micro], key_marks[micro], tiles
        )
        mixed_part, logs = attend(reach, *operands)
        came, mixed_part, proj_held = after((came, mixed_part, proj_held))
        if came:
            hops[micro + 1] = came
            windows.append(window_of(micro + 1))
            projected.append(project(micro + 1))
        if received:
            last_received = received
        kept.append((operands, mixed_part, logs))
        mixed.append(mixed_part)
    if outer_count > 1:
        last_received, mixed = after((last_received, mixed))
        parts = outer_joined(last_received)
    for number in range(2, outer_count):
        parts = outer_joined(outer_received(number))
    ffn_near, ffn_other = halves(jnp.stack(parts))
    hidden_one = token_rows + dot(jnp.concatenate(mixed, axis=0), w_out, NT)
    proj_near, proj_other = halves(proj_held)
    windows_flat = [flatten(window, rows) for window in windows]
    hidden_one, ffn_other, proj_other, windows_flat = after(
        (hidden_one, ffn_other, proj_other, windows_flat)
    )

    factor_two = norm_factor(hidden_one)
    normed_two = (hidden_one * factor_two * gains[1]).astype(BF16)
    hidden_two, activated, slopes = feed(normed_two, hidden_one, ffn_near, ffn_other)
    output = dot(hidden_two.astype(BF16), turn, NT).astype(BF16)

    factor_three = norm_factor(hidden_two)
    unit_three = hidden_two * factor_three
    normed_three = (unit_three * gains[2]).reshape(micro_count, rows, D)
    numbers = jnp.arange(segment_count, dtype=jnp.int32)
    member = (own_segments[:, None, :] == numbers[None, :, None]).astype(F32)
    counts = jnp.sum(
        (segment_ids[:, 0][:, None, :] == numbers[None, :, None]).astype(F32), axis=2, keepdims=True
    )
    pooled = lax.dot_general(
        member, normed_three, (((2,), (1,)), ((0,), (0,))), precision=HIGHEST, preferred_element_type=F32
    )
    pooled = sum_at_once(pooled, "mp") / counts
    pooled = dot(pooled.reshape(-1, D).astype(BF16), turn, NT).astype(BF16)
    pooled = pooled.reshape(1, micro_count, segment_count, D)
    pooled_all = gather_wide(jnp.concatenate([pooled, marks], axis=-1))
    rank = jnp.stack([wide_rank, narrow_rank]).astype(jnp.int32)
    pooled_grad, proj_grad = contrast(
        rank, pooled_all.reshape(-1, pooled_all.shape[-1]), proj_near[0], proj_other[0], turn,
        micro_count, segment_count,
    )
    proj_reduced = proj_grad[:block, : projection.shape[1]]
    pooled_grad = pooled_grad.reshape(micro_count, segment_count, D) / counts
    normed_three_grad = lax.dot_general(
        member, pooled_grad, (((1,), (1,)), ((0,), (0,))), precision=HIGHEST, preferred_element_type=F32
    ).reshape(micro_count * rows, D)
    gain_three = jnp.sum(normed_three_grad * unit_three, axis=0)

    upstream = dot(cotangent.reshape(micro_count * rows, D), turn)
    hidden_two_grad = upstream + norm_back(hidden_two, factor_three, normed_three_grad * gains[2])
    hidden_two_low = hidden_two_grad.astype(BF16)
    normed_two_grad, ffn_keep, ffn_send = feed_back(
        normed_two, hidden_two_low, ffn_near, ffn_other, activated, slopes
    )
    ffn_received = swap(ffn_send, "dp", 1)
    gain_two = jnp.sum(normed_two_grad * hidden_one * factor_two, axis=0)
    hidden_one_grad = hidden_two_grad + norm_back(
        hidden_one, factor_two, normed_two_grad * gains[1]
    )
    hidden_one_low = hidden_one_grad.astype(BF16)
    mixed_grad = dot(hidden_one_low, w_out).astype(BF16).reshape(micro_count, rows, D)
    out_part = dot(hidden_one_low, jnp.concatenate(mixed, axis=0), TN).astype(BF16)
    ffn_received, mixed_grad, out_part = after((ffn_received, mixed_grad, out_part))

    def outer_split(parts):
        return [split_outer(terms, masks, first) for (terms, masks), first in zip(parts, (False, True))]

    ffn_blocks = [to_blocks(ffn_keep), to_blocks(ffn_received)]
    parts = [
        ([held[number : number + 1] for held in ffn_blocks], outer_masks()) for number in range(2)
    ]
    grads, owns, bias_parts, flows = [], [], [], []

    def leave(flow, n):
        even, odd = flow[2 * n - 2], flow[2 * n - 1]
        return link(even, False), link(odd, True)

    def join(flow, n, came):
        if n > 0:
            flow[2 * n - 1] = add_low(flow[2 * n - 1], came[0])
            flow[2 * n - 2] = add_low(flow[2 * n - 2], came[1])

    def flow_of(dq, dk, dv):
        partial = dot(dk, w_both[:, :D], NT) + dot(dv, w_both[:, D:], NT)
        own = partial[:rows] + dot(dq, w_query, NT)
        low_parts = partial.astype(BF16)
        return own, [low_parts[n * rows : (n + 1) * rows] for n in range(1, span)]

    came = []
    for micro in range(micro_count):
        operands, mixed_part, logs = kept[micro]
        last = micro == micro_count - 1
        steps = outer_split(parts) if parts[0][1] else []
        upstream_low, flows, sent = after(
            (mixed_grad[micro], flows, [step[1] for step in steps])
        )
        received = [swap(leaves, "dp", step[2]) for leaves, step in zip(sent, steps)]
        came = [leave(flow, reach) for flow in flows]
        dq, dk, dv, bias_part = attend_back(reach, *operands, upstream_low, mixed_part, logs)
        flow = None if last else flow_of(dq, dk, dv)
        received, came, dq, dk, dv, flow = after(
            (received, came, dq, dk, dv, flow)
        )
        if steps:
            parts = [(step[0] + [got], step[3]) for step, got in zip(steps, received)]
        grads.append((dq, dk, dv))
        bias_parts.append(bias_part)
        if not last:
            owns.append(flow[0])
            flows.append(list(flow[1]))
    while parts[0][1]:
        parts = [
            (stay + [swap(leaves, "dp", mask)], masks)
            for stay, leaves, mask, masks in outer_split(parts)
        ]
    others = came
    for flow, got in zip(flows, others):
        join(flow, reach - 1, got)
    ffn_last = [add_low(*terms)[0, 0] for terms, _ in parts]
    ffn_last, grads = after((ffn_last, grads))
    ffn_last = jnp.stack(ffn_last)
    ffn_column = send_columns_chain(ffn_last)
    attn_keep, attn_send = collect(windows_flat, grads, out_part)
    last = flow_of(*grads[-1])
    attn_keep, attn_send, ffn_column, flows, owns, last = after(
        (attn_keep, attn_send, ffn_column, flows, owns, last)
    )
    owns.append(last[0])
    last = list(last[1])
    attn_received = swap(attn_send, "dp", 1)
    came = leave(last, reach) if reach > 1 else ()
    others = [leave(flow, 1) for flow in flows]
    attn_received, came, others, ffn_column = after((attn_received, came, others, ffn_column))
    attn_blocks = [to_blocks(attn_keep), to_blocks(attn_received)]
    attn_parts = [([held[k : k + 2] for held in attn_blocks], outer_masks()) for k in (0, 2)]
    if reach > 1:
        join(last, reach - 1, came)
    hopped, ffn_reduced = (), None
    while attn_parts[0][1]:
        steps = outer_split(attn_parts)
        sent, last = after(([step[1] for step in steps], last))
        received = [swap(leaves, "dp", step[2]) for leaves, step in zip(sent, steps)]
        if ffn_reduced is None:
            hopped = leave(last, 1)
            ffn_reduced = finish_columns_chain(ffn_last, ffn_column)
        received, hopped, ffn_reduced = after((received, hopped, ffn_reduced))
        attn_parts = [(step[0] + [got], step[3]) for step, got in zip(steps, received)]
    attn_last = jnp.concatenate([add_low(*terms) for terms, _ in attn_parts])[:, 0]
    attn_columns = send_columns(attn_last)
    normed_one_grad = jnp.concatenate(
        [
            own + even.astype(F32) + odd.astype(F32)
            for own, (even, odd) in zip(owns, [*others, hopped])
        ]
    )
    gain_one = jnp.sum(normed_one_grad * token_rows * factor_one, axis=0)
    tokens_grad = hidden_one_grad + norm_back(token_rows, factor_one, normed_one_grad * gains[0])
    tokens_grad = dot(tokens_grad, turn_wide, NT, HIGHEST)
    attn_columns, tokens_grad, gain_one = after((attn_columns, tokens_grad, gain_one))

    bias_sum = sum(bias_parts)
    heads = table.shape[1]
    bias_sum = bias_sum.reshape(heads, 8, rows)
    spot = (jnp.arange(rows, dtype=jnp.int32) + 1) % rows
    relative = jnp.where(spot < FAR, -spot, rows - spot)
    buckets = jnp.arange(table.shape[0], dtype=jnp.int32)
    near_hot = (bucket_of(relative)[:, None] == buckets[None, :]) & (
        jnp.abs(relative) < FAR
    )[:, None]
    table_grad = dot(near_hot.astype(F32), bias_sum[:, 0], (((0,), (1,)), ((), ())), HIGHEST)
    table_grad = (
        table_grad
        + (buckets == 15).astype(F32)[:, None] * jnp.sum(bias_sum[:, 1], axis=1)[None, :]
        + (buckets == 31).astype(F32)[:, None] * jnp.sum(bias_sum[:, 2], axis=1)[None, :]
    )
    full_table = dot(table_grad, head_turn, NT, HIGHEST)
    gains_part = dot(jnp.stack([gain_one, gain_two, gain_three]), turn_wide, NT, HIGHEST)
    table_row = jnp.pad(full_table.reshape(1, -1), ((0, 0), (0, D - full_table.size)))
    attn_reduced, small = pack(
        [attn_last[..., : attn_columns[0].shape[-1]], *attn_columns],
        ffn_reduced, proj_reduced, gains_part, table_row,
    )
    small = sum_everywhere(small)
    table_full_grad = small[3, : full_table.size].reshape(full_table.shape)
    grad_norm, *updated = update(
        small,
        [attn_reduced, ffn_reduced, proj_reduced],
        [
            (attention_weights, attention_first, attention_second),
            (feedforward_weights, feedforward_first, feedforward_second),
            (projection, projection_first, projection_second),
            (norm_gains, gains_first, gains_second),
        ],
    )
    grad_norm = grad_norm.reshape(())
    attn_new, ffn_new, proj_new, gains_new = (updated[3 * k : 3 * k + 3] for k in range(4))
    factor = jnp.minimum(1.0, CLIP_NORM / (grad_norm + 1e-06))
    table_new = adam_update(
        bias_table, table_full_grad * factor, bias_first, bias_second, RATE_SMALL, 0.0
    )
    return (
        output.reshape(tokens.shape),
        tokens_grad.reshape(tokens.shape),
        grad_norm,
        *attn_new,
        *ffn_new,
        *proj_new,
        *gains_new,
        *table_new,
    )


def solution(mesh):
    return jax.shard_map(
        local,
        mesh=mesh,
        in_specs=(
            P(None, "dp", "mp", None),
            P(None, "dp", "mp", None),
            P(None, "dp", None),
            P(None, "dp", None),
            P(None, "dp", "mp"),
            P(None, "dp", "mp"),
            P("dp", "mp"),
            P(),
            P(),
            P(None, "dp", "mp"),
            P(None, "dp", "mp"),
            P(None, "dp", "mp"),
            P(None, "dp", "mp"),
            P("dp", "mp"),
            P("dp", "mp"),
            P(),
            P(),
            P(),
            P(),
        ),
        out_specs=(
            P(None, "dp", "mp", None),
            P(None, "dp", "mp", None),
            P(),
            P(None, "dp", "mp"),
            P(None, "dp", "mp"),
            P(None, "dp", "mp"),
            P(None, "dp", "mp"),
            P(None, "dp", "mp"),
            P(None, "dp", "mp"),
            P("dp", "mp"),
            P("dp", "mp"),
            P("dp", "mp"),
            P(),
            P(),
            P(),
            P(),
            P(),
            P(),
        ),
        check_vma=False,
    )
```

```python
import functools

import jax
import jax.numpy as jnp
from jax import lax
from jax.experimental import pallas as pl
from jax.experimental.pallas import tpu as pltpu
from jax.sharding import PartitionSpec as P

D = 768
HD = 64
STEP = 10
SEG_MOST = 512

EPS_NORM = 1e-06
EPS_ADAM = 1e-08
SIM_SCALE = 50.0
NEG_FILL = -1000000000.0
BETA_ONE = 0.9
BETA_TWO = 0.999
CLIP_NORM = 1.0
RATE_MATRIX = 0.05
RATE_SMALL = 0.2
DECAY_MATRIX = 0.01
LIMITS = (12, 16, 23, 32, 46, 64, 91)
FAR = LIMITS[-1]
MASKED = -float(2**30)
HIGHEST = lax.Precision.HIGHEST
BF16 = jnp.bfloat16
F32 = jnp.float32
NN = (((1,), (0,)), ((), ()))
NT = (((1,), (1,)), ((), ()))
TN = (((0,), (0,)), ((), ()))
VMEM_LIMIT = 48 * 1024 * 1024


def dot(left, right, dims=NN, precision=None):
    return lax.dot_general(left, right, dims, precision=precision, preferred_element_type=F32)


def bucket_of(relative):
    distance = jnp.abs(relative)
    far_bucket = 8 + sum(((distance >= threshold).astype(jnp.int32) for threshold in LIMITS))
    near_bucket = jnp.where(distance < 8, distance, far_bucket)
    return near_bucket + 16 * (relative > 0).astype(jnp.int32)


def norm_factor(values):
    return lax.rsqrt(jnp.mean(values * values, axis=-1, keepdims=True) + EPS_NORM)


def norm_back(values, factor, upstream):
    return factor * upstream - values * (factor * factor * factor) * jnp.mean(
        upstream * values, axis=-1, keepdims=True
    )


def adam_update(weight_now, clipped, first_old, second_old, step_rate, weight_decay):
    first_new = BETA_ONE * first_old + (1.0 - BETA_ONE) * clipped
    second_new = BETA_TWO * second_old + (1.0 - BETA_TWO) * clipped * clipped
    first_hat = first_new / (1.0 - BETA_ONE**STEP)
    second_hat = second_new / (1.0 - BETA_TWO**STEP)
    weight_new = weight_now - step_rate * (
        first_hat / (jnp.sqrt(second_hat) + EPS_ADAM) + weight_decay * weight_now
    )
    return (weight_new, first_new, second_new)


def swap(values, axis, mask):
    count = lax.axis_size(axis)
    return lax.ppermute(values, axis, [(i, i ^ mask) for i in range(count)])


def link(values, odd):
    count = lax.axis_size("mp")
    pairs = [(i, i + 1) for i in range(int(odd), count - 1, 2)]
    return lax.ppermute(values, "mp", pairs + [(j, i) for i, j in pairs])


def gather_columns_chain(values):
    bit = 1
    while bit < lax.axis_size("mp"):
        values = jnp.concatenate([values, swap(values, "mp", bit)], axis=-1)
        bit *= 2
    return values


def after(values, *earlier):
    return lax.optimization_barrier((values,) + earlier)[0]


def outer_masks():
    return [1 << bit for bit in range(1, lax.axis_size("dp").bit_length() - 1)]


def core_masks():
    return [1] if lax.axis_size("dp") > 1 else []


def gather_columns(values):
    return [swap(values, "mp", k) for k in range(1, lax.axis_size("mp"))]


def plane_masks():
    masks = [0]
    for mask in outer_masks():
        masks += [held | mask for held in masks]
    return masks[1:]


def gather_plane(values):
    return jnp.stack([values] + [swap(values, "dp", mask) for mask in plane_masks()], axis=1)


def halves(values):
    c, n, r, w = values.shape
    near = values.reshape(c, n * r, w)
    return near, swap(near, "dp", 1)


def to_blocks(values):
    c, rows, w = values.shape
    count = lax.axis_size("dp") // 2
    return values.reshape(c, count, rows // count, w)


def add_low(stay, *received):
    return sum([part.astype(F32) for part in received], stay.astype(F32)).astype(BF16)


def split_outer(terms, masks, first):
    spot = 0 if first else len(masks) - 1
    c, n, r, w = terms[0].shape
    split = [term.reshape(c, n >> (spot + 1), 2, 1 << spot, r, w) for term in terms]
    stay, leave = ([term[:, :, k].reshape(c, n // 2, r, w) for term in split] for k in range(2))
    return stay, add_low(*leave), masks[spot], masks[:spot] + masks[spot + 1 :]


def gather_outer(part, number, low_first):
    masks = outer_masks()
    return swap(part, "dp", masks[number] if low_first else masks[len(masks) - 1 - number])


def join_outer(part, received, low_first):
    if low_first:
        return jnp.concatenate([part, received], axis=0)
    n, r, w = part.shape
    return jnp.stack([part, received], axis=1).reshape(2 * n, r, w)


def send_columns(values):
    count = lax.axis_size("mp")
    width = values.shape[-1] // count
    return [swap(values[..., k * width : (k + 1) * width], "mp", k) for k in range(1, count)]


def send_columns_chain(values):
    count = lax.axis_size("mp")
    if count == 1:
        return values[..., :0]
    return swap(values[..., values.shape[-1] // 2 :], "mp", count // 2)


def finish_columns_chain(values, received):
    bit = lax.axis_size("mp") // 2
    while bit:
        half = values.shape[-1] // 2
        values = values[..., :half].astype(F32) + received.astype(F32)
        bit //= 2
        if bit:
            received = swap(values[..., half // 2 :].astype(BF16), "mp", bit)
    return values


def add_columns(values, received):
    width = values.shape[-1] // lax.axis_size("mp")
    return sum([part.astype(F32) for part in received], values[..., :width].astype(F32))


def sum_over(values, axis):
    bit = 1
    while bit < lax.axis_size(axis):
        values = values + swap(values, axis, bit)
        bit *= 2
    return values


def sum_at_once(values, axis):
    received = [values] + [swap(values, axis, mask) for mask in range(1, lax.axis_size(axis))]
    while len(received) > 1:
        received = [one + two for one, two in zip(received[::2], received[1::2])]
    return received[0]


def sum_everywhere(values):
    if lax.axis_size("dp") != 8:
        return sum_over(sum_over(values, "dp"), "mp")
    values = values + swap(values, "dp", 1)
    across = [swap(values, "dp", mask) for mask in (2, 4, 6)]
    values = (values + across[0]) + (across[1] + across[2])
    return sum_at_once(values, "mp")


def gather_wide(values):
    if lax.axis_size("dp") != 8:
        return gather_near(values)
    values = jnp.concatenate([values, swap(values, "dp", 1)], axis=0)
    return jnp.concatenate([values] + [swap(values, "dp", mask) for mask in (2, 4, 6)], axis=0)


def gather_near(values):
    bit = 1
    while bit < lax.axis_size("dp"):
        values = jnp.concatenate([values, swap(values, "dp", bit)], axis=0)
        bit *= 2
    return values


def bias_kernel(line_ref, tile_ref):
    rows = tile_ref.shape[2]
    for block in range(tile_ref.shape[1]):
        line = jnp.broadcast_to(line_ref[0, block : block + 1, :], (rows, 2 * rows))
        tile_ref[0, block] = pltpu.roll(line, 0, 1, stride=1, stride_axis=0)[:, :rows]


def bias_tiles(table, rows):
    heads = table.shape[1]
    lane = jnp.arange(2 * rows, dtype=jnp.int32)
    back = jnp.where(lane < rows, lane, lane - 2 * rows)
    relative = (jnp.arange(3, dtype=jnp.int32)[:, None] - 1) * rows - back[None, :]
    hot = (bucket_of(relative)[..., None] == jnp.arange(table.shape[0])).astype(F32)
    lines = dot(table, hot.reshape(-1, table.shape[0]), (((0,), (1,)), ((), ())), HIGHEST)
    lines = lines.reshape(heads, 3, 2 * rows)
    return pl.pallas_call(
        bias_kernel,
        grid=(heads,),
        in_specs=[pl.BlockSpec((1, 3, 2 * rows), lambda h: (h, 0, 0))],
        out_specs=pl.BlockSpec((1, 3, rows, rows), lambda h: (h, 0, 0, 0)),
        out_shape=jax.ShapeDtypeStruct((heads, 3, rows, rows), F32),
        compiler_params=pltpu.CompilerParams(vmem_limit_bytes=VMEM_LIMIT),
    )(lines)


def own_lanes(shape, part):
    lane = lax.broadcasted_iota(jnp.int32, shape, 1)
    return (lane < HD) if part == 0 else (lane >= HD)


def block_choices(reach):
    return [
        (lo, hi) for lo in range(reach + 1) for hi in range(reach + 1) if lo + hi < 2 * reach
    ]


def whole_rows(near_ref, far_ref, number):
    return jnp.concatenate([near_ref[number], far_ref[number]], axis=0)


def forward_kernel(reach, range_ref, far_ref, q_ref, k_ref, v_ref, qf_ref, kf_ref, bias_ref, o_ref, log_ref):
    pair = pl.program_id(0)
    rows = q_ref.shape[0]
    score_scale = HD ** (-0.5)
    low, high = range_ref[0], range_ref[1]

    def slot_of(block):
        return pl.ds(pl.multiple_of(range_ref[2 + block + reach] * rows, rows), rows)

    def work(lo, hi):
        query = q_ref[...] * jnp.asarray(score_scale, BF16)
        mixed, logs = [], []
        for part in range(2):
            own_q = own_lanes((rows, 2 * HD), part)
            query_low = jnp.where(own_q, query, qf_ref[...])
            scores = []
            for block in range(-lo, hi + 1):
                spot = pl.ds((block + reach) * rows, rows)
                key_low = jnp.where(own_q, k_ref[slot_of(block), :], kf_ref[spot, :])
                score = dot(key_low, query_low, NT)
                if abs(block) <= 1:
                    score = score + bias_ref[part, block + 1]
                else:
                    score = score + far_ref[int(block > 0), 2 * pair + part]
                scores.append(score)
            peak = jnp.max(functools.reduce(jnp.maximum, scores), axis=0, keepdims=True)
            total = jnp.zeros((2 * HD, rows), F32)
            for number, block in enumerate(range(-lo, hi + 1)):
                probs = jnp.exp(scores[number] - peak).astype(BF16)
                value_low = jnp.where(own_q, v_ref[slot_of(block), :], jnp.ones((), BF16))
                total = total + dot(value_low, probs, TN)
            row_sum = total[HD * (1 - part) : HD * (1 - part) + 1, :]
            mixed.append(total[HD * part : HD * (part + 1), :] / row_sum)
            logs.append(peak + jnp.log(row_sum))
        o_ref[...] = jnp.concatenate(mixed, axis=0).T.astype(BF16)
        log_ref[0] = jnp.concatenate(logs + [jnp.zeros((6, rows), F32)], axis=0)

    for lo, hi in block_choices(reach):
        pl.when((low == lo) & (high == hi))(functools.partial(work, lo, hi))


def backward_kernel(
    reach, range_ref, far_ref, q_ref, k_ref, v_ref, qf_ref, kf_ref, bias_ref, do_ref, o_ref, log_ref,
    dq_ref, dk_ref, dv_ref, bias_grad_ref,
):
    pair = pl.program_id(0)
    rows = q_ref.shape[0]
    score_scale = HD ** (-0.5)
    low, high = range_ref[0], range_ref[1]

    def slot_of(block):
        return pl.ds(pl.multiple_of(range_ref[2 + block + reach] * rows, rows), rows)

    def work(lo, hi):
        query = q_ref[...] * jnp.asarray(score_scale, BF16)
        upstream = do_ref[...]
        products = (upstream.astype(F32) * o_ref[...].astype(F32)).T
        nothing = jnp.zeros((), BF16)
        ahead = lax.broadcasted_iota(jnp.int32, (rows, rows), 0) - lax.broadcasted_iota(
            jnp.int32, (rows, rows), 1
        )
        own, query_low, query_own, up_own, delta, log_row, dq, near, far = ([None, None] for _ in range(9))
        for part in range(2):
            own[part] = own_lanes((rows, 2 * HD), part)
            query_low[part] = jnp.where(own[part], query, qf_ref[...])
            query_own[part] = jnp.where(own[part], query, nothing)
            up_own[part] = jnp.where(own[part], upstream, nothing)
            delta[part] = jnp.sum(products[HD * part : HD * (part + 1), :], axis=0, keepdims=True)
            log_row[part] = log_ref[0, part : part + 1, :]
            dq[part] = jnp.zeros((2 * HD, rows), F32)
            near[part] = jnp.zeros((rows, rows), F32)
            far[part] = [jnp.zeros((1, rows), F32), jnp.zeros((1, rows), F32)]
        for block in range(-reach, reach + 1):
            if not -lo <= block <= hi:
                dk_ref[slot_of(block), :] = jnp.zeros((rows, 2 * HD), BF16)
                dv_ref[slot_of(block), :] = jnp.zeros((rows, 2 * HD), BF16)
                continue
            spot = pl.ds((block + reach) * rows, rows)
            dk = jnp.zeros((rows, 2 * HD), F32)
            dv = jnp.zeros((rows, 2 * HD), F32)
            for part in range(2):
                key = k_ref[slot_of(block), :]
                score = dot(jnp.where(own[part], key, kf_ref[spot, :]), query_low[part], NT)
                if abs(block) <= 1:
                    score = score + bias_ref[part, block + 1]
                else:
                    score = score + far_ref[int(block > 0), 2 * pair + part]
                probs = jnp.exp(score - log_row[part])
                dprobs = dot(v_ref[slot_of(block), :], up_own[part], NT)
                dscore = probs * (dprobs - delta[part])
                probs_low, dscore_low = probs.astype(BF16), dscore.astype(BF16)
                dv = dv + dot(probs_low, up_own[part])
                dk = dk + dot(dscore_low, query_own[part])
                dq[part] = dq[part] + dot(key, dscore_low, TN)
                if block == 0:
                    close = jnp.abs(ahead) < FAR
                    near[part] = near[part] + jnp.where(close, dscore, 0.0)
                    far[part][0] += jnp.sum(jnp.where(ahead <= -FAR, dscore, 0.0), axis=0, keepdims=True)
                    far[part][1] += jnp.sum(jnp.where(ahead >= FAR, dscore, 0.0), axis=0, keepdims=True)
                elif abs(block) == 1:
                    close = (ahead < FAR - rows) if block > 0 else (ahead > rows - FAR)
                    near[part] = near[part] + jnp.where(close, dscore, 0.0)
                    far[part][int(block > 0)] += jnp.sum(jnp.where(close, 0.0, dscore), axis=0, keepdims=True)
                else:
                    far[part][int(block > 0)] += jnp.sum(dscore, axis=0, keepdims=True)
            dk_ref[slot_of(block), :] = dk.astype(BF16)
            dv_ref[slot_of(block), :] = dv.astype(BF16)
        dq_ref[...] = (
            jnp.concatenate([dq[0][:HD], dq[1][HD:]], axis=0).T * score_scale
        ).astype(BF16)
        flip = (
            lax.broadcasted_iota(jnp.int32, (rows, rows), 0) + lax.broadcasted_iota(jnp.int32, (rows, rows), 1)
            == rows - 1
        ).astype(BF16)
        for part in range(2):
            turned = dot(flip, near[part].astype(BF16))
            turned = pltpu.roll(turned, 0, 1, stride=1, stride_axis=0)
            line = jnp.sum(turned, axis=0, keepdims=True)
            bias_grad_ref[0, part] = jnp.concatenate(
                [line, far[part][0], far[part][1], jnp.zeros((5, rows), F32)], axis=0
            )

    for lo, hi in block_choices(reach):
        pl.when((low == lo) & (high == hi))(functools.partial(work, lo, hi))


def pair_block(*shape):
    count = len(shape)
    return pl.BlockSpec(shape, lambda p: (0,) * (count - 1) + (p,))


def same_block(*shape):
    count = len(shape)
    return pl.BlockSpec(shape, lambda p: (0,) * count)


def attention_specs(rows, window, pairs):
    smem = pl.BlockSpec(memory_space=pltpu.SMEM)
    return [
        smem,
        smem,
        pair_block(rows, 2 * HD),
        pair_block(window, 2 * HD),
        pl.BlockSpec((window, 2 * HD), lambda p: (0, pairs + p)),
        same_block(rows, 2 * HD),
        same_block(window, 2 * HD),
        pl.BlockSpec((2, 3, rows, rows), lambda p: (p, 0, 0, 0)),
    ]


LITTLE = pl.CostEstimate(flops=10**5, bytes_accessed=10**4, transcendentals=0)


def attend(reach, ranges, far_bias, queries, both, *operands):
    rows, width = queries.shape
    window = both.shape[0]
    pairs = width // (2 * HD)
    return pl.pallas_call(
        functools.partial(forward_kernel, reach),
        grid=(pairs,),
        in_specs=attention_specs(rows, window, pairs),
        out_specs=[pair_block(rows, 2 * HD), pl.BlockSpec((1, 8, rows), lambda p: (p, 0, 0))],
        out_shape=[
            jax.ShapeDtypeStruct((rows, width), BF16),
            jax.ShapeDtypeStruct((pairs, 8, rows), F32),
        ],
        compiler_params=pltpu.CompilerParams(vmem_limit_bytes=VMEM_LIMIT),
        cost_estimate=LITTLE,
        name="attend",
    )(ranges, far_bias, queries, both, both, *operands)


def attend_back(reach, ranges, far_bias, queries, both, *operands):
    rows, width = queries.shape
    window = both.shape[0]
    pairs = width // (2 * HD)
    tall, short = pair_block(window, 2 * HD), pair_block(rows, 2 * HD)
    return pl.pallas_call(
        functools.partial(backward_kernel, reach),
        grid=(pairs,),
        in_specs=attention_specs(rows, window, pairs)
        + [short, short, pl.BlockSpec((1, 8, rows), lambda p: (p, 0, 0))],
        out_specs=[short, tall, tall, pl.BlockSpec((1, 2, 8, rows), lambda p: (p, 0, 0, 0))],
        out_shape=[
            jax.ShapeDtypeStruct((rows, width), BF16),
            jax.ShapeDtypeStruct((window, width), BF16),
            jax.ShapeDtypeStruct((window, width), BF16),
            jax.ShapeDtypeStruct((pairs, 2, 8, rows), F32),
        ],
        compiler_params=pltpu.CompilerParams(vmem_limit_bytes=VMEM_LIMIT),
        cost_estimate=LITTLE,
        name="attend_back",
    )(ranges, far_bias, queries, both, both, *operands)


def flatten_kernel(rows_ref, flat_ref):
    flat_ref[...] = rows_ref[...].T


def flatten(window, rows):
    return pl.pallas_call(
        flatten_kernel,
        grid=(window.shape[0] // rows,),
        in_specs=[pl.BlockSpec((rows, window.shape[1]), lambda n: (n, 0))],
        out_specs=pair_block(window.shape[1], rows),
        out_shape=jax.ShapeDtypeStruct(window.shape[::-1], BF16),
        compiler_params=pltpu.CompilerParams(vmem_limit_bytes=VMEM_LIMIT),
        cost_estimate=LITTLE,
        name="flatten",
    )(window)


def collect_kernel(count, *refs):
    half = refs[-1].shape[1]
    flat_refs, grad_refs = refs[:count], refs[count : 4 * count]
    out_part_ref, keep_ref, send_ref = refs[4 * count :]
    for number in range(3):
        grad = jnp.zeros((2 * half, keep_ref.shape[2]), F32)
        for flat_ref, grad_ref in zip(flat_refs, grad_refs[number::3]):
            grad = grad + dot(flat_ref[:, : grad_ref.shape[0]], grad_ref[...])
        keep_ref[number] = grad[:half].astype(BF16)
        send_ref[number] = grad[half:].astype(BF16)
    keep_ref[3] = out_part_ref[:half, :]
    send_ref[3] = out_part_ref[half:, :]


def collect(windows_flat, grads, out_part):
    count = len(grads)
    chunk = 4 * HD
    flat_grads = [part for grad in grads for part in grad]
    return pl.pallas_call(
        functools.partial(collect_kernel, count),
        grid=(D // chunk,),
        in_specs=[same_block(*part.shape) for part in windows_flat]
        + [pair_block(part.shape[0], chunk) for part in (*flat_grads, out_part)],
        out_specs=[pair_block(4, D // 2, chunk)] * 2,
        out_shape=[jax.ShapeDtypeStruct((4, D // 2, D), BF16)] * 2,
        compiler_params=pltpu.CompilerParams(vmem_limit_bytes=VMEM_LIMIT),
        cost_estimate=LITTLE,
        name="collect",
    )(*windows_flat, *flat_grads, out_part)


CUBE = 0.044715
ROOT = (2.0 / 3.141592653589793) ** 0.5


def feed_kernel(normed_ref, hidden_ref, near_ref, other_ref, out_ref, act_ref, slope_ref):
    @pl.when(pl.program_id(0) == 0)
    def _():
        out_ref[...] = hidden_ref[...]

    w_up = whole_rows(near_ref, other_ref, 0)
    chunk = act_ref.shape[1]
    step = 256 if chunk % 256 == 0 else chunk
    for start in range(0, chunk, step):
        pre = dot(normed_ref[...], w_up[:, start : start + step])
        square = pre * pre
        gate = 0.5 + 0.5 * jnp.tanh(pre * (ROOT + (ROOT * CUBE) * square))
        act = pre * gate
        slope = gate + act * ((1.0 - gate) * (2.0 * ROOT + (6.0 * ROOT * CUBE) * square))
        act_ref[:, start : start + step] = act.astype(BF16)
        slope_ref[:, start : start + step] = slope.astype(BF16)
    out_ref[...] += dot(act_ref[...], whole_rows(near_ref, other_ref, 1), NT)


def feed_back_kernel(
    normed_ref, up_ref, near_ref, other_ref, act_ref, slope_ref, out_ref, keep_ref, send_ref,
    normed_flat_ref, up_flat_ref,
):
    half = keep_ref.shape[1]

    @pl.when(pl.program_id(0) == 0)
    def _():
        out_ref[...] = jnp.zeros_like(out_ref)
        normed_flat_ref[...] = normed_ref[...].T
        up_flat_ref[...] = up_ref[...].T

    act_grad = dot(up_ref[...], whole_rows(near_ref, other_ref, 1))
    pre_grad = (act_grad * slope_ref[...].astype(F32)).astype(BF16)
    out_ref[...] += dot(pre_grad, whole_rows(near_ref, other_ref, 0), NT)
    for number, grad in enumerate(
        (dot(normed_flat_ref[...], pre_grad), dot(up_flat_ref[...], act_ref[...]))
    ):
        keep_ref[number] = grad[:half].astype(BF16)
        send_ref[number] = grad[half:].astype(BF16)


def unit_chunk(units):
    return 1024 if units % 1024 == 0 else units


def feed(normed, hidden, near, other):
    count, width = normed.shape
    _, half, units = near.shape
    chunk = unit_chunk(units)
    weights = pair_block(2, half, chunk)
    wide = pair_block(count, chunk)
    return pl.pallas_call(
        feed_kernel,
        grid=(units // chunk,),
        in_specs=[same_block(count, width), same_block(count, width), weights, weights],
        out_specs=[same_block(count, width), wide, wide],
        out_shape=[
            jax.ShapeDtypeStruct((count, width), F32),
            jax.ShapeDtypeStruct((count, units), BF16),
            jax.ShapeDtypeStruct((count, units), BF16),
        ],
        compiler_params=pltpu.CompilerParams(vmem_limit_bytes=VMEM_LIMIT),
        cost_estimate=LITTLE,
        name="feed",
    )(normed, hidden, near, other)


def feed_back(normed, upstream, near, other, act, slope):
    count, width = normed.shape
    _, half, units = near.shape
    chunk = unit_chunk(units)
    weights = pair_block(2, half, chunk)
    wide = pair_block(count, chunk)
    return pl.pallas_call(
        feed_back_kernel,
        grid=(units // chunk,),
        in_specs=[same_block(count, width), same_block(count, width), weights, weights, wide, wide],
        out_specs=[same_block(count, width), weights, weights],
        out_shape=[
            jax.ShapeDtypeStruct((count, width), F32),
            jax.ShapeDtypeStruct((2, half, units), BF16),
            jax.ShapeDtypeStruct((2, half, units), BF16),
        ],
        scratch_shapes=[pltpu.VMEM((width, count), BF16), pltpu.VMEM((width, count), BF16)],
        compiler_params=pltpu.CompilerParams(vmem_limit_bytes=VMEM_LIMIT),
        cost_estimate=LITTLE,
        name="feed_back",
    )(normed, upstream, near, other, act, slope)


def contrast_kernel(
    micro_count, segment_count, rank_ref, pooled_ref, near_ref, other_ref, turn_ref, grad_ref, proj_grad_ref
):
    every = pooled_ref.shape[0]
    own = micro_count * segment_count

    def place(axis):
        number = lax.broadcasted_iota(jnp.int32, (every, every), axis)
        segment = number % segment_count
        micro = (number // segment_count) % micro_count
        owner = rank_ref[0] ^ (number // own)
        return owner * segment_count + segment, micro

    spot, micro = place(0)
    other_spot, other_micro = place(1)
    together = micro == other_micro
    pooled = dot(pooled_ref[:, :D], turn_ref[...]).astype(BF16)
    proj = jnp.concatenate([near_ref[...], other_ref[...]], axis=0)
    marks = pooled_ref[:, D:].astype(F32)
    target = (marks[:, 0:1] * 16.0 + marks[:, 1:2]).astype(jnp.int32)
    picked = target + (target >= spot).astype(jnp.int32)
    chosen = together & (picked == other_spot)
    embedded = dot(pooled, proj)
    inverse = lax.rsqrt(jnp.sum(embedded * embedded, axis=1, keepdims=True) + EPS_NORM)
    unit = (embedded * inverse).astype(BF16)
    logits = jnp.where(together & (spot != other_spot), SIM_SCALE * dot(unit, unit, NT), NEG_FILL)
    shifted = jnp.exp(logits - jnp.max(logits, axis=1, keepdims=True))
    shares = shifted / jnp.sum(shifted, axis=1, keepdims=True)
    logit_grad = (shares - chosen.astype(F32)).astype(BF16)
    unit_grad = SIM_SCALE * (dot(logit_grad, unit) + dot(logit_grad, unit, TN))
    unit_grad = unit_grad.astype(BF16).astype(F32)
    along = jnp.sum(unit_grad * embedded, axis=1, keepdims=True)
    embed_grad = inverse * unit_grad - embedded * (inverse * inverse * inverse) * along
    embed_grad = embed_grad.astype(BF16)
    grad_ref[...] = dot(embed_grad[:own], proj, NT)
    proj_grad_ref[...] = dot(pooled, embed_grad, TN)


def contrast(rank, pooled, near, other, turn, micro_count, segment_count):
    vmem = pl.BlockSpec(memory_space=pltpu.VMEM)
    return pl.pallas_call(
        functools.partial(contrast_kernel, micro_count, segment_count),
        in_specs=[pl.BlockSpec(memory_space=pltpu.SMEM), vmem, vmem, vmem, vmem],
        out_specs=[vmem, vmem],
        out_shape=[
            jax.ShapeDtypeStruct((micro_count * segment_count, D), F32),
            jax.ShapeDtypeStruct((D, D), F32),
        ],
        compiler_params=pltpu.CompilerParams(vmem_limit_bytes=VMEM_LIMIT),
        cost_estimate=LITTLE,
        name="contrast",
    )(rank, pooled, near, other, turn)


def pack_kernel(parts, *refs):
    ffn_ref, proj_ref, gains_ref, table_ref, total_ref, small_ref = refs[parts:]
    squares = jnp.zeros((1, 1), F32)

    def square(values):
        return jnp.sum(jnp.sum(values * values, axis=1, keepdims=True), axis=0, keepdims=True)

    for layer in range(total_ref.shape[0]):
        total = refs[0][layer].astype(F32)
        for ref in refs[1:parts]:
            total = total + ref[layer].astype(F32)
        total_ref[layer] = total
        squares = squares + square(total)
    for layer in range(ffn_ref.shape[0]):
        squares = squares + square(ffn_ref[layer])
    squares = squares + square(proj_ref[...])
    small_ref[0:3, :] = gains_ref[...]
    small_ref[3:4, :] = table_ref[...]
    small_ref[4:8, :] = jnp.broadcast_to(squares, (4, small_ref.shape[1]))


def pack(parts, ffn, proj, gains, table_row):
    return pl.pallas_call(
        functools.partial(pack_kernel, len(parts)),
        out_shape=[
            jax.ShapeDtypeStruct(parts[0].shape, F32),
            jax.ShapeDtypeStruct((8, gains.shape[1]), F32),
        ],
        compiler_params=pltpu.CompilerParams(vmem_limit_bytes=VMEM_LIMIT),
        name="pack",
    )(*parts, ffn, proj, gains, table_row)


def update_kernel(matrices, *refs):
    small_ref, grad_refs, rest = refs[0], refs[1 : matrices + 1], refs[matrices + 1 :]
    old_refs, norm_ref, new_refs = rest[: 3 * matrices + 3], rest[3 * matrices + 3], rest[3 * matrices + 4 :]
    few = small_ref[0:4, :]
    total = small_ref[4:5, 0:1] + jnp.sum(
        jnp.sum(few * few, axis=1, keepdims=True), axis=0, keepdims=True
    )
    norm = jnp.sqrt(total)
    norm_ref[...] = norm
    factor = jnp.minimum(1.0, CLIP_NORM / (norm + 1e-06))
    for number in range(matrices + 1):
        weight_ref, first_ref, second_ref = old_refs[3 * number : 3 * number + 3]
        is_matrix = number < matrices
        rate, decay = (RATE_MATRIX, DECAY_MATRIX) if is_matrix else (RATE_SMALL, 0.0)
        layers = range(weight_ref.shape[0]) if len(weight_ref.shape) == 3 else [Ellipsis]
        for layer in layers:
            grad = grad_refs[number][layer] if is_matrix else small_ref[0:3, :]
            results = adam_update(
                weight_ref[layer], grad * factor, first_ref[layer], second_ref[layer], rate, decay
            )
            for new_ref, result in zip(new_refs[3 * number : 3 * number + 3], results):
                new_ref[layer] = result


def update(small, grads, old):
    flat = [part for group in old for part in group]
    return pl.pallas_call(
        functools.partial(update_kernel, len(grads)),
        out_shape=[jax.ShapeDtypeStruct((1, 1), F32)]
        + [jax.ShapeDtypeStruct(part.shape, F32) for part in flat],
        compiler_params=pltpu.CompilerParams(vmem_limit_bytes=VMEM_LIMIT),
        name="update",
    )(small, *grads, *flat)


def local(
    tokens,
    cotangent,
    segment_ids,
    targets,
    attention_weights,
    feedforward_weights,
    projection,
    norm_gains,
    bias_table,
    attention_first,
    attention_second,
    feedforward_first,
    feedforward_second,
    projection_first,
    projection_second,
    gains_first,
    gains_second,
    bias_first,
    bias_second,
):
    wide_count = lax.axis_size("dp")
    narrow_count = lax.axis_size("mp")
    wide_rank = lax.axis_index("dp")
    narrow_rank = lax.axis_index("mp")
    micro_count, _, rows, _ = tokens.shape
    segment_count = targets.shape[2]
    block = D // wide_count
    heads_part = attention_weights.shape[2] // HD
    reach = min(narrow_count - 1, -(-(SEG_MOST - 1) // rows))
    span = 2 * reach + 1

    feature = jnp.arange(D, dtype=jnp.int32)
    place = feature // block
    order = outer_masks() + core_masks()
    away = sum(((place >> bit) & 1) * mask for bit, mask in enumerate(order)) + jnp.zeros_like(place)
    source = (wide_rank ^ away) * block + feature % block
    turn = (feature[:, None] == source[None, :]).astype(BF16)
    turn_wide = turn.astype(F32)

    attention_low = attention_weights.astype(BF16)
    feedforward_low = feedforward_weights.astype(BF16)
    projection_low = projection.astype(BF16)

    token_rows = dot(tokens.reshape(micro_count * rows, D), turn)
    gains = dot(norm_gains, turn_wide, precision=HIGHEST)
    factor_one = norm_factor(token_rows)
    normed_one = (token_rows * factor_one * gains[0]).astype(BF16)
    normed_one = normed_one.reshape(micro_count, rows, D)

    head = jnp.arange(bias_table.shape[1], dtype=jnp.int32)
    head_source = (narrow_rank ^ (head // heads_part)) * heads_part + head % heads_part
    head_turn = (head[:, None] == head_source[None, :]).astype(F32)

    is_even = narrow_rank % 2 == 0

    def hop(held):
        return link(held[1], False), link(held[0], True)

    hops = [[] for _ in range(micro_count)]

    def window_of(micro):
        return jnp.concatenate([normed_one[micro]] + [part for pair in hops[micro] for part in pair])

    def project(micro):
        return (
            dot(normed_one[micro], w_query).astype(BF16),
            dot(windows[micro], w_both).astype(BF16),
        )

    def finish_hops(micro):
        while len(hops[micro]) < reach:
            hops[micro].append(hop(hops[micro][-1]))

    def chain_step(values, bit):
        return jnp.concatenate([values, swap(values, "mp", bit)], axis=-1)

    bits = []
    while 1 << len(bits) < narrow_count:
        bits.append(1 << len(bits))
    attn_parts = gather_columns(attention_low)
    ffn_cols = feedforward_low
    for bit in bits[:1]:
        ffn_cols = chain_step(ffn_cols, bit)
    attn_parts, ffn_cols, normed_late = after((attn_parts, ffn_cols, normed_one))
    segment_ids, bias_late, targets_late = after((segment_ids, bias_table, targets), *attn_parts)
    table = dot(bias_late, head_turn, precision=HIGHEST)
    tiles = bias_tiles(table, rows)
    marks = jnp.stack([targets_late[:, 0] // 16, targets_late[:, 0] % 16], axis=-1).astype(BF16)
    marks = jnp.pad(marks[None], ((0, 0), (0, 0), (0, 0), (0, 126)))
    attn_held = gather_plane(jnp.concatenate([attention_low] + attn_parts, axis=-1))
    for bit in bits[1:]:
        ffn_cols = chain_step(ffn_cols, bit)
    attn_held, ffn_cols, normed_late, tiles, marks = after(
        (attn_held, ffn_cols, normed_late, tiles, marks)
    )
    attn_near, attn_other = halves(attn_held)
    first_hop = hop((normed_late, normed_late))
    parts = [ffn_cols[0][None], ffn_cols[1][None]]

    def outer_received(number):
        return [gather_outer(part, number, first) for part, first in zip(parts, (True, False))]

    def outer_joined(received):
        return [
            join_outer(part, got, first) for part, got, first in zip(parts, received, (True, False))
        ]

    outer_count = len(outer_masks())
    received = outer_received(0)
    attn_other, first_hop, received = after((attn_other, first_hop, received))
    parts = outer_joined(received)
    attn_all = jnp.concatenate([attn_near, attn_other], axis=1)
    w_query, w_out = attn_all[0], attn_all[3]
    w_both = jnp.concatenate([attn_all[1], attn_all[2]], axis=1)
    for micro in range(micro_count):
        hops[micro].append((first_hop[0][micro], first_hop[1][micro]))
    finish_hops(0)
    proj_parts = gather_columns(after(projection_low, attn_other))
    w_both, w_query, hops, parts, proj_parts = after((w_both, w_query, hops, parts, proj_parts))
    proj_cols = jnp.concatenate([projection_low] + proj_parts, axis=-1)[None]
    windows = [window_of(0)]
    projected = [project(0)]
    slots = jnp.stack(
        [
            jnp.int32(0)
            if n == 0
            else jnp.where(is_even == (n > 0), 2 * abs(n) - 1, 2 * abs(n)).astype(jnp.int32)
            for n in range(-reach, reach + 1)
        ]
    )

    far_bias = jnp.stack([table[15], table[31]])
    lanes = jnp.arange(2 * HD, dtype=jnp.int32) % HD
    padded = jnp.pad(
        segment_ids[:, 0], ((0, 0), (reach * rows, reach * rows)), constant_values=segment_count
    )
    window_segments = lax.dynamic_slice_in_dim(padded, narrow_rank * rows, span * rows, 1)
    own_segments = window_segments[:, reach * rows : (reach + 1) * rows]
    key_marks = (window_segments[:, :, None] == lanes).astype(BF16)
    query_marks = jnp.where(
        (own_segments[:, :, None] != lanes) & (lanes <= segment_count), MASKED, 0.0
    ).astype(BF16)
    first, last = own_segments[:, 0], own_segments[:, -1]
    low_count = sum(
        (window_segments[:, (reach - n) * rows + rows - 1] == first).astype(jnp.int32)
        for n in range(1, reach + 1)
    )
    high_count = sum(
        (window_segments[:, (reach + n) * rows] == last).astype(jnp.int32)
        for n in range(1, reach + 1)
    )
    ranges = jnp.concatenate(
        [
            jnp.stack([low_count, high_count], axis=1),
            jnp.broadcast_to(slots, (micro_count, span)),
        ],
        axis=1,
    )

    mixed, kept = [], []
    proj_held = []
    for micro in range(micro_count):
        came, received = [], []
        parts, projected[micro] = after((parts, projected[micro]))
        if micro == 0 and outer_count > 1:
            received = outer_received(1)
        if micro + 1 < micro_count:
            finish_hops(micro + 1)
            came = hops[micro + 1]
        else:
            proj_held = gather_plane(after(proj_cols, projected[micro][0]))
        operands = (
            ranges[micro], far_bias, *projected[micro], query_marks[micro], key_marks[micro], tiles
        )
        mixed_part, logs = attend(reach, *operands)
        came, mixed_part, proj_held = after((came, mixed_part, proj_held))
        if came:
            hops[micro + 1] = came
            windows.append(window_of(micro + 1))
            projected.append(project(micro + 1))
        if received:
            last_received = received
        kept.append((operands, mixed_part, logs))
        mixed.append(mixed_part)
    if outer_count > 1:
        last_received, mixed = after((last_received, mixed))
        parts = outer_joined(last_received)
    for number in range(2, outer_count):
        parts = outer_joined(outer_received(number))
    ffn_near, ffn_other = halves(jnp.stack(parts))
    hidden_one = token_rows + dot(jnp.concatenate(mixed, axis=0), w_out, NT)
    proj_near, proj_other = halves(proj_held)
    windows_flat = [flatten(window, rows) for window in windows]
    hidden_one, ffn_other, proj_other, windows_flat = after(
        (hidden_one, ffn_other, proj_other, windows_flat)
    )

    factor_two = norm_factor(hidden_one)
    normed_two = (hidden_one * factor_two * gains[1]).astype(BF16)
    hidden_two, activated, slopes = feed(normed_two, hidden_one, ffn_near, ffn_other)
    output = dot(hidden_two.astype(BF16), turn, NT).astype(BF16)

    factor_three = norm_factor(hidden_two)
    unit_three = hidden_two * factor_three
    normed_three = (unit_three * gains[2]).reshape(micro_count, rows, D)
    numbers = jnp.arange(segment_count, dtype=jnp.int32)
    member = (own_segments[:, None, :] == numbers[None, :, None]).astype(F32)
    counts = jnp.sum(
        (segment_ids[:, 0][:, None, :] == numbers[None, :, None]).astype(F32), axis=2, keepdims=True
    )
    pooled = lax.dot_general(
        member, normed_three, (((2,), (1,)), ((0,), (0,))), precision=HIGHEST, preferred_element_type=F32
    )
    pooled = sum_at_once(pooled, "mp") / counts
    pooled = dot(pooled.reshape(-1, D).astype(BF16), turn, NT).astype(BF16)
    pooled = pooled.reshape(1, micro_count, segment_count, D)
    pooled_all = gather_wide(jnp.concatenate([pooled, marks], axis=-1))
    rank = jnp.stack([wide_rank, narrow_rank]).astype(jnp.int32)
    pooled_grad, proj_grad = contrast(
        rank, pooled_all.reshape(-1, pooled_all.shape[-1]), proj_near[0], proj_other[0], turn,
        micro_count, segment_count,
    )
    proj_reduced = proj_grad[:block, : projection.shape[1]]
    pooled_grad = pooled_grad.reshape(micro_count, segment_count, D) / counts
    normed_three_grad = lax.dot_general(
        member, pooled_grad, (((1,), (1,)), ((0,), (0,))), precision=HIGHEST, preferred_element_type=F32
    ).reshape(micro_count * rows, D)
    gain_three = jnp.sum(normed_three_grad * unit_three, axis=0)

    upstream = dot(cotangent.reshape(micro_count * rows, D), turn)
    hidden_two_grad = upstream + norm_back(hidden_two, factor_three, normed_three_grad * gains[2])
    hidden_two_low = hidden_two_grad.astype(BF16)
    normed_two_grad, ffn_keep, ffn_send = feed_back(
        normed_two, hidden_two_low, ffn_near, ffn_other, activated, slopes
    )
    ffn_received = swap(ffn_send, "dp", 1)
    gain_two = jnp.sum(normed_two_grad * hidden_one * factor_two, axis=0)
    hidden_one_grad = hidden_two_grad + norm_back(
        hidden_one, factor_two, normed_two_grad * gains[1]
    )
    hidden_one_low = hidden_one_grad.astype(BF16)
    mixed_grad = dot(hidden_one_low, w_out).astype(BF16).reshape(micro_count, rows, D)
    out_part = dot(hidden_one_low, jnp.concatenate(mixed, axis=0), TN).astype(BF16)
    ffn_received, mixed_grad, out_part = after((ffn_received, mixed_grad, out_part))

    def outer_split(parts):
        return [split_outer(terms, masks, first) for (terms, masks), first in zip(parts, (False, True))]

    ffn_blocks = [to_blocks(ffn_keep), to_blocks(ffn_received)]
    parts = [
        ([held[number : number + 1] for held in ffn_blocks], outer_masks()) for number in range(2)
    ]
    grads, owns, bias_parts, flows = [], [], [], []

    def leave(flow, n):
        even, odd = flow[2 * n - 2], flow[2 * n - 1]
        return link(even, False), link(odd, True)

    def join(flow, n, came):
        if n > 0:
            flow[2 * n - 1] = add_low(flow[2 * n - 1], came[0])
            flow[2 * n - 2] = add_low(flow[2 * n - 2], came[1])

    def flow_of(dq, dk, dv):
        partial = dot(dk, w_both[:, :D], NT) + dot(dv, w_both[:, D:], NT)
        own = partial[:rows] + dot(dq, w_query, NT)
        low_parts = partial.astype(BF16)
        return own, [low_parts[n * rows : (n + 1) * rows] for n in range(1, span)]

    came = []
    for micro in range(micro_count):
        operands, mixed_part, logs = kept[micro]
        last = micro == micro_count - 1
        steps = outer_split(parts) if parts[0][1] else []
        upstream_low, flows, sent = after(
            (mixed_grad[micro], flows, [step[1] for step in steps])
        )
        received = [swap(leaves, "dp", step[2]) for leaves, step in zip(sent, steps)]
        came = [leave(flow, reach) for flow in flows]
        dq, dk, dv, bias_part = attend_back(reach, *operands, upstream_low, mixed_part, logs)
        flow = None if last else flow_of(dq, dk, dv)
        received, came, dq, dk, dv, flow = after(
            (received, came, dq, dk, dv, flow)
        )
        if steps:
            parts = [(step[0] + [got], step[3]) for step, got in zip(steps, received)]
        grads.append((dq, dk, dv))
        bias_parts.append(bias_part)
        if not last:
            owns.append(flow[0])
            flows.append(list(flow[1]))
    while parts[0][1]:
        parts = [
            (stay + [swap(leaves, "dp", mask)], masks)
            for stay, leaves, mask, masks in outer_split(parts)
        ]
    others = came
    for flow, got in zip(flows, others):
        join(flow, reach - 1, got)
    ffn_last = [add_low(*terms)[0, 0] for terms, _ in parts]
    ffn_last, grads = after((ffn_last, grads))
    ffn_last = jnp.stack(ffn_last)
    ffn_column = send_columns_chain(ffn_last)
    attn_keep, attn_send = collect(windows_flat, grads, out_part)
    last = flow_of(*grads[-1])
    attn_keep, attn_send, ffn_column, flows, owns, last = after(
        (attn_keep, attn_send, ffn_column, flows, owns, last)
    )
    owns.append(last[0])
    last = list(last[1])
    attn_received = swap(attn_send, "dp", 1)
    came = leave(last, reach) if reach > 1 else ()
    others = [leave(flow, 1) for flow in flows]
    attn_received, came, others, ffn_column = after((attn_received, came, others, ffn_column))
    attn_blocks = [to_blocks(attn_keep), to_blocks(attn_received)]
    attn_parts = [([held[k : k + 2] for held in attn_blocks], outer_masks()) for k in (0, 2)]
    if reach > 1:
        join(last, reach - 1, came)
    hopped, ffn_reduced = (), None
    while attn_parts[0][1]:
        steps = outer_split(attn_parts)
        sent, last = after(([step[1] for step in steps], last))
        received = [swap(leaves, "dp", step[2]) for leaves, step in zip(sent, steps)]
        if ffn_reduced is None:
            hopped = leave(last, 1)
            ffn_reduced = finish_columns_chain(ffn_last, ffn_column)
        received, hopped, ffn_reduced = after((received, hopped, ffn_reduced))
        attn_parts = [(step[0] + [got], step[3]) for step, got in zip(steps, received)]
    attn_last = jnp.concatenate([add_low(*terms) for terms, _ in attn_parts])[:, 0]
    attn_columns = send_columns(attn_last)
    normed_one_grad = jnp.concatenate(
        [
            own + even.astype(F32) + odd.astype(F32)
            for own, (even, odd) in zip(owns, [*others, hopped])
        ]
    )
    gain_one = jnp.sum(normed_one_grad * token_rows * factor_one, axis=0)
    tokens_grad = hidden_one_grad + norm_back(token_rows, factor_one, normed_one_grad * gains[0])
    tokens_grad = dot(tokens_grad, turn_wide, NT, HIGHEST)
    attn_columns, tokens_grad, gain_one = after((attn_columns, tokens_grad, gain_one))

    bias_sum = sum(bias_parts)
    heads = table.shape[1]
    bias_sum = bias_sum.reshape(heads, 8, rows)
    spot = (jnp.arange(rows, dtype=jnp.int32) + 1) % rows
    relative = jnp.where(spot < FAR, -spot, rows - spot)
    buckets = jnp.arange(table.shape[0], dtype=jnp.int32)
    near_hot = (bucket_of(relative)[:, None] == buckets[None, :]) & (
        jnp.abs(relative) < FAR
    )[:, None]
    table_grad = dot(near_hot.astype(F32), bias_sum[:, 0], (((0,), (1,)), ((), ())), HIGHEST)
    table_grad = (
        table_grad
        + (buckets == 15).astype(F32)[:, None] * jnp.sum(bias_sum[:, 1], axis=1)[None, :]
        + (buckets == 31).astype(F32)[:, None] * jnp.sum(bias_sum[:, 2], axis=1)[None, :]
    )
    full_table = dot(table_grad, head_turn, NT, HIGHEST)
    gains_part = dot(jnp.stack([gain_one, gain_two, gain_three]), turn_wide, NT, HIGHEST)
    table_row = jnp.pad(full_table.reshape(1, -1), ((0, 0), (0, D - full_table.size)))
    attn_reduced, small = pack(
        [attn_last[..., : attn_columns[0].shape[-1]], *attn_columns],
        ffn_reduced, proj_reduced, gains_part, table_row,
    )
    small = sum_everywhere(small)
    table_full_grad = small[3, : full_table.size].reshape(full_table.shape)
    grad_norm, *updated = update(
        small,
        [attn_reduced, ffn_reduced, proj_reduced],
        [
            (attention_weights, attention_first, attention_second),
            (feedforward_weights, feedforward_first, feedforward_second),
            (projection, projection_first, projection_second),
            (norm_gains, gains_first, gains_second),
        ],
    )
    grad_norm = grad_norm.reshape(())
    attn_new, ffn_new, proj_new, gains_new = (updated[3 * k : 3 * k + 3] for k in range(4))
    factor = jnp.minimum(1.0, CLIP_NORM / (grad_norm + 1e-06))
    table_new = adam_update(
        bias_table, table_full_grad * factor, bias_first, bias_second, RATE_SMALL, 0.0
    )
    return (
        output.reshape(tokens.shape),
        tokens_grad.reshape(tokens.shape),
        grad_norm,
        *attn_new,
        *ffn_new,
        *proj_new,
        *gains_new,
        *table_new,
    )


def solution(mesh):
    return jax.shard_map(
        local,
        mesh=mesh,
        in_specs=(
            P(None, "dp", "mp", None),
            P(None, "dp", "mp", None),
            P(None, "dp", None),
            P(None, "dp", None),
            P(None, "dp", "mp"),
            P(None, "dp", "mp"),
            P("dp", "mp"),
            P(),
            P(),
            P(None, "dp", "mp"),
            P(None, "dp", "mp"),
            P(None, "dp", "mp"),
            P(None, "dp", "mp"),
            P("dp", "mp"),
            P("dp", "mp"),
            P(),
            P(),
            P(),
            P(),
        ),
        out_specs=(
            P(None, "dp", "mp", None),
            P(None, "dp", "mp", None),
            P(),
            P(None, "dp", "mp"),
            P(None, "dp", "mp"),
            P(None, "dp", "mp"),
            P(None, "dp", "mp"),
            P(None, "dp", "mp"),
            P(None, "dp", "mp"),
            P("dp", "mp"),
            P("dp", "mp"),
            P("dp", "mp"),
            P(),
            P(),
            P(),
            P(),
            P(),
            P(),
        ),
        check_vma=False,
    )
```
